512 devices in a mesh: slab: 16 (over y, z_hi), tile: 32 (over z_lo, x, core).
Axes of the slice: x: 4, y: 4, z: 16 (z_hi: 4, z_lo: 4; z = z_hi * 4 + z_lo), core: 2. Of those that a mesh axis runs over, the one named last changes fastest.
Arguments:
- positions: float32 [16, 32, 32, 3, 128], P('slab', 'tile'), as said below
- charges: float32 [16, 32, 32, 128], P('slab', 'tile'), may hold values from -3 to 3
- radii: float32 [16, 32, 32, 128], P('slab', 'tile'), may hold values from 1.4 to 2
- scales: float32 [16, 32, 32, 128], P('slab', 'tile'), may hold values from 0.7 to 0.95
- neighbours: int32 [16, 32, 32, 8], P('slab', 'tile'), may hold values from 0 to 16383, as said below
- pad_mask: int32 [16, 32, 32, 8], P('slab', 'tile'), may hold values from 0 to 1, as said below
Outputs:
- born_radii: float32 [16, 32, 32, 128], P('slab', 'tile')
- radius_grad: float32 [16, 32, 32, 128], P('slab', 'tile')
- forces: float32 [16, 32, 32, 3, 128], P('slab', 'tile')
The draws below stay inside these ranges and needn't reach their ends.
Inputs may be any that keep to these rules, and one draw needn't show every extreme that they name: positions: each tile's atoms sit in that tile's own box of a cylindrical shell, at one of two radial levels; any two atoms of different tiles or of one tile lie 0.9 or more apart. `neighbours`: ids count tiles as (slab * 32 + cycle index) * 32 + local index. A tile held by the device at slab s and cycle index t lists only tiles of slabs s - 1, s, s + 1 held at cycle index t or t + 1 (modulo 32); tiles held at cycle index t + 1 are listed only at local index 0 or 1, and only by tiles of local index 30 or 31; slot 0 names the tile itself, other slots name other tiles, and no two tiles list each other on live slots. `pad_mask`: each tile's live slots come first; slot 0 is always live; some tile has all 8 slots live.
All inputs are finite; a program needn't handle non-finite values.
Results may differ from the reference program's by a relative error of at most 0.0003.
Values sent between devices are 32-bit elements; how exact they have to be, the bound alone decides.
No kernel may reach another device: no remote copies, remote signals or barrier semaphores. Data moves between devices by JAX's collectives and lax.ppermute only.
A program may use at most 64 MiB of HBM per device.

```python
import math
import jax
import jax.numpy as jnp
from jax import lax

SLABS = 16
CYCLE = 32
TILE_DEV = 32
ATOMS = 128
NB = 8


arc_length = 10.0


shell_width = 14.0


slab_height = 10.0


level_lift = 50.0


radial_spread = 0.73


def step_tables():
    step_slab = jnp.array([0, -1, 0, 1, -1, 0, 1, 1], jnp.int32)
    step_cycle = jnp.array([0, 1, 1, 1, 2, 2, 2, 0], jnp.int32)
    return (step_slab, step_cycle)


def lift_pattern(key):
    cycle_tiles = CYCLE * TILE_DEV
    tile_shape = (SLABS, CYCLE, TILE_DEV)
    keys = jax.random.split(jax.random.fold_in(key, 101), 4)
    level = jax.random.randint(keys[0], (SLABS, CYCLE, 1), 0, 4)
    lift = (jax.random.randint(keys[1], tile_shape, 0, 4) < level).astype(jnp.int32)
    forced_slab = jax.random.randint(keys[2], (), 1, SLABS - 1)
    forced_place = jax.random.randint(keys[3], (), 0, cycle_tiles)
    slab_index = lax.broadcasted_iota(jnp.int32, tile_shape, 0)
    cycle_place = lax.broadcasted_iota(jnp.int32, tile_shape, 1) * TILE_DEV + lax.broadcasted_iota(jnp.int32, tile_shape, 2)
    step_slab, step_cycle = step_tables()
    nearby = jnp.zeros(tile_shape, jnp.bool_)
    for slot in range(8):
        nearby = nearby | (slab_index == forced_slab + step_slab[slot]) & (cycle_place == (forced_place + step_cycle[slot]) % cycle_tiles)
    return jnp.where(nearby, 0, lift).astype(jnp.int32)


def tile_lists(key):
    lift = lift_pattern(key)
    grid_shape = (SLABS, CYCLE, TILE_DEV, NB)
    cycle_tiles = CYCLE * TILE_DEV
    slab_index = lax.broadcasted_iota(jnp.int32, grid_shape, 0)
    cycle_place = lax.broadcasted_iota(jnp.int32, grid_shape, 1) * TILE_DEV + lax.broadcasted_iota(jnp.int32, grid_shape, 2)
    slot_index = lax.broadcasted_iota(jnp.int32, grid_shape, 3)
    step_slab, step_cycle = step_tables()
    target = slab_index + step_slab
    in_range = (target >= 0) & (target < SLABS)
    slab_other = jnp.where(in_range, target, slab_index)
    cycle_other = jnp.where(in_range, cycle_place + step_cycle, cycle_place + 1) % cycle_tiles
    listed = slab_other * cycle_tiles + cycle_other
    lift_other = lift.reshape(-1)[listed]
    live_raw = in_range & (lift_other == lift[..., None])
    keys = jax.random.split(key, 2)
    sort_key = jax.random.randint(keys[1], grid_shape, 0, 8) * NB + slot_index
    sort_key = jnp.where(slot_index == 0, -1, sort_key)
    sort_key = jnp.where(live_raw, sort_key, sort_key + 1000)
    ranking = jnp.argsort(sort_key, axis=-1)
    listed_sorted = jnp.take_along_axis(listed, ranking, axis=-1)
    live = jnp.take_along_axis(live_raw, ranking, axis=-1)
    return (listed_sorted.astype(jnp.int32), live.astype(jnp.int32))


def draw_neighbours(key, part):
    listed, live = tile_lists(key)
    return listed


def draw_pad_mask(key, part):
    listed, live = tile_lists(key)
    return live


def draw_positions(key, part):
    lift = lift_pattern(key)
    key = jax.random.fold_in(key, 7)
    grid_shape = (SLABS, CYCLE, TILE_DEV, ATOMS)
    jitter_draw = jax.random.uniform(key, (3,) + grid_shape, jnp.float32, -0.3, 0.3)
    slab_index = lax.broadcasted_iota(jnp.float32, grid_shape, 0)
    cycle_place = lax.broadcasted_iota(jnp.float32, grid_shape, 1) * TILE_DEV + lax.broadcasted_iota(jnp.float32, grid_shape, 2)
    atom_index = lax.broadcasted_iota(jnp.int32, grid_shape, 3)
    layers = ATOMS // 16
    radial_index = (atom_index % layers).astype(jnp.float32)
    height_index = (atom_index // layers % 4).astype(jnp.float32)
    arc_index = (atom_index // (4 * layers)).astype(jnp.float32)
    cycle_tiles = CYCLE * TILE_DEV
    lifted = lift.astype(jnp.float32)[..., None] * level_lift
    azimuth = 2.0 * math.pi * (cycle_place + (arc_index + 0.5 + jitter_draw[0]) / 4.0) / cycle_tiles
    distance = cycle_tiles * arc_length / (2.0 * math.pi) + (radial_index + 0.5 + radial_spread * jitter_draw[1]) * shell_width / layers + lifted
    height = (slab_index + (height_index + 0.5 + jitter_draw[2]) / 4.0) * slab_height
    return jnp.stack([distance * jnp.cos(azimuth), distance * jnp.sin(azimuth), height], axis=3)


def shard_levels(own_key, extent, shards, low, high):
    def one(position, blocks):
        heights = jax.random.uniform(jax.random.fold_in(jax.random.fold_in(own_key, 6), position), (blocks,), jnp.float32, low / len(shards), high / len(shards))
        return jnp.repeat(jnp.exp(heights), extent[position] // blocks).reshape((-1,) + (1,) * (len(extent) - position - 1))

    level = one(*shards[0])
    for cut in shards[1:]:
        level = level * one(*cut)
    return level


def normal_values(own_key, shape, spread, most, cuts=(), kind=jnp.bfloat16):
    values = jax.random.normal(own_key, shape, jnp.float32) * spread
    if len(cuts) > 0:
        values = shard_levels(own_key, shape, cuts, -0.22, 0.18) * values
    return jnp.clip(values, min=-most, max=most).astype(kind)


def setup_inputs(seed: int = 0) -> dict:
    seeds = jax.random.split(jax.random.key(seed), 7)
    return {
        "positions": draw_positions(jax.random.fold_in(seeds[6], 71), 0),
        "charges": normal_values(seeds[1], (SLABS, CYCLE, TILE_DEV, ATOMS), 1.0, 3.0, ((0, 16), (1, 32)), jnp.float32),
        "radii": jnp.clip(1.4 + 0.6 * jax.random.uniform(seeds[2], (SLABS, CYCLE, TILE_DEV, ATOMS), jnp.float32) ** shard_levels(seeds[2], (SLABS, CYCLE, TILE_DEV, ATOMS), ((0, 16), (1, 32)), -0.2, 0.2), 1.4, 2.0),
        "scales": jnp.clip(0.7 + 0.25 * jax.random.uniform(seeds[3], (SLABS, CYCLE, TILE_DEV, ATOMS), jnp.float32) ** shard_levels(seeds[3], (SLABS, CYCLE, TILE_DEV, ATOMS), ((0, 16), (1, 32)), -0.2, 0.2), 0.7, 0.95),
        "neighbours": draw_neighbours(jax.random.fold_in(seeds[6], 71), 0),
        "pad_mask": draw_pad_mask(jax.random.fold_in(seeds[6], 71), 0),
    }


radius_offset = 0.09
obc_alpha = 1.0
obc_beta = 0.8
obc_gamma = 4.85
cutoff_len = 14.0

def gap_squared(coords_one, coords_two, self_flag):
    differ = coords_one[..., :, :, None] - coords_two[..., :, None, :]
    squared = lax.optimization_barrier(jnp.sum(differ * differ, axis=-3))
    unit_diag = jnp.eye(coords_one.shape[-1], dtype=jnp.float32)
    return squared + self_flag[..., None, None] * unit_diag * (4.0 * cutoff_len * cutoff_len)

def smooth_switch(squared):
    switch_base = jnp.maximum(1.0 - squared / (cutoff_len * cutoff_len), 0.0)
    return switch_base * switch_base

def descreen(distance, radius_own, radius_far):
    upper_end = distance + radius_far
    lower_end = jnp.minimum(jnp.maximum(radius_own, jnp.abs(distance - radius_far)), upper_end)
    inv_lower = 1.0 / lower_end
    inv_upper = 1.0 / upper_end
    return 0.5 * (inv_lower - inv_upper + 0.25 * distance * (inv_upper * inv_upper - inv_lower * inv_lower) + 0.5 / distance * jnp.log(lower_end * inv_upper) + 0.25 * radius_far * radius_far / distance * (inv_lower * inv_lower - inv_upper * inv_upper))

def born_pair(data_one, data_two, self_flag, live_weight):
    squared = gap_squared(data_one[..., 0:3, :], data_two[..., 0:3, :], self_flag)
    distance = jnp.sqrt(squared)
    weight = smooth_switch(squared) * live_weight[..., None, None]
    own_part = lax.optimization_barrier(jnp.sum(weight * descreen(distance, data_one[..., 4, :, None], data_two[..., 5, None, :]), axis=-1))
    far_part = (1.0 - self_flag)[..., None] * lax.optimization_barrier(jnp.sum(weight * descreen(distance, data_two[..., 4, None, :], data_one[..., 5, :, None]), axis=-2))
    return (own_part, far_part)

def screened(squared, radius_one, radius_two, data_one, data_two, self_flag, weight):
    product = radius_one[..., :, None] * radius_two[..., None, :]
    effective = jnp.sqrt(squared + product * jnp.exp(-squared / (4.0 * product)))
    return -(1.0 - 0.5 * self_flag)[..., None, None] * weight * data_one[..., 3, :, None] * data_two[..., 3, None, :] / effective

def radius_pair(radius_one, radius_two, data_one, data_two, self_flag, live_weight):
    squared = gap_squared(data_one[..., 0:3, :], data_two[..., 0:3, :], self_flag)
    weight = smooth_switch(squared) * live_weight[..., None, None]

    def energy(first_set, second_set):
        return jnp.sum(screened(squared, first_set, second_set, data_one, data_two, self_flag, weight))
    result_value, pullback = jax.vjp(energy, radius_one, radius_two)
    return pullback(jnp.ones_like(result_value))

def force_pair(coords_one, coords_two, data_one, data_two, radius_one, radius_two, chain_one, chain_two, self_flag, live_weight):

    def total_energy(first_set, second_set):
        squared = gap_squared(first_set, second_set, self_flag)
        distance = jnp.sqrt(squared)
        weight = smooth_switch(squared) * live_weight[..., None, None]
        energy = screened(squared, radius_one, radius_two, data_one, data_two, self_flag, weight)
        screen = chain_one[..., :, None] * descreen(distance, data_one[..., 4, :, None], data_two[..., 5, None, :])
        screen = screen + (1.0 - self_flag)[..., None, None] * chain_two[..., None, :] * descreen(distance, data_two[..., 4, None, :], data_one[..., 5, :, None])
        return jnp.sum(energy + weight * screen)
    result_value, pullback = jax.vjp(total_energy, coords_one, coords_two)
    grad_one, grad_two = pullback(jnp.ones_like(result_value))
    return (-grad_one, -grad_two)

def born_radius(descreen_sum, radius):
    radius_in = radius - radius_offset
    scaled = radius_in * descreen_sum
    polynomial = scaled * (obc_alpha + scaled * (-obc_beta + obc_gamma * scaled))
    tangent = jnp.tanh(polynomial)
    radii_born = 1.0 / (1.0 / radius_in - tangent / radius)
    radius_slope = radii_born * radii_born * (1.0 - tangent * tangent) / radius * (obc_alpha - 2.0 * obc_beta * scaled + 3.0 * obc_gamma * scaled * scaled) * radius_in
    return (radii_born, radius_slope)

def reference(positions, charges, radii, scales, neighbours, pad_mask):
    tile_total = SLABS * CYCLE * TILE_DEV
    groups = SLABS * CYCLE
    coords = positions.reshape(tile_total, 3, ATOMS)
    charge = charges.reshape(tile_total, ATOMS)
    radius = radii.reshape(tile_total, ATOMS)
    radius_in = radius - radius_offset
    atom_data = jnp.concatenate([coords, charge[:, None], radius_in[:, None], (scales.reshape(tile_total, ATOMS) * radius_in)[:, None]], axis=1)
    listed_all = neighbours.reshape(tile_total, NB).astype(jnp.int32)
    live_all = pad_mask.reshape(tile_total, NB).astype(jnp.float32)
    self_flag = (jnp.arange(NB) == 0).astype(jnp.float32)[None, :]

    def grouped(array):
        return array.reshape((groups, TILE_DEV) + array.shape[1:])

    def scatter_back(parts):
        rest = parts.shape[3:]
        flattened = parts.reshape((tile_total * NB,) + rest)
        return jnp.zeros((tile_total,) + rest, jnp.float32).at[listed_all.reshape(-1)].add(flattened)

    def born_block(block):
        data_block, listed, live_block = block
        own_part, far_part = born_pair(data_block[:, None], atom_data[listed], self_flag, live_block)
        return (lax.optimization_barrier(jnp.sum(own_part, axis=1)), far_part)
    own_sum, far_all = lax.map(born_block, (grouped(atom_data), grouped(listed_all), grouped(live_all)))
    descreen_sum = own_sum.reshape(tile_total, ATOMS) + scatter_back(far_all)
    radii_born, radius_slope = born_radius(descreen_sum, radius)

    def energy_block(block):
        data_block, radius_block, listed, live_block = block
        own_part, far_part = radius_pair(radius_block[:, None], radii_born[listed], data_block[:, None], atom_data[listed], self_flag, live_block)
        return (own_part[:, 0], far_part)
    own_sum, far_all = lax.map(energy_block, (grouped(atom_data), grouped(radii_born), grouped(listed_all), grouped(live_all)))
    gradient = own_sum.reshape(tile_total, ATOMS) + scatter_back(far_all) + 0.5 * charge * charge / (radii_born * radii_born)
    chain_coef = gradient * radius_slope

    def force_block(block):
        data_block, radius_block, chain_block, listed, live_block = block
        far_data = atom_data[listed]
        own_part, far_part = force_pair(data_block[:, None, 0:3], far_data[:, :, 0:3], data_block[:, None], far_data, radius_block[:, None], radii_born[listed], chain_block[:, None], chain_coef[listed], self_flag, live_block)
        return (own_part[:, 0], far_part)
    own_sum, far_all = lax.map(force_block, (grouped(atom_data), grouped(radii_born), grouped(chain_coef), grouped(listed_all), grouped(live_all)))
    forces = own_sum.reshape(tile_total, 3, ATOMS) + scatter_back(far_all)
    return (radii_born.reshape(SLABS, CYCLE, TILE_DEV, ATOMS), gradient.reshape(SLABS, CYCLE, TILE_DEV, ATOMS), forces.reshape(SLABS, CYCLE, TILE_DEV, 3, ATOMS))
```

```python
import functools
import math

import jax
import jax.numpy as jnp
from jax import lax
from jax.experimental import pallas as pl
from jax.experimental.pallas import tpu as pltpu
from jax.sharding import PartitionSpec as P

radius_offset = 0.09
obc_alpha = 1.0
obc_beta = 0.8
obc_gamma = 4.85
cutoff_len = 14.0
cutoff_sq = cutoff_len * cutoff_len

TILES = 32
EDGE = 2
HALF = TILES + EDGE
REGION = 2 * HALF
GROUPS = 2 * TILES
LISTED = 7
ATOMS = 128
RING = 16
LANES = (8, ATOMS)
VMEM_LIMIT = 40 * 1024 * 1024
EXP_SCALE = math.sqrt(0.25 / math.log(2.0))

ROW_X, ROW_Y, ROW_Z, ROW_Q, ROW_IN, ROW_SCALED, ROW_RADIUS, ROW_CODE = range(8)


def row_of(ref, tile, row):
    return jnp.broadcast_to(ref[tile, row : row + 1, :], LANES)


def fill_table(table, first, block, rows):
    columns = block.T
    for slot, row in enumerate(rows):
        table[first + slot] = jnp.broadcast_to(columns[:, row : row + 1], (ATOMS, ATOMS))


def fold_own(own):
    flipped = own.T
    total = flipped[0:8]
    for chunk in range(1, ATOMS // 8):
        total = total + flipped[8 * chunk : 8 * chunk + 8]
    return total


def group_row(group):
    return jnp.where(group < TILES, group, group + EDGE)


def chunk_loop(step, carry, unroll):
    return lax.fori_loop(0, ATOMS // 8, lambda c, s: step(pl.multiple_of(c * 8, 8), s), carry, unroll=unroll)


def diagonal(start):
    rows = lax.broadcasted_iota(jnp.int32, LANES, 0) + start
    lanes = lax.broadcasted_iota(jnp.int32, LANES, 1)
    return jnp.where(rows == lanes, 4.0 * cutoff_sq, 0.0)


def half_descreen(r, own, far):
    upper = r + far
    lower = r - far
    inner = jnp.minimum(jnp.maximum(own, lower), upper)
    ratio = upper * pl.reciprocal(inner, approx=True)
    slope = lower * pl.reciprocal(upper, approx=True)
    rise = ratio - 1.0
    log2x = jnp.log(ratio) * 2.0
    value = rise * (2.0 - slope * rise) - log2x
    deriv = (log2x + log2x) - (ratio * ratio - 1.0) * (slope * slope + 1.0)
    return value, deriv


def pair_shared(r2):
    inv = lax.rsqrt(r2)
    r = r2 * inv
    cut = jnp.maximum(1.0 - r2 * (1.0 / cutoff_sq), 0.0)
    cinv = cut * inv
    weight = cut * cinv
    g_deriv = cinv * cinv * inv
    g_value = cinv * (8.0 / cutoff_sq)
    return r, weight, g_deriv, g_value


def born_kernel(unroll, count, place, data, part, d_self, d_pair, table, own, far, ring, s_ring, sems, s_sems):
    far[...] = jnp.zeros_like(far)

    def separation(start, bx, by, bz):
        rows = pl.ds(start, 8)
        dx = table[0, rows, :] - bx
        dy = table[1, rows, :] - by
        dz = table[2, rows, :] - bz
        return dx * dx + dy * dy + dz * dz

    def group_step(group, done):
        tile = group_row(group)
        fill_table(table, 0, data[tile], (ROW_X, ROW_Y, ROW_Z, ROW_IN, ROW_SCALED))
        own[...] = jnp.zeros_like(own)

        @pl.when(group < TILES)
        def _():
            slot = lax.rem(group, 2)
            copy = pltpu.make_async_copy(s_ring.at[slot], d_self.at[group], s_sems.at[slot])

            @pl.when(group >= 2)
            def _():
                copy.wait()

            bx, by, bz, bs = (row_of(data, tile, row) for row in (ROW_X, ROW_Y, ROW_Z, ROW_SCALED))

            def step(start, carry):
                rows = pl.ds(start, 8)
                r2 = separation(start, bx, by, bz) + diagonal(start)
                r, weight, g_deriv, g_value = pair_shared(r2)
                value, deriv = half_descreen(r, table[3, rows, :], bs)
                own[rows, :] = weight * value
                s_ring[slot, rows, :] = g_deriv * deriv - g_value * value
                return carry

            chunk_loop(step, 0, unroll)
            copy.start()

        number = count[group]

        def pair_step(k, carry):
            index = done + k
            other = place[group, k]
            slot = lax.rem(index, RING)
            copy = pltpu.make_async_copy(ring.at[slot], d_pair.at[index], sems.at[slot])

            @pl.when(index >= RING)
            def _():
                copy.wait()

            bx, by, bz, bp, bs = (
                row_of(data, other, row) for row in (ROW_X, ROW_Y, ROW_Z, ROW_IN, ROW_SCALED)
            )

            def step(start, total):
                rows = pl.ds(start, 8)
                r2 = separation(start, bx, by, bz)
                r, weight, g_deriv, g_value = pair_shared(r2)
                value, deriv = half_descreen(r, table[3, rows, :], bs)
                own[rows, :] += weight * value
                ring[slot, 0, rows, :] = g_deriv * deriv - g_value * value
                value, deriv = half_descreen(r, bp, table[4, rows, :])
                ring[slot, 1, rows, :] = g_deriv * deriv - g_value * value
                return total + weight * value

            total = chunk_loop(step, jnp.zeros(LANES, jnp.float32), unroll)
            far[other] += total
            copy.start()
            return carry

        lax.fori_loop(0, number, pair_step, 0)
        far[tile] += fold_own(own[...])
        return done + number

    done = lax.fori_loop(0, GROUPS, group_step, 0)
    part[...] = jnp.sum(far[...], axis=1) * 0.125
    for slot in range(2):
        pltpu.make_async_copy(s_ring.at[slot], d_self.at[slot], s_sems.at[slot]).wait()
    for slot in range(RING):

        @pl.when(slot < done)
        def _():
            pltpu.make_async_copy(ring.at[slot], d_pair.at[slot], sems.at[slot]).wait()


def energy_kernel(unroll, count, place, data, born, part, force, table, own, far):
    far[...] = jnp.zeros_like(far)
    force[...] = jnp.zeros_like(force)

    def group_step(group, carry):
        tile = group_row(group)
        fill_table(table, 0, data[tile], (ROW_X, ROW_Y, ROW_Z, ROW_Q))
        fill_table(table, 4, born[tile], (0, 1))
        own[...] = jnp.zeros_like(own)

        def pair_block(other, is_self):
            bx, by, bz, bq = (row_of(data, other, row) for row in (ROW_X, ROW_Y, ROW_Z, ROW_Q))
            br, bi = row_of(born, other, 0), -row_of(born, other, 1)

            def step(start, totals):
                rows = pl.ds(start, 8)
                dx = table[0, rows, :] - bx
                dy = table[1, rows, :] - by
                dz = table[2, rows, :] - bz
                r2 = dx * dx + dy * dy + dz * dz
                if is_self:
                    r2 = r2 + diagonal(start)
                cut = jnp.maximum(1.0 - r2 * (1.0 / cutoff_sq), 0.0)
                power = r2 * (table[5, rows, :] * bi)
                decay = lax.exp2(power)
                screen = (table[4, rows, :] * br) * decay
                inv = lax.rsqrt(r2 + screen)
                lead = (cut * (table[3, rows, :] * bq)) * inv
                square = cut * (inv * inv)
                grad = (lead * square) * (screen * (1.0 - math.log(2.0) * power))
                pull = lead * (square * (4.0 - decay) + 16.0 / cutoff_sq)
                fx, fy, fz = pull * dx, pull * dy, pull * dz
                own[0, rows, :] += grad
                own[1, rows, :] += fx
                own[2, rows, :] += fy
                own[3, rows, :] += fz
                if is_self:
                    return totals
                t0, t1, t2, t3 = totals
                return (t0 + grad, t1 + fx, t2 + fy, t3 + fz)

            zero = jnp.zeros(LANES, jnp.float32)
            totals = chunk_loop(step, 0 if is_self else (zero,) * 4, unroll)
            if not is_self:
                far[other] += totals[0]
                for axis in range(3):
                    force[other, axis] -= totals[1 + axis]

        @pl.when(group < TILES)
        def _():
            pair_block(tile, True)

        def pair_step(k, c):
            pair_block(place[group, k], False)
            return c

        lax.fori_loop(0, count[group], pair_step, 0)
        far[tile] += fold_own(own[0])
        for axis in range(3):
            force[tile, axis] += fold_own(own[1 + axis])
        return carry

    lax.fori_loop(0, GROUPS, group_step, 0)
    part[...] = jnp.sum(far[...], axis=1) * 0.5


def force_kernel(unroll, count, place, data, chain, force_in, d_self, d_pair, force, table, own, far, ring, s_ring, sems, s_sems):
    far[...] = force_in[...] * 4.0

    def total_pairs(group, total):
        return total + count[group]

    pairs = lax.fori_loop(0, GROUPS, total_pairs, 0)

    def fetch(index):
        slot = lax.rem(index, RING)
        return pltpu.make_async_copy(d_pair.at[index], ring.at[slot], sems.at[slot])

    def fetch_self(index):
        slot = lax.rem(index, 2)
        return pltpu.make_async_copy(d_self.at[index], s_ring.at[slot], s_sems.at[slot])

    fetch_self(0).start()
    fetch_self(1).start()
    for index in range(RING):

        @pl.when(index < pairs)
        def _():
            fetch(index).start()

    def group_step(group, done):
        tile = group_row(group)
        fill_table(table, 0, data[tile], (ROW_X, ROW_Y, ROW_Z))
        fill_table(table, 3, chain[tile], (0,))
        own[...] = jnp.zeros_like(own)

        def pair_block(other, coefficient):
            bx, by, bz = (row_of(data, other, row) for row in (ROW_X, ROW_Y, ROW_Z))

            def step(start, totals):
                rows = pl.ds(start, 8)
                pull = coefficient(rows)
                fx = pull * (table[0, rows, :] - bx)
                fy = pull * (table[1, rows, :] - by)
                fz = pull * (table[2, rows, :] - bz)
                own[0, rows, :] += fx
                own[1, rows, :] += fy
                own[2, rows, :] += fz
                t0, t1, t2 = totals
                return (t0 + fx, t1 + fy, t2 + fz)

            zero = jnp.zeros(LANES, jnp.float32)
            totals = chunk_loop(step, (zero,) * 3, unroll)
            for axis in range(3):
                far[other, axis] -= totals[axis]

        @pl.when(group < TILES)
        def _():
            fetch_self(group).wait()
            slot = lax.rem(group, 2)
            pair_block(tile, lambda rows: table[3, rows, :] * s_ring[slot, rows, :])

            @pl.when(group < TILES - 2)
            def _():
                fetch_self(group + 2).start()

        number = count[group]

        def pair_step(k, carry):
            index = done + k
            other = place[group, k]
            slot = lax.rem(index, RING)
            fetch(index).wait()
            chain_b = row_of(chain, other, 0)
            pair_block(
                other,
                lambda rows: table[3, rows, :] * ring[slot, 0, rows, :] + chain_b * ring[slot, 1, rows, :],
            )

            @pl.when(index + RING < pairs)
            def _():
                fetch(index + RING).start()

            return carry

        lax.fori_loop(0, number, pair_step, 0)
        for axis in range(3):
            far[tile, axis] += fold_own(own[axis])
        return done + number

    lax.fori_loop(0, GROUPS, group_step, 0)
    force[...] = jnp.sum(far[...], axis=2) * (-1.0 / 16.0)


SMEM = pl.BlockSpec(memory_space=pltpu.SMEM)
VMEM = pl.BlockSpec(memory_space=pltpu.VMEM)
ANY = pl.BlockSpec(memory_space=pl.ANY)
PARAMS = pltpu.CompilerParams(vmem_limit_bytes=VMEM_LIMIT)
BLOCK = (ATOMS, ATOMS)


def f32(*shape):
    return jax.ShapeDtypeStruct(shape, jnp.float32)


def run_born(count, place, data, unroll=4):
    return pl.pallas_call(
        functools.partial(born_kernel, unroll),
        name="born_sums",
        out_shape=(
            f32(REGION, ATOMS),
            f32(TILES, *BLOCK),
            f32(GROUPS * LISTED, 2, *BLOCK),
        ),
        in_specs=[SMEM, SMEM, VMEM],
        out_specs=(VMEM, ANY, ANY),
        scratch_shapes=[
            pltpu.VMEM((5,) + BLOCK, jnp.float32),
            pltpu.VMEM(BLOCK, jnp.float32),
            pltpu.VMEM((REGION,) + LANES, jnp.float32),
            pltpu.VMEM((RING, 2) + BLOCK, jnp.float32),
            pltpu.VMEM((2,) + BLOCK, jnp.float32),
            pltpu.SemaphoreType.DMA((RING,)),
            pltpu.SemaphoreType.DMA((2,)),
        ],
        compiler_params=PARAMS,
    )(count, place, data)


def run_energy(count, place, data, born, unroll=4):
    return pl.pallas_call(
        functools.partial(energy_kernel, unroll),
        name="radius_gradient",
        out_shape=(f32(REGION, ATOMS), f32(REGION, 3, *LANES)),
        in_specs=[SMEM, SMEM, VMEM, VMEM],
        out_specs=(VMEM, VMEM),
        scratch_shapes=[
            pltpu.VMEM((6,) + BLOCK, jnp.float32),
            pltpu.VMEM((4,) + BLOCK, jnp.float32),
            pltpu.VMEM((REGION,) + LANES, jnp.float32),
        ],
        compiler_params=PARAMS,
    )(count, place, data, born)


def run_force(count, place, data, chain, force_in, d_self, d_pair, unroll=4):
    return pl.pallas_call(
        functools.partial(force_kernel, unroll),
        name="forces",
        out_shape=f32(REGION, 3, ATOMS),
        in_specs=[SMEM, SMEM, VMEM, VMEM, VMEM, ANY, ANY],
        out_specs=VMEM,
        scratch_shapes=[
            pltpu.VMEM((4,) + BLOCK, jnp.float32),
            pltpu.VMEM((3,) + BLOCK, jnp.float32),
            pltpu.VMEM((REGION, 3) + LANES, jnp.float32),
            pltpu.VMEM((RING, 2) + BLOCK, jnp.float32),
            pltpu.VMEM((2,) + BLOCK, jnp.float32),
            pltpu.SemaphoreType.DMA((RING,)),
            pltpu.SemaphoreType.DMA((2,)),
        ],
        compiler_params=PARAMS,
    )(count, place, data, chain, force_in, d_self, d_pair)


def born_radius(descreen_sum, radius, radius_in):
    scaled = radius_in * descreen_sum
    polynomial = scaled * (obc_alpha + scaled * (-obc_beta + obc_gamma * scaled))
    tangent = jnp.tanh(polynomial)
    radii_born = 1.0 / (1.0 / radius_in - tangent / radius)
    radius_slope = (
        radii_born
        * radii_born
        * (1.0 - tangent * tangent)
        / radius
        * (obc_alpha - 2.0 * obc_beta * scaled + 3.0 * obc_gamma * scaled * scaled)
        * radius_in
    )
    return (radii_born, radius_slope)


def above_to_here(block):
    ends = lax.axis_size("slab") - 1
    return lax.ppermute(block, "slab", [(i + 1, i) for i in range(ends)])


def here_to_above(block):
    ends = lax.axis_size("slab") - 1
    return lax.ppermute(block, "slab", [(i, i + 1) for i in range(ends)])


def next_to_here(block):
    count = lax.axis_size("tile")
    return lax.ppermute(block, "tile", [((i + 1) % count, i) for i in range(count)])


def here_to_next(block):
    count = lax.axis_size("tile")
    return lax.ppermute(block, "tile", [(i, (i + 1) % count) for i in range(count)])


def swap_sums(part):
    to_next = jnp.concatenate([part[TILES:HALF], part[HALF + TILES :]])
    to_last = jnp.concatenate([part[0:EDGE], part[HALF : HALF + EDGE]])
    from_last = here_to_next(to_next)
    from_next = next_to_here(to_last)
    column = jnp.concatenate(
        [
            part[0:EDGE] + from_last[0:EDGE],
            part[EDGE:TILES],
            part[TILES:HALF] + from_next[0:EDGE],
            part[HALF : HALF + EDGE] + from_last[EDGE:],
            part[HALF + EDGE : HALF + TILES],
            part[HALF + TILES :] + from_next[EDGE:],
        ]
    )
    own, above = column[0:HALF], column[HALF:]
    from_below = here_to_above(above)
    from_above = above_to_here(own)
    return jnp.concatenate([own + from_below, above + from_above])


def pair_lists(neighbours, pad_mask):
    cycle_count = lax.axis_size("tile")
    cycle_tiles = cycle_count * TILES
    slab_step = neighbours // cycle_tiles - lax.axis_index("slab")
    within = neighbours % cycle_tiles
    cycle_step = (within // TILES - lax.axis_index("tile")) % cycle_count
    place = cycle_step * TILES + within % TILES
    live = (pad_mask == 1) & (jnp.arange(neighbours.shape[1]) > 0)[None, :]
    here = jnp.where(live & (slab_step >= 0), slab_step * HALF + place, -1)
    below = jnp.where(live & (slab_step < 0), place, -1)
    return here, below


def packed(place):
    valid = place >= 0
    slots = jnp.arange(place.shape[1])
    rank = jnp.sum(valid[:, None, :] & (slots[None, None, :] < slots[None, :, None]), axis=2)
    chosen = valid[:, :, None] & (rank[:, :, None] == slots[None, None, :])
    listed = jnp.sum(jnp.where(chosen, place[:, :, None], 0), axis=1)
    return jnp.sum(valid, axis=1).astype(jnp.int32), listed.astype(jnp.int32)


def body(positions, charges, radii, scales, neighbours, pad_mask):
    coords = positions[0, 0]
    charge = charges[0, 0]
    radius = radii[0, 0]
    radius_in = radius - radius_offset
    here, below = pair_lists(neighbours[0, 0], pad_mask[0, 0])
    code = jnp.pad(below.astype(jnp.float32), ((0, 0), (0, ATOMS - below.shape[1])))
    own = jnp.concatenate(
        [coords, jnp.stack([charge, radius_in, scales[0, 0] * radius_in, radius, code], axis=1)], axis=1
    )
    own = jnp.concatenate([own, next_to_here(own[0:EDGE])])
    above = above_to_here(own)
    data = jnp.concatenate([own, above])
    from_above = above[0:TILES, ROW_CODE, 0 : below.shape[1]].astype(jnp.int32)
    has_above = lax.axis_index("slab") < lax.axis_size("slab") - 1
    from_above = jnp.where(has_above, from_above, -1)
    count, place = packed(jnp.concatenate([here, from_above]))

    part, d_self, d_pair = run_born(count, place, data)
    radii_born, radius_slope = born_radius(swap_sums(part), data[:, ROW_RADIUS], data[:, ROW_IN])
    inverse = 1.0 / radii_born
    born = jnp.stack([radii_born, EXP_SCALE * inverse], axis=1)
    part, force = run_energy(count, place, data, born)
    own_charge = data[0:TILES, ROW_Q] * inverse[0:TILES]
    part = part * inverse + jnp.pad(0.5 * own_charge * own_charge, ((0, REGION - TILES), (0, 0)))
    gradient = swap_sums(part)
    chain = (gradient * radius_slope)[:, None]
    force = run_force(count, place, data, chain, force, d_self, d_pair)
    back = here_to_above(force[HALF:])
    mine = force[0:HALF] + back
    last = here_to_next(mine[TILES:])
    forces = jnp.concatenate([mine[0:EDGE] + last, mine[EDGE:TILES]])
    return (radii_born[None, None, 0:TILES], gradient[None, None, 0:TILES], forces[None, None])


def solution(mesh):
    return jax.shard_map(
        body,
        mesh=mesh,
        in_specs=(
            P("slab", "tile", None, None, None),
            P("slab", "tile", None, None),
            P("slab", "tile", None, None),
            P("slab", "tile", None, None),
            P("slab", "tile", None, None),
            P("slab", "tile", None, None),
        ),
        out_specs=(
            P("slab", "tile", None, None),
            P("slab", "tile", None, None),
            P("slab", "tile", None, None, None),
        ),
        check_vma=False,
    )
```

```python
import functools
import math

import jax
import jax.numpy as jnp
import numpy as np
from jax import lax
from jax.experimental import pallas as pl
from jax.experimental.pallas import tpu as pltpu
from jax.sharding import PartitionSpec as P

radius_offset = 0.09
obc_alpha = 1.0
obc_beta = 0.8
obc_gamma = 4.85
cutoff_len = 14.0
cutoff_sq = cutoff_len * cutoff_len

TILES = 32
EDGE = 2
HALF = TILES + EDGE
REGION = 2 * HALF
OWN_ROWS = HALF + 1
ALL_ROWS = REGION + 1
LISTED = 7
ATOMS = 128
CHUNK = 16
CHUNKS = ATOMS // CHUNK
FULL_WIDTH = 2
PART_WIDTH = 4
FULL_RING = 32
PART_RING = 32
SELF_WIDTH = 4
PAIRS = 2 * TILES * LISTED + 4
ITEMS = 512
DUMMY = HALF * ATOMS + REGION
ROW = (1, ATOMS)
LANES = (8, ATOMS)
ROWS = (CHUNK, ATOMS)
BLOCK = (ATOMS, ATOMS)
PART = ATOMS // 2
VMEM_LIMIT = 56 * 1024 * 1024
SCALE = math.sqrt(8.0) / cutoff_len
CUT = 8.0
EXP_SCALE = math.sqrt(0.25 / math.log(2.0)) / SCALE

ROW_X, ROW_Y, ROW_Z, ROW_Q, ROW_IN, ROW_SCALED, ROW_RADIUS, ROW_CODE = range(8)

F32 = jnp.float32


def fold2(block):
    return block[0:8] + block[8:16]


def fold_own(own):
    flipped = own.T
    total = flipped[0:8]
    for chunk in range(1, ATOMS // 8):
        total = total + flipped[8 * chunk : 8 * chunk + 8]
    return total


def by_fours(step):
    def fours(index, carry):
        start = jnp.minimum(index * 4, HALF - 4)
        for k in range(4):
            step(start + k)
        return carry

    lax.fori_loop(0, (HALF + 3) // 4, fours, 0)


def fill_table(table, tile, first, ref, rows, factor=None):
    for slot, row in enumerate(rows):
        values = ref[tile, row : row + 1, :]
        if factor is not None:
            values = values * factor
        table[tile, first + slot] = jnp.broadcast_to(values, BLOCK).T


def fold_rows(own, target, index):
    def fours(quad, carry):
        for k in range(4):
            tile = quad * 4 + k
            target[(tile,) + index] += fold_own(own[(tile,) + index])
        return carry

    lax.fori_loop(0, TILES // 4, fours, 0)
    for tile in range(TILES, HALF):
        target[(tile,) + index] += fold_own(own[(tile,) + index])


def clear(ref):
    def step(tile, carry):
        ref[tile] = jnp.zeros(ref.shape[1:], F32)
        return carry

    lax.fori_loop(0, ref.shape[0], step, 0)


def diagonal(start):
    rows = lax.broadcasted_iota(jnp.int32, ROWS, 0) + start
    return jnp.where(rows == lax.broadcasted_iota(jnp.int32, ROWS, 1), 4.0 * CUT, 0.0)


def decode(item):
    return lax.shift_right_logical(item, 7), lax.bitwise_and(item, ATOMS - 1)


def span(start):
    return pl.ds(start if isinstance(start, int) else pl.multiple_of(start, CHUNK), CHUNK)


def part_starts(code):
    return [lax.bitwise_and(lax.shift_right_logical(code, 3 * j), 7) * CHUNK for j in range(CHUNKS // 2)]


def row_of(ref, tile, row):
    return jnp.broadcast_to(ref[tile, row : row + 1, :], ROWS)


def differences(table, tile, rows, far):
    return tuple(table[tile, axis, rows, :] - far[axis] for axis in range(3))


def distance_squared(gaps):
    dx, dy, dz = gaps
    return dx * dx + dy * dy + dz * dz


def half_descreen(r, own, far):
    upper = r + far
    lower = r - far
    inner = jnp.minimum(jnp.maximum(own, lower), upper)
    ratio = upper * pl.reciprocal(inner, approx=True)
    slope = lower * pl.reciprocal(upper, approx=True)
    square = ratio * ratio
    rise = ratio - 1.0
    twice = jnp.log(square)
    value = rise * (2.0 - slope * rise) - twice
    deriv = (twice + twice) - (square - 1.0) * (slope * slope + 1.0)
    return value, deriv


def ring_copies(ring, blocks, sems, size, rows):
    def copy(index, place, inward):
        slot = lax.rem(index, size)
        here = ring.at[slot]
        there = blocks.at[place, :, pl.ds(0, rows), :]
        source, target = (there, here) if inward else (here, there)
        return pltpu.make_async_copy(source, target, sems.at[slot])

    return copy


def born_kernel(total, items, reach, data, part, d_self, d_pair, table, own, far, rings, sems):
    full_ring, part_ring, self_ring = rings
    full_sems, part_sems, self_sems = sems
    far[...] = jnp.zeros_like(far)
    fulls, parts = total[0], total[1]

    def prepare(tile):
        fill_table(table, tile, 0, data, (ROW_X, ROW_Y, ROW_Z, ROW_IN, ROW_SCALED))

    by_fours(prepare)
    for tile in range(TILES, OWN_ROWS):
        own[tile] = jnp.zeros(BLOCK, F32)

    def shared(tile, rows, r2):
        inv = lax.rsqrt(r2)
        cut = jnp.maximum(1.0 - r2 * (1.0 / CUT), 0.0)
        cinv = cut * inv
        return r2 * inv, cut, cinv, cinv * cinv * inv

    def self_pair(tile):
        far_xyz = [row_of(data, tile, axis) for axis in range(3)]
        bs = row_of(data, tile, ROW_SCALED)
        for start in range(0, ATOMS, CHUNK):
            rows = span(start)
            r2 = distance_squared(differences(table, tile, rows, far_xyz)) + diagonal(start)
            r, cut, cinv, g_deriv = shared(tile, rows, r2)
            value, deriv = half_descreen(r, table[tile, 3, rows, :], bs)
            value = cinv * value
            own[tile, rows, :] = cut * value
            self_ring[tile, rows, :] = g_deriv * deriv - value

    def self_copy(tile):
        return pltpu.make_async_copy(self_ring.at[tile], d_self.at[tile], self_sems.at[tile])

    def self_step(quad, carry):
        for k in range(SELF_WIDTH):
            self_pair(quad * SELF_WIDTH + k)
        for k in range(SELF_WIDTH):
            self_copy(quad * SELF_WIDTH + k).start()
        return carry

    lax.fori_loop(0, TILES // SELF_WIDTH, self_step, 0)

    def pair(item, ring, slot, starts):
        first, second = item
        far_xyz = [row_of(data, second, axis) for axis in range(3)]
        bp, bs = row_of(data, second, ROW_IN), row_of(data, second, ROW_SCALED)
        sums = jnp.zeros(ROWS, F32)
        for place, start in enumerate(starts):
            rows = span(start)
            kept = span(place * CHUNK)
            r2 = distance_squared(differences(table, first, rows, far_xyz))
            r, cut, cinv, g_deriv = shared(first, rows, r2)
            value, deriv = half_descreen(r, table[first, 3, rows, :], bs)
            value = cinv * value
            own[first, rows, :] += cut * value
            ring[slot, 0, kept, :] = g_deriv * deriv - value
            value, deriv = half_descreen(r, bp, table[first, 4, rows, :])
            value = cinv * value
            ring[slot, 1, kept, :] = g_deriv * deriv - value
            sums = sums + cut * value
        far[second] += fold2(sums)

    def run(width, size, ring, ring_sems, base, number, rows, starts_of):
        copy = ring_copies(ring, d_pair, ring_sems, size, rows)

        def body(index, carry):
            begin = index * width
            for k in range(width):

                @pl.when(begin + k >= size)
                def _():
                    copy(begin + k, base + begin + k, False).wait()

            for k in range(width):
                item = decode(items[base + begin + k])
                pair(item, ring, lax.rem(begin + k, size), starts_of(item))
            for k in range(width):
                copy(begin + k, base + begin + k, False).start()
            return carry

        lax.fori_loop(0, lax.div(number, width), body, 0)

    def drain(size, ring, ring_sems, number, rows):
        copy = ring_copies(ring, d_pair, ring_sems, size, rows)

        def wait(slot, carry):
            copy(slot, slot, False).wait()
            return carry

        lax.fori_loop(0, jnp.minimum(number, size), wait, 0)

    def listed_starts(item):
        return part_starts(reach[item[0] * ALL_ROWS + item[1]])

    run(FULL_WIDTH, FULL_RING, full_ring, full_sems, 0, fulls, ATOMS, lambda item: range(0, ATOMS, CHUNK))
    run(PART_WIDTH, PART_RING, part_ring, part_sems, fulls, parts, PART, listed_starts)
    fold_rows(own, far, ())
    part[...] = jnp.sum(far[0:REGION], axis=1) * (0.125 * SCALE)
    for tile in range(TILES):
        self_copy(tile).wait()
    drain(FULL_RING, full_ring, full_sems, fulls, ATOMS)
    drain(PART_RING, part_ring, part_sems, parts, PART)


def energy_kernel(total, items, reach, data, born, part, force, table, own, far):
    far[...] = jnp.zeros_like(far)
    force[...] = jnp.zeros_like(force)
    fulls, parts = total[0], total[1]

    def prepare(tile):
        fill_table(table, tile, 0, data, (ROW_X, ROW_Y, ROW_Z, ROW_Q))
        fill_table(table, tile, 4, born, (0, 1))

    by_fours(prepare)
    for tile in range(TILES, OWN_ROWS):
        own[tile] = jnp.zeros((4,) + BLOCK, F32)

    def pair(first, second, starts, is_self):
        far_xyz = [row_of(data, second, axis) for axis in range(3)]
        br, bi, bq = row_of(born, second, 0), -row_of(born, second, 1), row_of(data, second, ROW_Q)
        sums = [jnp.zeros(ROWS, F32)] * 4
        for start in starts:
            rows = span(start)
            gaps = differences(table, first, rows, far_xyz)
            r2 = distance_squared(gaps)
            if is_self:
                r2 = r2 + diagonal(start)
            cut = jnp.maximum(1.0 - r2 * (1.0 / CUT), 0.0)
            power = r2 * (table[first, 5, rows, :] * bi)
            decay = lax.exp2(power)
            screen = (table[first, 4, rows, :] * br) * decay
            inv = lax.rsqrt(r2 + screen)
            lead = (cut * (table[first, 3, rows, :] * bq)) * inv
            square = cut * (inv * inv)
            grad = (lead * square) * (screen * (1.0 - math.log(2.0) * power))
            pull = lead * (square * (4.0 - decay) + 16.0 / CUT)
            terms = [grad] + [pull * gap for gap in gaps]
            for which, term in enumerate(terms):
                if is_self:
                    own[first, which, rows, :] = term
                else:
                    own[first, which, rows, :] += term
                    sums[which] = sums[which] + term
        if not is_self:
            far[second] += fold2(sums[0])
            for axis in range(3):
                force[second, axis] -= fold2(sums[1 + axis])

    def self_step(quad, carry):
        for k in range(2):
            pair(quad * 2 + k, quad * 2 + k, range(0, ATOMS, CHUNK), True)
        return carry

    lax.fori_loop(0, TILES // 2, self_step, 0)

    def full_step(index, carry):
        for k in range(FULL_WIDTH):
            first, second = decode(items[index * FULL_WIDTH + k])
            pair(first, second, range(0, ATOMS, CHUNK), False)
        return carry

    def part_step(index, carry):
        for k in range(PART_WIDTH):
            first, second = decode(items[fulls + index * PART_WIDTH + k])
            pair(first, second, part_starts(reach[first * ALL_ROWS + second]), False)
        return carry

    lax.fori_loop(0, lax.div(fulls, FULL_WIDTH), full_step, 0)
    lax.fori_loop(0, lax.div(parts, PART_WIDTH), part_step, 0)

    def fold_step(pairs, carry):
        for k in range(2):
            tile = pairs * 2 + k
            far[tile] += fold_own(own[tile, 0])
            for axis in range(3):
                force[tile, axis] += fold_own(own[tile, 1 + axis])
        return carry

    lax.fori_loop(0, HALF // 2, fold_step, 0)
    part[...] = jnp.sum(far[0:REGION], axis=1) * (0.5 * SCALE)


def force_kernel(total, items, reach, data, chain, force_in, d_self, d_pair, force, table, own, far, rings, sems):
    full_ring, part_ring, self_ring = rings
    full_sems, part_sems, self_sems = sems
    far[...] = force_in[...] * 4.0
    fulls, parts = total[0], total[1]
    full_copy = ring_copies(full_ring, d_pair, full_sems, FULL_RING, ATOMS)
    part_copy = ring_copies(part_ring, d_pair, part_sems, PART_RING, PART)

    def self_copy(tile):
        return pltpu.make_async_copy(d_self.at[tile], self_ring.at[tile], self_sems.at[tile])

    def start(copy, base):
        def step(index, carry):
            copy(index, base + index, True).start()
            return carry

        return step

    for tile in range(TILES):
        self_copy(tile).start()
    lax.fori_loop(0, jnp.minimum(fulls, FULL_RING), start(full_copy, 0), 0)
    lax.fori_loop(0, jnp.minimum(parts, PART_RING), start(part_copy, fulls), 0)

    def prepare(tile):
        fill_table(table, tile, 0, data, (ROW_X, ROW_Y, ROW_Z))
        fill_table(table, tile, 3, chain, (0,))

    by_fours(prepare)
    for tile in range(TILES, OWN_ROWS):
        own[tile] = jnp.zeros((3,) + BLOCK, F32)

    def pair(first, second, starts, pull_of, is_self):
        far_xyz = [row_of(data, second, axis) for axis in range(3)]
        sums = [jnp.zeros(ROWS, F32)] * 3
        for place, start in enumerate(starts):
            rows = span(start)
            pull = pull_of(rows, span(place * CHUNK))
            terms = [pull * gap for gap in differences(table, first, rows, far_xyz)]
            for which, term in enumerate(terms):
                if is_self:
                    own[first, which, rows, :] = term
                else:
                    own[first, which, rows, :] += term
                sums[which] = sums[which] + term
        for axis in range(3):
            far[second, axis] -= fold2(sums[axis])

    def self_step(quad, carry):
        begin = quad * SELF_WIDTH
        for k in range(SELF_WIDTH):
            self_copy(begin + k).wait()
        for k in range(SELF_WIDTH):
            tile = begin + k
            pair(
                tile,
                tile,
                range(0, ATOMS, CHUNK),
                lambda rows, kept: table[tile, 3, rows, :] * self_ring[tile, kept, :],
                True,
            )
        return carry

    lax.fori_loop(0, TILES // SELF_WIDTH, self_step, 0)

    def run(width, size, ring, copy, base, number, starts_of):
        def body(index, carry):
            begin = index * width
            for k in range(width):
                copy(begin + k, base + begin + k, True).wait()
            for k in range(width):
                first, second = decode(items[base + begin + k])
                slot = lax.rem(begin + k, size)
                factor = row_of(chain, second, 0)
                pair(
                    first,
                    second,
                    starts_of(first, second),
                    lambda rows, kept: table[first, 3, rows, :] * ring[slot, 0, kept, :]
                    + factor * ring[slot, 1, kept, :],
                    False,
                )
            for k in range(width):

                @pl.when(begin + k + size < number)
                def _():
                    copy(begin + k + size, base + begin + k + size, True).start()

            return carry

        lax.fori_loop(0, lax.div(number, width), body, 0)

    run(FULL_WIDTH, FULL_RING, full_ring, full_copy, 0, fulls, lambda *_: range(0, ATOMS, CHUNK))
    run(
        PART_WIDTH,
        PART_RING,
        part_ring,
        part_copy,
        fulls,
        parts,
        lambda first, second: part_starts(reach[first * ALL_ROWS + second]),
    )

    def fold_step(pairs, carry):
        for k in range(2):
            tile = pairs * 2 + k
            for axis in range(3):
                far[tile, axis] += fold_own(own[tile, axis])
        return carry

    lax.fori_loop(0, HALF // 2, fold_step, 0)
    force[...] = jnp.sum(far[0:REGION], axis=2) * (-SCALE * SCALE / 16.0)


SMEM = pl.BlockSpec(memory_space=pltpu.SMEM)
VMEM = pl.BlockSpec(memory_space=pltpu.VMEM)
ANY = pl.BlockSpec(memory_space=pl.ANY)
PARAMS = pltpu.CompilerParams(vmem_limit_bytes=VMEM_LIMIT)
RING_BLOCKS = (
    pltpu.VMEM((FULL_RING, 2) + BLOCK, F32),
    pltpu.VMEM((PART_RING, 2, PART, ATOMS), F32),
    pltpu.VMEM((TILES,) + BLOCK, F32),
)
RING_SEMS = (
    pltpu.SemaphoreType.DMA((FULL_RING,)),
    pltpu.SemaphoreType.DMA((PART_RING,)),
    pltpu.SemaphoreType.DMA((TILES,)),
)


def f32(*shape):
    return jax.ShapeDtypeStruct(shape, F32)


def run_born(total, items, reach, data):
    return pl.pallas_call(
        born_kernel,
        name="born_sums",
        out_shape=(f32(REGION, ATOMS), f32(TILES, *BLOCK), f32(PAIRS, 2, *BLOCK)),
        in_specs=[SMEM, SMEM, SMEM, VMEM],
        out_specs=(VMEM, ANY, ANY),
        scratch_shapes=[
            pltpu.VMEM((OWN_ROWS, 5) + BLOCK, F32),
            pltpu.VMEM((OWN_ROWS,) + BLOCK, F32),
            pltpu.VMEM((ALL_ROWS,) + LANES, F32),
            RING_BLOCKS,
            RING_SEMS,
        ],
        compiler_params=PARAMS,
    )(total, items, reach, data)


def run_energy(total, items, reach, data, born):
    return pl.pallas_call(
        energy_kernel,
        name="radius_gradient",
        out_shape=(f32(REGION, ATOMS), f32(ALL_ROWS, 3, *LANES)),
        in_specs=[SMEM, SMEM, SMEM, VMEM, VMEM],
        out_specs=(VMEM, VMEM),
        scratch_shapes=[
            pltpu.VMEM((OWN_ROWS, 6) + BLOCK, F32),
            pltpu.VMEM((OWN_ROWS, 4) + BLOCK, F32),
            pltpu.VMEM((ALL_ROWS,) + LANES, F32),
        ],
        compiler_params=PARAMS,
    )(total, items, reach, data, born)


def run_force(total, items, reach, data, chain, force_in, d_self, d_pair):
    return pl.pallas_call(
        force_kernel,
        name="forces",
        out_shape=f32(REGION, 3, ATOMS),
        in_specs=[SMEM, SMEM, SMEM, VMEM, VMEM, VMEM, ANY, ANY],
        out_specs=VMEM,
        scratch_shapes=[
            pltpu.VMEM((OWN_ROWS, 4) + BLOCK, F32),
            pltpu.VMEM((OWN_ROWS, 3) + BLOCK, F32),
            pltpu.VMEM((ALL_ROWS, 3) + LANES, F32),
            RING_BLOCKS,
            RING_SEMS,
        ],
        compiler_params=PARAMS,
    )(total, items, reach, data, chain, force_in, d_self, d_pair)


def born_radius(descreen_sum, radius, radius_in):
    scaled = radius_in * descreen_sum
    polynomial = scaled * (obc_alpha + scaled * (-obc_beta + obc_gamma * scaled))
    tangent = jnp.tanh(polynomial)
    radii_born = 1.0 / (1.0 / radius_in - tangent / radius)
    radius_slope = (
        radii_born
        * radii_born
        * (1.0 - tangent * tangent)
        / radius
        * (obc_alpha - 2.0 * obc_beta * scaled + 3.0 * obc_gamma * scaled * scaled)
        * radius_in
    )
    return (radii_born, radius_slope)


def above_to_here(block):
    ends = lax.axis_size("slab") - 1
    return lax.ppermute(block, "slab", [(i + 1, i) for i in range(ends)])


def here_to_above(block):
    ends = lax.axis_size("slab") - 1
    return lax.ppermute(block, "slab", [(i, i + 1) for i in range(ends)])


def next_to_here(block):
    count = lax.axis_size("tile")
    return lax.ppermute(block, "tile", [((i + 1) % count, i) for i in range(count)])


def here_to_next(block):
    count = lax.axis_size("tile")
    return lax.ppermute(block, "tile", [(i, (i + 1) % count) for i in range(count)])


def swap_sums(part):
    to_next = jnp.concatenate([part[TILES:HALF], part[HALF + TILES :]])
    to_last = jnp.concatenate([part[0:EDGE], part[HALF : HALF + EDGE]])
    from_last = here_to_next(to_next)
    from_next = next_to_here(to_last)
    column = jnp.concatenate(
        [
            part[0:EDGE] + from_last[0:EDGE],
            part[EDGE:TILES],
            part[TILES:HALF] + from_next[0:EDGE],
            part[HALF : HALF + EDGE] + from_last[EDGE:],
            part[HALF + EDGE : HALF + TILES],
            part[HALF + TILES :] + from_next[EDGE:],
        ]
    )
    own, above = column[0:HALF], column[HALF:]
    from_below = here_to_above(above)
    from_above = above_to_here(own)
    return jnp.concatenate([own + from_below, above + from_above])


def pair_lists(neighbours, pad_mask):
    cycle_count = lax.axis_size("tile")
    cycle_tiles = cycle_count * TILES
    slab_step = neighbours // cycle_tiles - lax.axis_index("slab")
    within = neighbours % cycle_tiles
    cycle_step = (within // TILES - lax.axis_index("tile")) % cycle_count
    place = cycle_step * TILES + within % TILES
    live = (pad_mask == 1) & (jnp.arange(neighbours.shape[1]) > 0)[None, :]
    here = jnp.where(live & (slab_step >= 0), slab_step * HALF + place, -1)
    below = jnp.where(live & (slab_step < 0), place, -1)
    return here, below


def chunk_reach(data, across, along):
    inverse = lax.rsqrt(across * across + along * along)
    across, along = across * inverse, along * inverse
    x, y, z = data[:, ROW_X], data[:, ROW_Y], data[:, ROW_Z]
    turned = jnp.stack([x * across + y * along, y * across - x * along, z])
    pieces = turned.reshape(3, REGION, CHUNKS, CHUNK)
    low, high = jnp.min(pieces, axis=3), jnp.max(pieces, axis=3)
    tile_low, tile_high = jnp.min(low, axis=2), jnp.max(high, axis=2)
    near = []
    for chunk in range(CHUNKS):
        own_low, own_high = low[:, :HALF, chunk, None], high[:, :HALF, chunk, None]
        gap = jnp.maximum(jnp.maximum(tile_low[:, None, :] - own_high, own_low - tile_high[:, None, :]), 0.0)
        far = jnp.sum(gap * gap, axis=0) >= CUT * 1.001
        near.append(jnp.logical_not(far).astype(jnp.int32))
    number = sum(near)
    code = number << (3 * CHUNKS)
    before = jnp.zeros_like(number)
    for chunk in range(CHUNKS):
        rank = jnp.where(near[chunk] == 1, before, number + chunk - before)
        code = code + (chunk << (3 * rank))
        before = before + near[chunk]
    is_part = number <= CHUNKS // 2
    edge = ((0, OWN_ROWS - HALF), (0, ALL_ROWS - REGION))
    return jnp.pad(code, edge).reshape(-1), is_part


def packed(first, second, valid, is_part):
    first, second, valid = first.reshape(-1), second.reshape(-1), valid.reshape(-1)
    mine = (first[:, None] == jnp.arange(HALF)[None, :]).astype(jnp.bfloat16)
    rows = jnp.dot(mine, is_part.astype(jnp.bfloat16), preferred_element_type=F32)
    in_part = jnp.sum(jnp.where(second[:, None] == jnp.arange(REGION)[None, :], rows, 0.0), axis=1) > 0.5
    entry = jnp.arange(valid.shape[0])
    ahead = valid[None, :] & (entry[None, :] < entry[:, None]) & (in_part[None, :] == in_part[:, None])
    rank = jnp.sum(ahead, axis=1)
    fulls = jnp.sum(valid & jnp.logical_not(in_part), dtype=jnp.int32)
    parts = jnp.sum(valid & in_part, dtype=jnp.int32)
    fulls = (fulls + FULL_WIDTH - 1) // FULL_WIDTH * FULL_WIDTH
    parts = (parts + PART_WIDTH - 1) // PART_WIDTH * PART_WIDTH
    rank = jnp.where(in_part, fulls + rank, rank)
    chosen = valid[None, :] & (rank[None, :] == jnp.arange(ITEMS)[:, None])
    value = first * ATOMS + second - DUMMY
    items = DUMMY + jnp.sum(jnp.where(chosen, value[None, :], 0), axis=1)
    return jnp.stack([fulls, parts]), items.astype(jnp.int32)


def region_data(own, above):
    origin = jnp.pad(own[TILES // 2, 0:3, 0:1], ((0, 5), (0, 0)))
    factor = np.ones((1, 8, 1), np.float32)
    factor[0, [ROW_X, ROW_Y, ROW_Z, ROW_IN, ROW_SCALED]] = SCALE
    return jnp.concatenate([own - origin, above - origin, jnp.zeros_like(own[0:1])]) * factor


def body(positions, charges, radii, scales, neighbours, pad_mask):
    coords = positions[0, 0]
    charge = charges[0, 0]
    radius = radii[0, 0]
    radius_in = radius - radius_offset
    here, below = pair_lists(neighbours[0, 0], pad_mask[0, 0])
    code = jnp.pad(below.astype(jnp.float32), ((0, 0), (0, ATOMS - below.shape[1])))
    own = jnp.concatenate(
        [coords, jnp.stack([charge, radius_in, scales[0, 0] * radius_in, radius, code], axis=1)], axis=1
    )
    own = jnp.concatenate([own, next_to_here(own[0:EDGE])])
    above = above_to_here(own)
    data = region_data(own, above)
    listed_above = above[0:TILES, ROW_CODE, 0 : below.shape[1]].astype(jnp.int32)
    has_above = lax.axis_index("slab") < lax.axis_size("slab") - 1
    tiles = jnp.broadcast_to(jnp.arange(TILES, dtype=jnp.int32)[:, None], here.shape)
    reach, is_part = chunk_reach(data[0:REGION], coords[TILES // 2, 0, 0], coords[TILES // 2, 1, 0])
    total, items = packed(
        jnp.concatenate([tiles, listed_above]),
        jnp.concatenate([here, HALF + tiles]),
        jnp.concatenate([here >= 0, (listed_above >= 0) & has_above]),
        is_part,
    )
    region_radius = jnp.concatenate([own[:, ROW_RADIUS], above[:, ROW_RADIUS]])
    region_in = jnp.concatenate([own[:, ROW_IN], above[:, ROW_IN]])

    part, d_self, d_pair = run_born(total, items, reach, data)
    radii_born, radius_slope = born_radius(swap_sums(part), region_radius, region_in)
    inverse = 1.0 / radii_born
    born = jnp.stack([SCALE * radii_born, EXP_SCALE * inverse], axis=1)
    part, force = run_energy(total, items, reach, data, jnp.pad(born, ((0, 1), (0, 0), (0, 0))))
    own_charge = charge * inverse[0:TILES]
    part = part * inverse + jnp.pad(0.5 * own_charge * own_charge, ((0, REGION - TILES), (0, 0)))
    gradient = swap_sums(part)
    chain = jnp.pad((gradient * radius_slope)[:, None], ((0, 1), (0, 0), (0, 0)))
    force = run_force(total, items, reach, data, chain, force, d_self, d_pair)
    back = here_to_above(force[HALF:])
    mine = force[0:HALF] + back
    last = here_to_next(mine[TILES:])
    forces = jnp.concatenate([mine[0:EDGE] + last, mine[EDGE:TILES]])
    return (radii_born[None, None, 0:TILES], gradient[None, None, 0:TILES], forces[None, None])


def solution(mesh):
    return jax.shard_map(
        body,
        mesh=mesh,
        in_specs=(
            P("slab", "tile", None, None, None),
            P("slab", "tile", None, None),
            P("slab", "tile", None, None),
            P("slab", "tile", None, None),
            P("slab", "tile", None, None),
            P("slab", "tile", None, None),
        ),
        out_specs=(
            P("slab", "tile", None, None),
            P("slab", "tile", None, None),
            P("slab", "tile", None, None, None),
        ),
        check_vma=False,
    )
```

```python
import functools
import math

import jax
import jax.numpy as jnp
import numpy as np
from jax import lax
from jax.experimental import pallas as pl
from jax.experimental.pallas import tpu as pltpu
from jax.sharding import PartitionSpec as P

radius_offset = 0.09
obc_alpha = 1.0
obc_beta = 0.8
obc_gamma = 4.85
cutoff_len = 14.0
cutoff_sq = cutoff_len * cutoff_len

TILES = 32
EDGE = 2
LIVE = TILES + EDGE
HALF = 40
REGION = 2 * HALF
OWN_ROWS = LIVE + 1
SENT_ROWS = 6 * TILES + 8
LISTED = 7
ATOMS = 128
CHUNK = 16
CHUNKS = ATOMS // CHUNK
FULL_WIDTH = 2
PART_WIDTH = 4
FULL_RING = 32
PART_RING = 32
SELF_WIDTH = 4
PAIRS = 2 * TILES * LISTED + 4
ITEMS = 512
DUMMY = LIVE * ATOMS + LIVE
ROW = (1, ATOMS)
LANES = (8, ATOMS)
ROWS = (CHUNK, ATOMS)
BLOCK = (ATOMS, ATOMS)
PART = ATOMS // 2
VMEM_LIMIT = 56 * 1024 * 1024
SCALE = math.sqrt(8.0) / cutoff_len
CUT = 8.0
EXP_SCALE = math.sqrt(0.25 / math.log(2.0)) / SCALE

ROW_X, ROW_Y, ROW_Z, ROW_Q, ROW_IN, ROW_SCALED = range(6)
AT_Q, AT_RADIUS, AT_SCALED = 3, 4, 5

F32 = jnp.float32


def fold2(block):
    return block[0:8] + block[8:16]


def fold_own(own):
    flipped = own.T
    total = flipped[0:8]
    for chunk in range(1, ATOMS // 8):
        total = total + flipped[8 * chunk : 8 * chunk + 8]
    return total


def by_fours(step):
    def fours(index, carry):
        start = jnp.minimum(index * 4, LIVE - 4)
        for k in range(4):
            step(start + k)
        return carry

    lax.fori_loop(0, (LIVE + 3) // 4, fours, 0)


def fill_table(table, tile, first, ref, rows, factor=None):
    for slot, row in enumerate(rows):
        values = ref[tile, row : row + 1, :]
        if factor is not None:
            values = values * factor
        table[tile, first + slot] = jnp.broadcast_to(values, BLOCK).T


def fold_rows(own, target, index):
    def fours(quad, carry):
        for k in range(4):
            tile = quad * 4 + k
            target[(tile,) + index] += fold_own(own[(tile,) + index])
        return carry

    lax.fori_loop(0, TILES // 4, fours, 0)
    for tile in range(TILES, LIVE):
        target[(tile,) + index] += fold_own(own[(tile,) + index])


def diagonal(start):
    rows = lax.broadcasted_iota(jnp.int32, ROWS, 0) + start
    return jnp.where(rows == lax.broadcasted_iota(jnp.int32, ROWS, 1), 4.0 * CUT, 0.0)


def decode(item):
    return lax.shift_right_logical(item, 7), lax.bitwise_and(item, ATOMS - 1)


def span(start):
    return pl.ds(start if isinstance(start, int) else pl.multiple_of(start, CHUNK), CHUNK)


def part_starts(code):
    return [lax.bitwise_and(lax.shift_right_logical(code, 3 * j), 7) * CHUNK for j in range(CHUNKS // 2)]


def row_of(ref, tile, row):
    return jnp.broadcast_to(ref[tile, row : row + 1, :], ROWS)


def differences(table, tile, rows, far):
    return tuple(table[tile, axis, rows, :] - far[axis] for axis in range(3))


def distance_squared(gaps):
    dx, dy, dz = gaps
    return dx * dx + dy * dy + dz * dz


def half_descreen(r, own, far):
    upper = r + far
    lower = r - far
    inner = jnp.minimum(jnp.maximum(own, lower), upper)
    ratio = upper * pl.reciprocal(inner, approx=True)
    slope = lower * pl.reciprocal(upper, approx=True)
    square = ratio * ratio
    rise = ratio - 1.0
    twice = jnp.log(square)
    value = rise * (2.0 - slope * rise) - twice
    deriv = (twice + twice) - (square - 1.0) * (slope * slope + 1.0)
    return value, deriv


def ring_copies(ring, blocks, sems, size, rows):
    def copy(index, place, inward):
        slot = lax.rem(index, size)
        here = ring.at[slot]
        there = blocks.at[place, :, pl.ds(0, rows), :]
        source, target = (there, here) if inward else (here, there)
        return pltpu.make_async_copy(source, target, sems.at[slot])

    return copy


def edge_rows(target, values, first, second):
    target[...] = jnp.zeros_like(target)
    target[0:EDGE, :] = values[first : first + EDGE]
    target[EDGE : 2 * EDGE, :] = values[second : second + EDGE]


def pack_kernel(positions, charges, radii, scales, neighbours, pad_mask, sent, edges, here):
    radius = radii[...]
    values = [positions[0], positions[1], positions[2], charges[...], radius, scales[...] * (radius - radius_offset)]
    edges[...] = jnp.zeros_like(edges)
    for index, value in enumerate(values):
        sent[index * TILES : (index + 1) * TILES, :] = value
        edges[EDGE * index : EDGE * (index + 1), :] = value[0:EDGE]
    cycle_count = lax.axis_size("tile")
    cycle_tiles = cycle_count * TILES
    listed = neighbours[...]
    slab_step = lax.div(listed, cycle_tiles) - lax.axis_index("slab")
    within = lax.rem(listed, cycle_tiles)
    cycle_step = lax.rem(lax.div(within, TILES) - lax.axis_index("tile") + cycle_count, cycle_count)
    place = cycle_step * TILES + lax.rem(within, TILES)
    slots = lax.broadcasted_iota(jnp.int32, listed.shape, 0)
    live = (pad_mask[...] == 1) & (slots > 0)
    here[...] = jnp.where(live & (slab_step >= 0), slab_step * HALF + place, -1)
    sent[6 * TILES :, :] = jnp.full(LANES, -1.0, F32)
    sent[6 * TILES :, 0:TILES] = jnp.where(live & (slab_step < 0), place, -1).astype(F32)


def born_kernel(
    total, items, reach, sent, edges, above, above_edges,
    own_part, above_part, to_next, to_last, data, plain, d_self, d_pair,
    table, own, far, rings, sems,
):
    full_ring, part_ring, self_ring = rings
    full_sems, part_sems, self_sems = sems
    far[...] = jnp.zeros_like(far)
    data[...] = jnp.zeros_like(data)
    plain[...] = jnp.ones_like(plain)
    fulls, parts = total[0], total[1]

    for index in range(6):
        origin = sent[index * TILES + TILES // 2 : index * TILES + TILES // 2 + 1, 0:1]
        for start, source, edge in ((0, sent, edges), (HALF, above, above_edges)):
            for place, values in (
                (start, source[index * TILES : (index + 1) * TILES, :]),
                (start + TILES, edge[EDGE * index : EDGE * (index + 1), :]),
            ):
                rows = slice(place, place + values.shape[0])
                if index < AT_Q:
                    data[rows, index, :] = (values - origin) * SCALE
                elif index == AT_Q:
                    data[rows, ROW_Q, :] = values
                    plain[2, rows, :] = values if place == 0 else jnp.zeros_like(values)
                elif index == AT_RADIUS:
                    data[rows, ROW_IN, :] = (values - radius_offset) * SCALE
                    plain[0, rows, :] = values
                    plain[1, rows, :] = values - radius_offset
                else:
                    data[rows, ROW_SCALED, :] = values * SCALE

    def prepare(tile):
        fill_table(table, tile, 0, data, (ROW_X, ROW_Y, ROW_Z, ROW_IN, ROW_SCALED))

    by_fours(prepare)
    for tile in range(TILES, OWN_ROWS):
        own[tile] = jnp.zeros(BLOCK, F32)

    def shared(tile, rows, r2):
        inv = lax.rsqrt(r2)
        cut = jnp.maximum(1.0 - r2 * (1.0 / CUT), 0.0)
        cinv = cut * inv
        return r2 * inv, cut, cinv, cinv * cinv * inv

    def self_pair(tile):
        far_xyz = [row_of(data, tile, axis) for axis in range(3)]
        bs = row_of(data, tile, ROW_SCALED)
        for start in range(0, ATOMS, CHUNK):
            rows = span(start)
            r2 = distance_squared(differences(table, tile, rows, far_xyz)) + diagonal(start)
            r, cut, cinv, g_deriv = shared(tile, rows, r2)
            value, deriv = half_descreen(r, table[tile, 3, rows, :], bs)
            value = cinv * value
            own[tile, rows, :] = cut * value
            self_ring[tile, rows, :] = g_deriv * deriv - value

    def self_copy(tile):
        return pltpu.make_async_copy(self_ring.at[tile], d_self.at[tile], self_sems.at[tile])

    def self_step(quad, carry):
        for k in range(SELF_WIDTH):
            self_pair(quad * SELF_WIDTH + k)
        for k in range(SELF_WIDTH):
            self_copy(quad * SELF_WIDTH + k).start()
        return carry

    lax.fori_loop(0, TILES // SELF_WIDTH, self_step, 0)

    def pair(item, ring, slot, starts):
        first, second = item
        far_xyz = [row_of(data, second, axis) for axis in range(3)]
        bp, bs = row_of(data, second, ROW_IN), row_of(data, second, ROW_SCALED)
        sums = jnp.zeros(ROWS, F32)
        for place, start in enumerate(starts):
            rows = span(start)
            kept = span(place * CHUNK)
            r2 = distance_squared(differences(table, first, rows, far_xyz))
            r, cut, cinv, g_deriv = shared(first, rows, r2)
            value, deriv = half_descreen(r, table[first, 3, rows, :], bs)
            value = cinv * value
            own[first, rows, :] += cut * value
            ring[slot, 0, kept, :] = g_deriv * deriv - value
            value, deriv = half_descreen(r, bp, table[first, 4, rows, :])
            value = cinv * value
            ring[slot, 1, kept, :] = g_deriv * deriv - value
            sums = sums + cut * value
        far[second] += fold2(sums)

    def run(width, size, ring, ring_sems, base, number, rows, starts_of):
        copy = ring_copies(ring, d_pair, ring_sems, size, rows)

        def body(index, carry):
            begin = index * width
            for k in range(width):

                @pl.when(begin + k >= size)
                def _():
                    copy(begin + k, base + begin + k, False).wait()

            for k in range(width):
                item = decode(items[base + begin + k])
                pair(item, ring, lax.rem(begin + k, size), starts_of(item))
            for k in range(width):
                copy(begin + k, base + begin + k, False).start()
            return carry

        lax.fori_loop(0, lax.div(number, width), body, 0)

    def drain(size, ring, ring_sems, number, rows):
        copy = ring_copies(ring, d_pair, ring_sems, size, rows)

        def wait(slot, carry):
            copy(slot, slot, False).wait()
            return carry

        lax.fori_loop(0, jnp.minimum(number, size), wait, 0)

    def listed_starts(item):
        return part_starts(reach[item[0] * REGION + item[1]])

    run(FULL_WIDTH, FULL_RING, full_ring, full_sems, 0, fulls, ATOMS, lambda item: range(0, ATOMS, CHUNK))
    run(PART_WIDTH, PART_RING, part_ring, part_sems, fulls, parts, PART, listed_starts)
    fold_rows(own, far, ())
    sums = jnp.sum(far[...], axis=1) * (0.125 * SCALE)
    own_part[...] = sums[0:HALF]
    above_part[...] = sums[HALF:]
    edge_rows(to_next, sums, TILES, HALF + TILES)
    edge_rows(to_last, sums, 0, HALF)
    for tile in range(TILES):
        self_copy(tile).wait()
    drain(FULL_RING, full_ring, full_sems, fulls, ATOMS)
    drain(PART_RING, part_ring, part_sems, parts, PART)


def energy_kernel(
    total, items, reach, data, plain, own_part, above_part, from_below, from_above,
    radii_born, slope, own_grad, above_grad, to_next, to_last, force,
    table, own, far, born,
):
    far[...] = jnp.zeros_like(far)
    force[...] = jnp.zeros_like(force)
    fulls, parts = total[0], total[1]
    sums = jnp.concatenate([own_part[...] + from_below[...], above_part[...] + from_above[...]])
    all_radii, all_slopes = born_radius(sums, plain[0], plain[1])
    inverse = 1.0 / all_radii
    radii_born[...] = all_radii[0:TILES]
    slope[...] = all_slopes
    born[:, 0, :] = SCALE * all_radii
    born[:, 1, :] = EXP_SCALE * inverse

    def prepare(tile):
        fill_table(table, tile, 0, data, (ROW_X, ROW_Y, ROW_Z, ROW_Q))
        fill_table(table, tile, 4, born, (0, 1))

    by_fours(prepare)
    for tile in range(TILES, OWN_ROWS):
        own[tile] = jnp.zeros((4,) + BLOCK, F32)

    def pair(first, second, starts, is_self):
        far_xyz = [row_of(data, second, axis) for axis in range(3)]
        br, bi, bq = row_of(born, second, 0), -row_of(born, second, 1), row_of(data, second, ROW_Q)
        sums = [jnp.zeros(ROWS, F32)] * 4
        for start in starts:
            rows = span(start)
            gaps = differences(table, first, rows, far_xyz)
            r2 = distance_squared(gaps)
            if is_self:
                r2 = r2 + diagonal(start)
            cut = jnp.maximum(1.0 - r2 * (1.0 / CUT), 0.0)
            power = r2 * (table[first, 5, rows, :] * bi)
            decay = lax.exp2(power)
            screen = (table[first, 4, rows, :] * br) * decay
            inv = lax.rsqrt(r2 + screen)
            lead = (cut * (table[first, 3, rows, :] * bq)) * inv
            square = cut * (inv * inv)
            grad = (lead * square) * (screen * (1.0 - math.log(2.0) * power))
            pull = lead * (square * (4.0 - decay) + 16.0 / CUT)
            terms = [grad] + [pull * gap for gap in gaps]
            for which, term in enumerate(terms):
                if is_self:
                    own[first, which, rows, :] = term
                else:
                    own[first, which, rows, :] += term
                    sums[which] = sums[which] + term
        if not is_self:
            far[second] += fold2(sums[0])
            for axis in range(3):
                force[second, axis] -= fold2(sums[1 + axis])

    def self_step(quad, carry):
        for k in range(2):
            pair(quad * 2 + k, quad * 2 + k, range(0, ATOMS, CHUNK), True)
        return carry

    lax.fori_loop(0, TILES // 2, self_step, 0)

    def full_step(index, carry):
        for k in range(FULL_WIDTH):
            first, second = decode(items[index * FULL_WIDTH + k])
            pair(first, second, range(0, ATOMS, CHUNK), False)
        return carry

    def part_step(index, carry):
        for k in range(PART_WIDTH):
            first, second = decode(items[fulls + index * PART_WIDTH + k])
            pair(first, second, part_starts(reach[first * REGION + second]), False)
        return carry

    lax.fori_loop(0, lax.div(fulls, FULL_WIDTH), full_step, 0)
    lax.fori_loop(0, lax.div(parts, PART_WIDTH), part_step, 0)

    def fold_step(pairs, carry):
        for k in range(2):
            tile = pairs * 2 + k
            far[tile] += fold_own(own[tile, 0])
            for axis in range(3):
                force[tile, axis] += fold_own(own[tile, 1 + axis])
        return carry

    lax.fori_loop(0, LIVE // 2, fold_step, 0)
    charge = plain[2] * inverse
    sums = jnp.sum(far[...], axis=1) * (0.5 * SCALE) * inverse + 0.5 * charge * charge
    own_grad[...] = sums[0:HALF]
    above_grad[...] = sums[HALF:]
    edge_rows(to_next, sums, TILES, HALF + TILES)
    edge_rows(to_last, sums, 0, HALF)


def force_kernel(
    total, items, reach, data, slope, own_grad, above_grad, from_below, from_above, force_in, d_self, d_pair,
    gradient, own_force, above_force, to_next,
    table, own, far, chain, rings, sems,
):
    full_ring, part_ring, self_ring = rings
    full_sems, part_sems, self_sems = sems
    fulls, parts = total[0], total[1]
    full_copy = ring_copies(full_ring, d_pair, full_sems, FULL_RING, ATOMS)
    part_copy = ring_copies(part_ring, d_pair, part_sems, PART_RING, PART)

    def self_copy(tile):
        return pltpu.make_async_copy(d_self.at[tile], self_ring.at[tile], self_sems.at[tile])

    def start(copy, base):
        def step(index, carry):
            copy(index, base + index, True).start()
            return carry

        return step

    for tile in range(TILES):
        self_copy(tile).start()
    lax.fori_loop(0, jnp.minimum(fulls, FULL_RING), start(full_copy, 0), 0)
    lax.fori_loop(0, jnp.minimum(parts, PART_RING), start(part_copy, fulls), 0)

    far[...] = force_in[...] * 4.0
    grads = jnp.concatenate([own_grad[...] + from_below[...], above_grad[...] + from_above[...]])
    gradient[...] = grads[0:TILES]
    chain[:, 0, :] = grads * slope[...]

    def prepare(tile):
        fill_table(table, tile, 0, data, (ROW_X, ROW_Y, ROW_Z))
        fill_table(table, tile, 3, chain, (0,))

    by_fours(prepare)
    for tile in range(TILES, OWN_ROWS):
        own[tile] = jnp.zeros((3,) + BLOCK, F32)

    def pair(first, second, starts, pull_of, is_self):
        far_xyz = [row_of(data, second, axis) for axis in range(3)]
        sums = [jnp.zeros(ROWS, F32)] * 3
        for place, start in enumerate(starts):
            rows = span(start)
            pull = pull_of(rows, span(place * CHUNK))
            terms = [pull * gap for gap in differences(table, first, rows, far_xyz)]
            for which, term in enumerate(terms):
                if is_self:
                    own[first, which, rows, :] = term
                else:
                    own[first, which, rows, :] += term
                sums[which] = sums[which] + term
        for axis in range(3):
            far[second, axis] -= fold2(sums[axis])

    def self_step(quad, carry):
        begin = quad * SELF_WIDTH
        for k in range(SELF_WIDTH):
            self_copy(begin + k).wait()
        for k in range(SELF_WIDTH):
            tile = begin + k
            pair(
                tile,
                tile,
                range(0, ATOMS, CHUNK),
                lambda rows, kept: table[tile, 3, rows, :] * self_ring[tile, kept, :],
                True,
            )
        return carry

    lax.fori_loop(0, TILES // SELF_WIDTH, self_step, 0)

    def run(width, size, ring, copy, base, number, starts_of):
        def body(index, carry):
            begin = index * width
            for k in range(width):
                copy(begin + k, base + begin + k, True).wait()
            for k in range(width):
                first, second = decode(items[base + begin + k])
                slot = lax.rem(begin + k, size)
                factor = row_of(chain, second, 0)
                pair(
                    first,
                    second,
                    starts_of(first, second),
                    lambda rows, kept: table[first, 3, rows, :] * ring[slot, 0, kept, :]
                    + factor * ring[slot, 1, kept, :],
                    False,
                )
            for k in range(width):

                @pl.when(begin + k + size < number)
                def _():
                    copy(begin + k + size, base + begin + k + size, True).start()

            return carry

        lax.fori_loop(0, lax.div(number, width), body, 0)

    run(FULL_WIDTH, FULL_RING, full_ring, full_copy, 0, fulls, lambda *_: range(0, ATOMS, CHUNK))
    run(
        PART_WIDTH,
        PART_RING,
        part_ring,
        part_copy,
        fulls,
        parts,
        lambda first, second: part_starts(reach[first * REGION + second]),
    )

    def fold_step(pairs, carry):
        for k in range(2):
            tile = pairs * 2 + k
            for axis in range(3):
                far[tile, axis] += fold_own(own[tile, axis])
        return carry

    lax.fori_loop(0, LIVE // 2, fold_step, 0)
    for axis in range(3):
        sums = jnp.sum(far[:, axis], axis=1) * (-SCALE * SCALE / 16.0)
        own_force[axis] = sums[0:HALF]
        above_force[axis] = sums[HALF:]
        edge_rows(to_next.at[axis], sums, TILES, HALF + TILES)


SMEM = pl.BlockSpec(memory_space=pltpu.SMEM)
VMEM = pl.BlockSpec(memory_space=pltpu.VMEM)
ANY = pl.BlockSpec(memory_space=pl.ANY)
PARAMS = pltpu.CompilerParams(vmem_limit_bytes=VMEM_LIMIT)
RING_BLOCKS = (
    pltpu.VMEM((FULL_RING, 2) + BLOCK, F32),
    pltpu.VMEM((PART_RING, 2, PART, ATOMS), F32),
    pltpu.VMEM((TILES,) + BLOCK, F32),
)
RING_SEMS = (
    pltpu.SemaphoreType.DMA((FULL_RING,)),
    pltpu.SemaphoreType.DMA((PART_RING,)),
    pltpu.SemaphoreType.DMA((TILES,)),
)


def f32(*shape):
    return jax.ShapeDtypeStruct(shape, F32)


def run_pack(positions, charges, radii, scales, neighbours, pad_mask):
    return pl.pallas_call(
        pack_kernel,
        name="pack_atoms",
        out_shape=(
            f32(SENT_ROWS, ATOMS),
            f32(16, ATOMS),
            jax.ShapeDtypeStruct(neighbours.shape, jnp.int32),
        ),
        in_specs=[VMEM] * 6,
        out_specs=(VMEM,) * 3,
        compiler_params=PARAMS,
    )(positions, charges, radii, scales, neighbours, pad_mask)


def run_born(total, items, reach, sent, edges, above, above_edges):
    return pl.pallas_call(
        born_kernel,
        name="born_sums",
        out_shape=(
            f32(HALF, ATOMS),
            f32(HALF, ATOMS),
            f32(*LANES),
            f32(*LANES),
            f32(REGION, *LANES),
            f32(3, REGION, ATOMS),
            f32(TILES, *BLOCK),
            f32(PAIRS, 2, *BLOCK),
        ),
        in_specs=[SMEM] * 3 + [VMEM] * 4,
        out_specs=(VMEM,) * 6 + (ANY,) * 2,
        scratch_shapes=[
            pltpu.VMEM((OWN_ROWS, 5) + BLOCK, F32),
            pltpu.VMEM((OWN_ROWS,) + BLOCK, F32),
            pltpu.VMEM((REGION,) + LANES, F32),
            RING_BLOCKS,
            RING_SEMS,
        ],
        compiler_params=PARAMS,
    )(total, items, reach, sent, edges, above, above_edges)


def run_energy(total, items, reach, data, plain, shares):
    return pl.pallas_call(
        energy_kernel,
        name="radius_gradient",
        out_shape=(
            f32(TILES, ATOMS),
            f32(REGION, ATOMS),
            f32(HALF, ATOMS),
            f32(HALF, ATOMS),
            f32(*LANES),
            f32(*LANES),
            f32(REGION, 3, *LANES),
        ),
        in_specs=[SMEM] * 3 + [VMEM] * 6,
        out_specs=(VMEM,) * 7,
        scratch_shapes=[
            pltpu.VMEM((OWN_ROWS, 6) + BLOCK, F32),
            pltpu.VMEM((OWN_ROWS, 4) + BLOCK, F32),
            pltpu.VMEM((REGION,) + LANES, F32),
            pltpu.VMEM((REGION,) + LANES, F32),
        ],
        compiler_params=PARAMS,
    )(total, items, reach, data, plain, *shares)


def run_force(total, items, reach, data, slope, shares, force_in, d_self, d_pair):
    return pl.pallas_call(
        force_kernel,
        name="forces",
        out_shape=(f32(TILES, ATOMS), f32(3, HALF, ATOMS), f32(3, HALF, ATOMS), f32(3, *LANES)),
        in_specs=[SMEM] * 3 + [VMEM] * 7 + [ANY] * 2,
        out_specs=(VMEM,) * 4,
        scratch_shapes=[
            pltpu.VMEM((OWN_ROWS, 4) + BLOCK, F32),
            pltpu.VMEM((OWN_ROWS, 3) + BLOCK, F32),
            pltpu.VMEM((REGION, 3) + LANES, F32),
            pltpu.VMEM((REGION,) + LANES, F32),
            RING_BLOCKS,
            RING_SEMS,
        ],
        compiler_params=PARAMS,
    )(total, items, reach, data, slope, *shares, force_in, d_self, d_pair)


def born_radius(descreen_sum, radius, radius_in):
    scaled = radius_in * descreen_sum
    polynomial = scaled * (obc_alpha + scaled * (-obc_beta + obc_gamma * scaled))
    tangent = jnp.tanh(polynomial)
    radii_born = 1.0 / (1.0 / radius_in - tangent / radius)
    radius_slope = (
        radii_born
        * radii_born
        * (1.0 - tangent * tangent)
        / radius
        * (obc_alpha - 2.0 * obc_beta * scaled + 3.0 * obc_gamma * scaled * scaled)
        * radius_in
    )
    return (radii_born, radius_slope)


def above_to_here(block):
    ends = lax.axis_size("slab") - 1
    return lax.ppermute(block, "slab", [(i + 1, i) for i in range(ends)])


def here_to_above(block):
    ends = lax.axis_size("slab") - 1
    return lax.ppermute(block, "slab", [(i, i + 1) for i in range(ends)])


def next_to_here(block):
    count = lax.axis_size("tile")
    return lax.ppermute(block, "tile", [((i + 1) % count, i) for i in range(count)])


def here_to_next(block):
    count = lax.axis_size("tile")
    return lax.ppermute(block, "tile", [(i, (i + 1) % count) for i in range(count)])


def across_to_here(block):
    slabs, count = lax.axis_size("slab"), lax.axis_size("tile")
    pairs = [
        ((slab + 1) * count + (tile + 1) % count, slab * count + tile)
        for slab in range(slabs - 1)
        for tile in range(count)
    ]
    return lax.ppermute(block, ("slab", "tile"), pairs)


def placed(block, first, last):
    return jnp.pad(block[first : first + EDGE], ((0, HALF - EDGE), (0, 0))) + jnp.pad(
        last[first : first + EDGE], ((TILES, HALF - LIVE), (0, 0))
    )


def swap_sums(own, above, to_next, to_last):
    from_last = here_to_next(to_next)
    from_next = next_to_here(to_last)
    own = own + placed(from_last, 0, from_next)
    above = above + placed(from_last, EDGE, from_next)
    own, above = lax.optimization_barrier((own, above))
    return own, above, here_to_above(above), above_to_here(own)


def whole_slab(component, block, edges):
    first, edge = component * TILES, component * EDGE
    return [block[first : first + TILES], edges[edge : edge + EDGE], jnp.zeros((HALF - LIVE, ATOMS), F32)]


def chunk_reach(sent, edges, above, above_edges):
    x, y, z = (
        jnp.concatenate(whole_slab(axis, sent, edges) + whole_slab(axis, above, above_edges)) for axis in range(3)
    )
    across, along = sent[TILES // 2, 0], sent[TILES + TILES // 2, 0]
    inverse = lax.rsqrt(across * across + along * along)
    across, along = across * inverse, along * inverse
    turned = jnp.stack([x * across + y * along, y * across - x * along, z])
    pieces = turned.reshape(3, REGION, CHUNKS, CHUNK)
    low, high = jnp.min(pieces, axis=3), jnp.max(pieces, axis=3)
    tile_low, tile_high = jnp.min(low, axis=2), jnp.max(high, axis=2)
    near = []
    for chunk in range(CHUNKS):
        own_low, own_high = low[:, :OWN_ROWS, chunk, None], high[:, :OWN_ROWS, chunk, None]
        gap = jnp.maximum(jnp.maximum(tile_low[:, None, :] - own_high, own_low - tile_high[:, None, :]), 0.0)
        far = jnp.sum(gap * gap, axis=0) >= cutoff_sq * 1.001
        near.append(jnp.logical_not(far).astype(jnp.int32))
    number = sum(near)
    code = number << (3 * CHUNKS)
    before = jnp.zeros_like(number)
    for chunk in range(CHUNKS):
        rank = jnp.where(near[chunk] == 1, before, number + chunk - before)
        code = code + (chunk << (3 * rank))
        before = before + near[chunk]
    return code.reshape(-1), number <= CHUNKS // 2


def packed(first, second, valid, is_part):
    first, second, valid = first.reshape(-1), second.reshape(-1), valid.reshape(-1)
    mine = (first[:, None] == jnp.arange(OWN_ROWS)[None, :]).astype(jnp.bfloat16)
    rows = jnp.dot(mine, is_part.astype(jnp.bfloat16), preferred_element_type=F32)
    in_part = jnp.sum(jnp.where(second[:, None] == jnp.arange(REGION)[None, :], rows, 0.0), axis=1) > 0.5
    entry = jnp.arange(valid.shape[0])
    ahead = valid[None, :] & (entry[None, :] < entry[:, None]) & (in_part[None, :] == in_part[:, None])
    rank = jnp.sum(ahead, axis=1)
    fulls = jnp.sum(valid & jnp.logical_not(in_part), dtype=jnp.int32)
    parts = jnp.sum(valid & in_part, dtype=jnp.int32)
    fulls = (fulls + FULL_WIDTH - 1) // FULL_WIDTH * FULL_WIDTH
    parts = (parts + PART_WIDTH - 1) // PART_WIDTH * PART_WIDTH
    rank = jnp.where(in_part, fulls + rank, rank)
    chosen = valid[None, :] & (rank[None, :] == jnp.arange(ITEMS)[:, None])
    value = first * ATOMS + second - DUMMY
    items = DUMMY + jnp.sum(jnp.where(chosen, value[None, :], 0), axis=1)
    return jnp.stack([fulls, parts]), items.astype(jnp.int32)


def pair_items(here, above, is_part):
    listed = above[6 * TILES :, 0:TILES].astype(jnp.int32)
    has_above = lax.axis_index("slab") < lax.axis_size("slab") - 1
    tiles = lax.broadcasted_iota(jnp.int32, here.shape, 1)
    return packed(
        jnp.concatenate([tiles, listed]),
        jnp.concatenate([here, HALF + tiles]),
        jnp.concatenate([here >= 0, (listed >= 0) & has_above]),
        is_part,
    )


def body(positions, charges, radii, scales, neighbours, pad_mask):
    sent, edges, here = run_pack(
        jnp.swapaxes(positions[0, 0], 0, 1),
        charges[0, 0],
        radii[0, 0],
        scales[0, 0],
        neighbours[0, 0].T,
        pad_mask[0, 0].T,
    )
    above = above_to_here(sent)
    next_edges = next_to_here(edges)
    above_edges = across_to_here(edges)
    reach, is_part = chunk_reach(sent, next_edges, above, above_edges)
    total, items = pair_items(here, above, is_part)

    *parts, data, plain, d_self, d_pair = run_born(total, items, reach, sent, next_edges, above, above_edges)
    shares = swap_sums(*parts)
    radii_born, slope, *parts, force = run_energy(total, items, reach, data, plain, shares)
    shares = swap_sums(*parts)
    gradient, own, over, to_next = run_force(total, items, reach, data, slope, shares, force, d_self, d_pair)
    from_last = here_to_next(to_next)
    edge = ((0, 0), (0, TILES - EDGE), (0, 0))
    over = over[:, 0:TILES] + jnp.pad(from_last[:, EDGE : 2 * EDGE], edge)
    own = own[:, 0:TILES] + jnp.pad(from_last[:, 0:EDGE], edge)
    forces = own + here_to_above(over)
    return (radii_born[None, None], gradient[None, None], jnp.swapaxes(forces, 0, 1)[None, None])


def solution(mesh):
    return jax.shard_map(
        body,
        mesh=mesh,
        in_specs=(
            P("slab", "tile", None, None, None),
            P("slab", "tile", None, None),
            P("slab", "tile", None, None),
            P("slab", "tile", None, None),
            P("slab", "tile", None, None),
            P("slab", "tile", None, None),
        ),
        out_specs=(
            P("slab", "tile", None, None),
            P("slab", "tile", None, None),
            P("slab", "tile", None, None, None),
        ),
        check_vma=False,
    )
```

```python
import functools
import math

import jax
import jax.numpy as jnp
import numpy as np
from jax import lax
from jax.experimental import pallas as pl
from jax.experimental.pallas import tpu as pltpu
from jax.sharding import PartitionSpec as P

radius_offset = 0.09
obc_alpha = 1.0
obc_beta = 0.8
obc_gamma = 4.85
cutoff_len = 14.0
cutoff_sq = cutoff_len * cutoff_len

TILES = 32
EDGE = 2
LIVE = TILES + EDGE
HALF = 40
REGION = 2 * HALF
OWN_ROWS = LIVE + 1
SENT_ROWS = 6 * TILES + 8
LISTED = 7
ATOMS = 128
CHUNK = 16
CHUNKS = ATOMS // CHUNK
FULL_WIDTH = 2
PART_WIDTH = 4
FULL_RING = 32
PART_RING = 32
PAIRS = 2 * TILES * LISTED + 4
ITEMS = 512
DUMMY = LIVE * ATOMS + LIVE
ROW = (1, ATOMS)
LANES = (8, ATOMS)
ROWS = (CHUNK, ATOMS)
BLOCK = (ATOMS, ATOMS)
PART = ATOMS // 2
VMEM_LIMIT = 56 * 1024 * 1024
SCALE = math.sqrt(8.0) / cutoff_len
CUT = 8.0
EXP_SCALE = math.sqrt(0.25 / math.log(2.0)) / SCALE

ROW_X, ROW_Y, ROW_Z, ROW_Q, ROW_IN, ROW_SCALED = range(6)
AT_Q, AT_RADIUS, AT_SCALED = 3, 4, 5

F32 = jnp.float32


def fold2(block):
    return block[0:8] + block[8:16]


def fold_own(own):
    flipped = own.T
    total = flipped[0:8]
    for chunk in range(1, ATOMS // 8):
        total = total + flipped[8 * chunk : 8 * chunk + 8]
    return total


def build_beside(build, work, table, fresh_a, fresh_b):
    def keep(tile, fresh, k):
        table[tile] = fresh[k]

    def step(index, carry):
        first = index * 4
        for k in range(2):
            build(first + 2 + k, fresh_b, k)
            work(first + k, fresh_a, k)
        for k in range(2):
            keep(first + k, fresh_a, k)
        for k in range(2):
            build(first + 4 + k, fresh_a, k)
            work(first + 2 + k, fresh_b, k)
        for k in range(2):
            keep(first + 2 + k, fresh_b, k)
        return carry

    for k in range(2):
        build(k, fresh_a, k)
    lax.fori_loop(0, TILES // 4, step, 0)
    for k in range(EDGE):
        keep(TILES + k, fresh_a, k)


def by_fours(step):
    def fours(index, carry):
        start = jnp.minimum(index * 4, LIVE - 4)
        for k in range(4):
            step(start + k)
        return carry

    lax.fori_loop(0, (LIVE + 3) // 4, fours, 0)


def fill_table(table, k, first, ref, tile, rows):
    for slot, row in enumerate(rows):
        table[k, first + slot] = jnp.broadcast_to(ref[tile, row : row + 1, :], BLOCK).T


def fold_rows(own, target, index):
    def fours(quad, carry):
        for k in range(4):
            tile = quad * 4 + k
            target[(tile,) + index] += fold_own(own[(tile,) + index])
        return carry

    lax.fori_loop(0, TILES // 4, fours, 0)
    for tile in range(TILES, LIVE):
        target[(tile,) + index] += fold_own(own[(tile,) + index])


def diagonal(start):
    rows = lax.broadcasted_iota(jnp.int32, ROWS, 0) + start
    return jnp.where(rows == lax.broadcasted_iota(jnp.int32, ROWS, 1), 4.0 * CUT, 0.0)


def decode(item):
    return lax.shift_right_logical(item, 7), lax.bitwise_and(item, ATOMS - 1)


def span(start):
    return pl.ds(start if isinstance(start, int) else pl.multiple_of(start, CHUNK), CHUNK)


def part_starts(code):
    return [lax.bitwise_and(lax.shift_right_logical(code, 3 * j), 7) * CHUNK for j in range(CHUNKS // 2)]


def row_of(ref, tile, row):
    return jnp.broadcast_to(ref[tile, row : row + 1, :], ROWS)


def differences(table, tile, rows, far):
    return tuple(table[tile, axis, rows, :] - far[axis] for axis in range(3))


def distance_squared(gaps):
    dx, dy, dz = gaps
    return dx * dx + dy * dy + dz * dz


def half_descreen(r, own, far):
    upper = r + far
    lower = r - far
    inner = jnp.minimum(jnp.maximum(own, lower), upper)
    ratio = upper * pl.reciprocal(inner, approx=True)
    slope = lower * pl.reciprocal(upper, approx=True)
    square = ratio * ratio
    rise = ratio - 1.0
    twice = jnp.log(square)
    value = rise * (2.0 - slope * rise) - twice
    deriv = (twice + twice) - (square - 1.0) * (slope * slope + 1.0)
    return value, deriv


def ring_copies(ring, blocks, sems, size, rows):
    def copy(index, place, inward):
        slot = lax.rem(index, size)
        here = ring.at[slot]
        there = blocks.at[place, :, pl.ds(0, rows), :]
        source, target = (there, here) if inward else (here, there)
        return pltpu.make_async_copy(source, target, sems.at[slot])

    return copy


def edge_rows(target, values, first, second):
    target[...] = jnp.zeros_like(target)
    target[0:EDGE, :] = values[first : first + EDGE]
    target[EDGE : 2 * EDGE, :] = values[second : second + EDGE]


def pack_kernel(positions, charges, radii, scales, neighbours, pad_mask, sent, edges, here):
    radius = radii[...]
    values = [positions[0], positions[1], positions[2], charges[...], radius, scales[...] * (radius - radius_offset)]
    edges[...] = jnp.zeros_like(edges)
    for index, value in enumerate(values):
        sent[index * TILES : (index + 1) * TILES, :] = value
        edges[EDGE * index : EDGE * (index + 1), :] = value[0:EDGE]
    cycle_count = lax.axis_size("tile")
    cycle_tiles = cycle_count * TILES
    listed = neighbours[...]
    slab_step = lax.div(listed, cycle_tiles) - lax.axis_index("slab")
    within = lax.rem(listed, cycle_tiles)
    cycle_step = lax.rem(lax.div(within, TILES) - lax.axis_index("tile") + cycle_count, cycle_count)
    place = cycle_step * TILES + lax.rem(within, TILES)
    slots = lax.broadcasted_iota(jnp.int32, listed.shape, 0)
    live = (pad_mask[...] == 1) & (slots > 0)
    here[...] = jnp.where(live & (slab_step >= 0), slab_step * HALF + place, -1)
    sent[6 * TILES :, :] = jnp.full(LANES, -1.0, F32)
    sent[6 * TILES :, 0:TILES] = jnp.where(live & (slab_step < 0), place, -1).astype(F32)


def born_kernel(
    total, items, reach, sent, edges, above, above_edges,
    own_part, above_part, to_next, to_last, data, plain, d_self, d_pair,
    table, fresh_a, fresh_b, own, far, rings, sems,
):
    full_ring, part_ring, self_ring = rings
    full_sems, part_sems, self_sems = sems
    far[...] = jnp.zeros_like(far)
    data[...] = jnp.zeros_like(data)
    plain[...] = jnp.ones_like(plain)
    fulls, parts = total[0], total[1]

    for index in range(6):
        origin = sent[index * TILES + TILES // 2 : index * TILES + TILES // 2 + 1, 0:1]
        for start, source, edge in ((0, sent, edges), (HALF, above, above_edges)):
            for place, values in (
                (start, source[index * TILES : (index + 1) * TILES, :]),
                (start + TILES, edge[EDGE * index : EDGE * (index + 1), :]),
            ):
                rows = slice(place, place + values.shape[0])
                if index < AT_Q:
                    data[rows, index, :] = (values - origin) * SCALE
                elif index == AT_Q:
                    data[rows, ROW_Q, :] = values
                    plain[2, rows, :] = values if place == 0 else jnp.zeros_like(values)
                elif index == AT_RADIUS:
                    data[rows, ROW_IN, :] = (values - radius_offset) * SCALE
                    plain[0, rows, :] = values
                    plain[1, rows, :] = values - radius_offset
                else:
                    data[rows, ROW_SCALED, :] = values * SCALE

    def build(tile, fresh, k):
        fill_table(fresh, k, 0, data, tile, (ROW_X, ROW_Y, ROW_Z, ROW_IN, ROW_SCALED))

    for tile in range(TILES, OWN_ROWS):
        own[tile] = jnp.zeros(BLOCK, F32)

    def shared(r2):
        inv = lax.rsqrt(r2)
        cut = jnp.maximum(1.0 - r2 * (1.0 / CUT), 0.0)
        cinv = cut * inv
        return r2 * inv, cut, cinv, cinv * cinv * inv

    def self_pair(tile, fresh, k):
        far_xyz = [row_of(data, tile, axis) for axis in range(3)]
        bs = row_of(data, tile, ROW_SCALED)
        for start in range(0, ATOMS, CHUNK):
            rows = span(start)
            r2 = distance_squared(differences(fresh, k, rows, far_xyz)) + diagonal(start)
            r, cut, cinv, g_deriv = shared(r2)
            value, deriv = half_descreen(r, fresh[k, 3, rows, :], bs)
            value = cinv * value
            own[tile, rows, :] = cut * value
            self_ring[tile, rows, :] = g_deriv * deriv - value

    def self_copy(tile):
        return pltpu.make_async_copy(self_ring.at[tile], d_self.at[tile], self_sems.at[tile])

    def self_step(tile, fresh, k):
        self_pair(tile, fresh, k)
        self_copy(tile).start()

    build_beside(build, self_step, table, fresh_a, fresh_b)

    def pair(item, ring, slot, starts):
        first, second = item
        far_xyz = [row_of(data, second, axis) for axis in range(3)]
        bp, bs = row_of(data, second, ROW_IN), row_of(data, second, ROW_SCALED)
        sums = jnp.zeros(ROWS, F32)
        for place, start in enumerate(starts):
            rows = span(start)
            kept = span(place * CHUNK)
            r2 = distance_squared(differences(table, first, rows, far_xyz))
            r, cut, cinv, g_deriv = shared(r2)
            value, deriv = half_descreen(r, table[first, 3, rows, :], bs)
            value = cinv * value
            own[first, rows, :] += cut * value
            ring[slot, 0, kept, :] = g_deriv * deriv - value
            value, deriv = half_descreen(r, bp, table[first, 4, rows, :])
            value = cinv * value
            ring[slot, 1, kept, :] = g_deriv * deriv - value
            sums = sums + cut * value
        far[second] += fold2(sums)

    def run(width, size, ring, ring_sems, base, number, rows, starts_of):
        copy = ring_copies(ring, d_pair, ring_sems, size, rows)

        def body(index, carry):
            begin = index * width
            for k in range(width):

                @pl.when(begin + k >= size)
                def _():
                    copy(begin + k, base + begin + k, False).wait()

            for k in range(width):
                item = decode(items[base + begin + k])
                pair(item, ring, lax.rem(begin + k, size), starts_of(item))
            for k in range(width):
                copy(begin + k, base + begin + k, False).start()
            return carry

        lax.fori_loop(0, lax.div(number, width), body, 0)

    def drain(size, ring, ring_sems, number, rows):
        copy = ring_copies(ring, d_pair, ring_sems, size, rows)

        def wait(slot, carry):
            copy(slot, slot, False).wait()
            return carry

        lax.fori_loop(0, jnp.minimum(number, size), wait, 0)

    def listed_starts(item):
        return part_starts(reach[item[0] * REGION + item[1]])

    run(FULL_WIDTH, FULL_RING, full_ring, full_sems, 0, fulls, ATOMS, lambda item: range(0, ATOMS, CHUNK))
    run(PART_WIDTH, PART_RING, part_ring, part_sems, fulls, parts, PART, listed_starts)
    fold_rows(own, far, ())
    sums = jnp.sum(far[...], axis=1) * (0.125 * SCALE)
    own_part[...] = sums[0:HALF]
    above_part[...] = sums[HALF:]
    edge_rows(to_next, sums, TILES, HALF + TILES)
    edge_rows(to_last, sums, 0, HALF)
    for tile in range(TILES):
        self_copy(tile).wait()
    drain(FULL_RING, full_ring, full_sems, fulls, ATOMS)
    drain(PART_RING, part_ring, part_sems, parts, PART)


def energy_kernel(
    total, items, reach, data, plain, own_part, above_part, from_below, from_above,
    radii_born, slope, own_grad, above_grad, to_next, to_last, force,
    table, fresh_a, fresh_b, own, far, born,
):
    far[...] = jnp.zeros_like(far)
    force[...] = jnp.zeros_like(force)
    fulls, parts = total[0], total[1]
    sums = jnp.concatenate([own_part[...] + from_below[...], above_part[...] + from_above[...]])
    all_radii, all_slopes = born_radius(sums, plain[0], plain[1])
    inverse = 1.0 / all_radii
    radii_born[...] = all_radii[0:TILES]
    slope[...] = all_slopes
    born[:, 0, :] = SCALE * all_radii
    born[:, 1, :] = EXP_SCALE * inverse

    def build(tile, fresh, k):
        fill_table(fresh, k, 0, data, tile, (ROW_X, ROW_Y, ROW_Z, ROW_Q))
        fill_table(fresh, k, 4, born, tile, (0, 1))

    for tile in range(TILES, OWN_ROWS):
        own[tile] = jnp.zeros((4,) + BLOCK, F32)

    def pair(first, second, starts, tables, k, is_self):
        far_xyz = [row_of(data, second, axis) for axis in range(3)]
        br, bi, bq = row_of(born, second, 0), -row_of(born, second, 1), row_of(data, second, ROW_Q)
        sums = [jnp.zeros(ROWS, F32)] * 4
        for start in starts:
            rows = span(start)
            gaps = differences(tables, k, rows, far_xyz)
            r2 = distance_squared(gaps)
            if is_self:
                r2 = r2 + diagonal(start)
            cut = jnp.maximum(1.0 - r2 * (1.0 / CUT), 0.0)
            power = r2 * (tables[k, 5, rows, :] * bi)
            decay = lax.exp2(power)
            screen = (tables[k, 4, rows, :] * br) * decay
            inv = lax.rsqrt(r2 + screen)
            cinv = cut * inv
            lead = (tables[k, 3, rows, :] * bq) * cinv
            square = cinv * inv
            grad = (lead * square) * (screen * (1.0 - math.log(2.0) * power))
            pull = lead * (square * (4.0 - decay) + 16.0 / CUT)
            terms = [grad] + [pull * gap for gap in gaps]
            for which, term in enumerate(terms):
                if is_self:
                    own[first, which, rows, :] = term
                else:
                    own[first, which, rows, :] += term
                    sums[which] = sums[which] + term
        if not is_self:
            far[second] += fold2(sums[0])
            for axis in range(3):
                force[second, axis] -= fold2(sums[1 + axis])

    def self_step(tile, fresh, k):
        pair(tile, tile, range(0, ATOMS, CHUNK), fresh, k, True)

    build_beside(build, self_step, table, fresh_a, fresh_b)

    def full_step(index, carry):
        for k in range(FULL_WIDTH):
            first, second = decode(items[index * FULL_WIDTH + k])
            pair(first, second, range(0, ATOMS, CHUNK), table, first, False)
        return carry

    def part_step(index, carry):
        for k in range(PART_WIDTH):
            first, second = decode(items[fulls + index * PART_WIDTH + k])
            starts = part_starts(reach[first * REGION + second])
            pair(first, second, starts, table, first, False)
        return carry

    lax.fori_loop(0, lax.div(fulls, FULL_WIDTH), full_step, 0)
    lax.fori_loop(0, lax.div(parts, PART_WIDTH), part_step, 0)

    def fold_step(pairs, carry):
        for k in range(2):
            tile = pairs * 2 + k
            far[tile] += fold_own(own[tile, 0])
            for axis in range(3):
                force[tile, axis] += fold_own(own[tile, 1 + axis])
        return carry

    lax.fori_loop(0, LIVE // 2, fold_step, 0)
    charge = plain[2] * inverse
    sums = jnp.sum(far[...], axis=1) * (0.5 * SCALE) * inverse + 0.5 * charge * charge
    own_grad[...] = sums[0:HALF]
    above_grad[...] = sums[HALF:]
    edge_rows(to_next, sums, TILES, HALF + TILES)
    edge_rows(to_last, sums, 0, HALF)


def force_kernel(
    total, items, reach, data, slope, own_grad, above_grad, from_below, from_above, force_in, d_self, d_pair,
    gradient, own_force, above_force, to_next, to_across,
    table, own, far, chain, rings, sems,
):
    full_ring, part_ring, self_ring = rings
    full_sems, part_sems, self_sems = sems
    fulls, parts = total[0], total[1]
    full_copy = ring_copies(full_ring, d_pair, full_sems, FULL_RING, ATOMS)
    part_copy = ring_copies(part_ring, d_pair, part_sems, PART_RING, PART)

    def self_copy(tile):
        return pltpu.make_async_copy(d_self.at[tile], self_ring.at[tile], self_sems.at[tile])

    def start(copy, base):
        def step(index, carry):
            copy(index, base + index, True).start()
            return carry

        return step

    for tile in range(TILES):
        self_copy(tile).start()
    lax.fori_loop(0, jnp.minimum(fulls, FULL_RING), start(full_copy, 0), 0)
    lax.fori_loop(0, jnp.minimum(parts, PART_RING), start(part_copy, fulls), 0)

    far[...] = force_in[...] * 4.0
    grads = jnp.concatenate([own_grad[...] + from_below[...], above_grad[...] + from_above[...]])
    gradient[...] = grads[0:TILES]
    chain[:, 0, :] = grads * slope[...]

    def build(tile):
        fill_table(table, tile, 0, data, tile, (ROW_X, ROW_Y, ROW_Z))
        fill_table(table, tile, 3, chain, tile, (0,))

    by_fours(build)
    for tile in range(TILES, OWN_ROWS):
        own[tile] = jnp.zeros((3,) + BLOCK, F32)

    def pair(first, second, starts, tables, k, pull_of, is_self):
        far_xyz = [row_of(data, second, axis) for axis in range(3)]
        sums = [jnp.zeros(ROWS, F32)] * 3
        for place, start in enumerate(starts):
            rows = span(start)
            pull = pull_of(rows, span(place * CHUNK))
            terms = [pull * gap for gap in differences(tables, k, rows, far_xyz)]
            for which, term in enumerate(terms):
                if is_self:
                    own[first, which, rows, :] = term
                else:
                    own[first, which, rows, :] += term
                sums[which] = sums[which] + term
        for axis in range(3):
            far[second, axis] -= fold2(sums[axis])

    def self_step(quad, carry):
        begin = quad * 4
        for k in range(4):
            self_copy(begin + k).wait()
        for k in range(4):
            tile = begin + k
            pair(
                tile,
                tile,
                range(0, ATOMS, CHUNK),
                table,
                tile,
                lambda rows, kept: table[tile, 3, rows, :] * self_ring[tile, kept, :],
                True,
            )
        return carry

    lax.fori_loop(0, TILES // 4, self_step, 0)

    def run(width, size, ring, copy, base, number, starts_of):
        def body(index, carry):
            begin = index * width
            for k in range(width):
                copy(begin + k, base + begin + k, True).wait()
            for k in range(width):
                first, second = decode(items[base + begin + k])
                slot = lax.rem(begin + k, size)
                factor = row_of(chain, second, 0)
                pair(
                    first,
                    second,
                    starts_of(first, second),
                    table,
                    first,
                    lambda rows, kept: table[first, 3, rows, :] * ring[slot, 0, kept, :]
                    + factor * ring[slot, 1, kept, :],
                    False,
                )
            for k in range(width):

                @pl.when(begin + k + size < number)
                def _():
                    copy(begin + k + size, base + begin + k + size, True).start()

            return carry

        lax.fori_loop(0, lax.div(number, width), body, 0)

    run(FULL_WIDTH, FULL_RING, full_ring, full_copy, 0, fulls, lambda *_: range(0, ATOMS, CHUNK))
    run(
        PART_WIDTH,
        PART_RING,
        part_ring,
        part_copy,
        fulls,
        parts,
        lambda first, second: part_starts(reach[first * REGION + second]),
    )

    def fold_step(pairs, carry):
        for k in range(2):
            tile = pairs * 2 + k
            for axis in range(3):
                far[tile, axis] += fold_own(own[tile, axis])
        return carry

    lax.fori_loop(0, LIVE // 2, fold_step, 0)
    for axis in range(3):
        sums = jnp.sum(far[:, axis], axis=1) * (-SCALE * SCALE / 16.0)
        own_force[axis] = sums[0:TILES]
        above_force[axis] = sums[HALF : HALF + TILES]
        to_next[axis] = sums[TILES : TILES + 8]
        to_across[axis] = sums[HALF + TILES : HALF + TILES + 8]


SMEM = pl.BlockSpec(memory_space=pltpu.SMEM)
VMEM = pl.BlockSpec(memory_space=pltpu.VMEM)
ANY = pl.BlockSpec(memory_space=pl.ANY)
PARAMS = pltpu.CompilerParams(vmem_limit_bytes=VMEM_LIMIT)
RING_BLOCKS = (
    pltpu.VMEM((FULL_RING, 2) + BLOCK, F32),
    pltpu.VMEM((PART_RING, 2, PART, ATOMS), F32),
    pltpu.VMEM((TILES,) + BLOCK, F32),
)
RING_SEMS = (
    pltpu.SemaphoreType.DMA((FULL_RING,)),
    pltpu.SemaphoreType.DMA((PART_RING,)),
    pltpu.SemaphoreType.DMA((TILES,)),
)


def f32(*shape):
    return jax.ShapeDtypeStruct(shape, F32)


def run_pack(positions, charges, radii, scales, neighbours, pad_mask):
    return pl.pallas_call(
        pack_kernel,
        name="pack_atoms",
        out_shape=(
            f32(SENT_ROWS, ATOMS),
            f32(16, ATOMS),
            jax.ShapeDtypeStruct(neighbours.shape, jnp.int32),
        ),
        in_specs=[VMEM] * 6,
        out_specs=(VMEM,) * 3,
        compiler_params=PARAMS,
    )(positions, charges, radii, scales, neighbours, pad_mask)


def run_born(total, items, reach, sent, edges, above, above_edges):
    return pl.pallas_call(
        born_kernel,
        name="born_sums",
        out_shape=(
            f32(HALF, ATOMS),
            f32(HALF, ATOMS),
            f32(*LANES),
            f32(*LANES),
            f32(REGION, *LANES),
            f32(3, REGION, ATOMS),
            f32(TILES, *BLOCK),
            f32(PAIRS, 2, *BLOCK),
        ),
        in_specs=[SMEM] * 3 + [VMEM] * 4,
        out_specs=(VMEM,) * 6 + (ANY,) * 2,
        scratch_shapes=[
            pltpu.VMEM((OWN_ROWS, 5) + BLOCK, F32),
            pltpu.VMEM((2, 5) + BLOCK, F32),
            pltpu.VMEM((2, 5) + BLOCK, F32),
            pltpu.VMEM((OWN_ROWS,) + BLOCK, F32),
            pltpu.VMEM((REGION,) + LANES, F32),
            RING_BLOCKS,
            RING_SEMS,
        ],
        compiler_params=PARAMS,
    )(total, items, reach, sent, edges, above, above_edges)


def run_energy(total, items, reach, data, plain, shares):
    return pl.pallas_call(
        energy_kernel,
        name="radius_gradient",
        out_shape=(
            f32(TILES, ATOMS),
            f32(REGION, ATOMS),
            f32(HALF, ATOMS),
            f32(HALF, ATOMS),
            f32(*LANES),
            f32(*LANES),
            f32(REGION, 3, *LANES),
        ),
        in_specs=[SMEM] * 3 + [VMEM] * 6,
        out_specs=(VMEM,) * 7,
        scratch_shapes=[
            pltpu.VMEM((OWN_ROWS, 6) + BLOCK, F32),
            pltpu.VMEM((2, 6) + BLOCK, F32),
            pltpu.VMEM((2, 6) + BLOCK, F32),
            pltpu.VMEM((OWN_ROWS, 4) + BLOCK, F32),
            pltpu.VMEM((REGION,) + LANES, F32),
            pltpu.VMEM((REGION,) + LANES, F32),
        ],
        compiler_params=PARAMS,
    )(total, items, reach, data, plain, *shares)


def run_force(total, items, reach, data, slope, shares, force_in, d_self, d_pair):
    return pl.pallas_call(
        force_kernel,
        name="forces",
        out_shape=(
            f32(TILES, ATOMS),
            f32(3, TILES, ATOMS),
            f32(3, TILES, ATOMS),
            f32(3, *LANES),
            f32(3, *LANES),
        ),
        in_specs=[SMEM] * 3 + [VMEM] * 7 + [ANY] * 2,
        out_specs=(VMEM,) * 5,
        scratch_shapes=[
            pltpu.VMEM((OWN_ROWS, 4) + BLOCK, F32),
            pltpu.VMEM((OWN_ROWS, 3) + BLOCK, F32),
            pltpu.VMEM((REGION, 3) + LANES, F32),
            pltpu.VMEM((REGION,) + LANES, F32),
            RING_BLOCKS,
            RING_SEMS,
        ],
        compiler_params=PARAMS,
    )(total, items, reach, data, slope, *shares, force_in, d_self, d_pair)


def born_radius(descreen_sum, radius, radius_in):
    scaled = radius_in * descreen_sum
    polynomial = scaled * (obc_alpha + scaled * (-obc_beta + obc_gamma * scaled))
    tangent = jnp.tanh(polynomial)
    radii_born = 1.0 / (1.0 / radius_in - tangent / radius)
    radius_slope = (
        radii_born
        * radii_born
        * (1.0 - tangent * tangent)
        / radius
        * (obc_alpha - 2.0 * obc_beta * scaled + 3.0 * obc_gamma * scaled * scaled)
        * radius_in
    )
    return (radii_born, radius_slope)


def above_to_here(block):
    ends = lax.axis_size("slab") - 1
    return lax.ppermute(block, "slab", [(i + 1, i) for i in range(ends)])


def here_to_above(block):
    ends = lax.axis_size("slab") - 1
    return lax.ppermute(block, "slab", [(i, i + 1) for i in range(ends)])


def next_to_here(block):
    count = lax.axis_size("tile")
    return lax.ppermute(block, "tile", [((i + 1) % count, i) for i in range(count)])


def here_to_next(block):
    count = lax.axis_size("tile")
    return lax.ppermute(block, "tile", [(i, (i + 1) % count) for i in range(count)])


def across_to_here(block):
    slabs, count = lax.axis_size("slab"), lax.axis_size("tile")
    pairs = [
        ((slab + 1) * count + (tile + 1) % count, slab * count + tile)
        for slab in range(slabs - 1)
        for tile in range(count)
    ]
    return lax.ppermute(block, ("slab", "tile"), pairs)


def placed(block, first, last):
    return jnp.pad(block[first : first + EDGE], ((0, HALF - EDGE), (0, 0))) + jnp.pad(
        last[first : first + EDGE], ((TILES, HALF - LIVE), (0, 0))
    )


def swap_sums(own, above, to_next, to_last):
    from_last = here_to_next(to_next)
    from_next = next_to_here(to_last)
    own = own + placed(from_last, 0, from_next)
    above = above + placed(from_last, EDGE, from_next)
    own, above = lax.optimization_barrier((own, above))
    return own, above, here_to_above(above), above_to_here(own)


def here_to_across(block):
    slabs, count = lax.axis_size("slab"), lax.axis_size("tile")
    pairs = [
        (slab * count + tile, (slab + 1) * count + (tile + 1) % count)
        for slab in range(slabs - 1)
        for tile in range(count)
    ]
    return lax.ppermute(block, ("slab", "tile"), pairs)


def whole_slab(component, block, edges):
    first, edge = component * TILES, component * EDGE
    return [block[first : first + TILES], edges[edge : edge + EDGE], jnp.zeros((HALF - LIVE, ATOMS), F32)]


def chunk_reach(sent, edges, above, above_edges):
    x, y, z = (
        jnp.concatenate(whole_slab(axis, sent, edges) + whole_slab(axis, above, above_edges)) for axis in range(3)
    )
    across, along = sent[TILES // 2, 0], sent[TILES + TILES // 2, 0]
    inverse = lax.rsqrt(across * across + along * along)
    across, along = across * inverse, along * inverse
    turned = jnp.stack([x * across + y * along, y * across - x * along, z])
    pieces = turned.reshape(3, REGION, CHUNKS, CHUNK)
    low, high = jnp.min(pieces, axis=3), jnp.max(pieces, axis=3)
    tile_low, tile_high = jnp.min(low, axis=2), jnp.max(high, axis=2)
    near = []
    for chunk in range(CHUNKS):
        own_low, own_high = low[:, :OWN_ROWS, chunk, None], high[:, :OWN_ROWS, chunk, None]
        gap = jnp.maximum(jnp.maximum(tile_low[:, None, :] - own_high, own_low - tile_high[:, None, :]), 0.0)
        far = jnp.sum(gap * gap, axis=0) >= cutoff_sq * 1.001
        near.append(jnp.logical_not(far).astype(jnp.int32))
    number = sum(near)
    code = number << (3 * CHUNKS)
    before = jnp.zeros_like(number)
    for chunk in range(CHUNKS):
        rank = jnp.where(near[chunk] == 1, before, number + chunk - before)
        code = code + (chunk << (3 * rank))
        before = before + near[chunk]
    return code.reshape(-1), number <= CHUNKS // 2


def packed(first, second, valid, is_part):
    first, second, valid = first.reshape(-1), second.reshape(-1), valid.reshape(-1)
    mine = (first[:, None] == jnp.arange(OWN_ROWS)[None, :]).astype(jnp.bfloat16)
    rows = jnp.dot(mine, is_part.astype(jnp.bfloat16), preferred_element_type=F32)
    in_part = jnp.sum(jnp.where(second[:, None] == jnp.arange(REGION)[None, :], rows, 0.0), axis=1) > 0.5
    entry = jnp.arange(valid.shape[0])
    ahead = valid[None, :] & (entry[None, :] < entry[:, None]) & (in_part[None, :] == in_part[:, None])
    rank = jnp.sum(ahead, axis=1)
    fulls = jnp.sum(valid & jnp.logical_not(in_part), dtype=jnp.int32)
    parts = jnp.sum(valid & in_part, dtype=jnp.int32)
    fulls = (fulls + FULL_WIDTH - 1) // FULL_WIDTH * FULL_WIDTH
    parts = (parts + PART_WIDTH - 1) // PART_WIDTH * PART_WIDTH
    rank = jnp.where(in_part, fulls + rank, rank)
    chosen = valid[None, :] & (rank[None, :] == jnp.arange(ITEMS)[:, None])
    value = first * ATOMS + second - DUMMY
    items = DUMMY + jnp.sum(jnp.where(chosen, value[None, :], 0), axis=1)
    return jnp.stack([fulls, parts]), items.astype(jnp.int32)


def pair_items(here, above, is_part):
    listed = above[6 * TILES :, 0:TILES].astype(jnp.int32)
    has_above = lax.axis_index("slab") < lax.axis_size("slab") - 1
    tiles = lax.broadcasted_iota(jnp.int32, here.shape, 1)
    return packed(
        jnp.concatenate([tiles, listed]),
        jnp.concatenate([here, HALF + tiles]),
        jnp.concatenate([here >= 0, (listed >= 0) & has_above]),
        is_part,
    )


def body(positions, charges, radii, scales, neighbours, pad_mask):
    sent, edges, here = run_pack(
        jnp.swapaxes(positions[0, 0], 0, 1),
        charges[0, 0],
        radii[0, 0],
        scales[0, 0],
        neighbours[0, 0].T,
        pad_mask[0, 0].T,
    )
    above = above_to_here(sent)
    next_edges = next_to_here(edges)
    above_edges = across_to_here(edges)
    reach, is_part = chunk_reach(sent, next_edges, above, above_edges)
    total, items = pair_items(here, above, is_part)

    *parts, data, plain, d_self, d_pair = run_born(total, items, reach, sent, next_edges, above, above_edges)
    shares = swap_sums(*parts)
    radii_born, slope, *parts, force = run_energy(total, items, reach, data, plain, shares)
    shares = swap_sums(*parts)
    gradient, own, over, to_next, to_across = run_force(
        total, items, reach, data, slope, shares, force, d_self, d_pair
    )
    from_below = here_to_above(over)
    edge = here_to_next(to_next) + here_to_across(to_across)
    forces = own + from_below + jnp.pad(edge[:, 0:EDGE], ((0, 0), (0, TILES - EDGE), (0, 0)))
    return (radii_born[None, None], gradient[None, None], jnp.swapaxes(forces, 0, 1)[None, None])


def solution(mesh):
    return jax.shard_map(
        body,
        mesh=mesh,
        in_specs=(
            P("slab", "tile", None, None, None),
            P("slab", "tile", None, None),
            P("slab", "tile", None, None),
            P("slab", "tile", None, None),
            P("slab", "tile", None, None),
            P("slab", "tile", None, None),
        ),
        out_specs=(
            P("slab", "tile", None, None),
            P("slab", "tile", None, None),
            P("slab", "tile", None, None, None),
        ),
        check_vma=False,
    )
```

```python
import functools
import math

import jax
import jax.numpy as jnp
import numpy as np
from jax import lax
from jax.experimental import pallas as pl
from jax.experimental.pallas import tpu as pltpu
from jax.sharding import PartitionSpec as P

radius_offset = 0.09
obc_alpha = 1.0
obc_beta = 0.8
obc_gamma = 4.85
cutoff_len = 14.0
cutoff_sq = cutoff_len * cutoff_len

TILES = 32
EDGE = 2
LIVE = TILES + EDGE
HALF = 40
REGION = 2 * HALF
OWN_ROWS = LIVE + 1
SENT_ROWS = 6 * TILES + 8
LISTED = 7
ATOMS = 128
CHUNK = 16
CHUNKS = ATOMS // CHUNK
FULL_WIDTH = 2
PART_WIDTH = 4
FULL_RING = 32
PART_RING = 32
PAIRS = 2 * TILES * LISTED + 4
ITEMS = 512
DUMMY = LIVE * ATOMS + LIVE
ROW = (1, ATOMS)
LANES = (8, ATOMS)
ROWS = (CHUNK, ATOMS)
BLOCK = (ATOMS, ATOMS)
PART = ATOMS // 2
VMEM_LIMIT = 56 * 1024 * 1024
SCALE = math.sqrt(8.0) / cutoff_len
CUT = 8.0
EXP_SCALE = math.sqrt(0.25 / math.log(2.0)) / SCALE

ROW_X, ROW_Y, ROW_Z, ROW_Q, ROW_IN, ROW_SCALED = range(6)
AT_Q, AT_RADIUS, AT_SCALED = 3, 4, 5

F32 = jnp.float32


def fold2(block):
    return block[0:8] + block[8:16]


def fold_own(own):
    flipped = own.T
    total = flipped[0:8]
    for chunk in range(1, ATOMS // 8):
        total = total + flipped[8 * chunk : 8 * chunk + 8]
    return total


def build_beside(build, work, table, fresh_a, fresh_b):
    def keep(tile, fresh, k):
        table[tile] = fresh[k]

    def step(index, carry):
        first = index * 4
        for k in range(2):
            build(first + 2 + k, fresh_b, k)
            work(first + k, fresh_a, k)
        for k in range(2):
            keep(first + k, fresh_a, k)
        for k in range(2):
            build(first + 4 + k, fresh_a, k)
            work(first + 2 + k, fresh_b, k)
        for k in range(2):
            keep(first + 2 + k, fresh_b, k)
        return carry

    for k in range(2):
        build(k, fresh_a, k)
    lax.fori_loop(0, TILES // 4, step, 0)
    for k in range(EDGE):
        keep(TILES + k, fresh_a, k)


def by_fours(step):
    def fours(index, carry):
        start = jnp.minimum(index * 4, LIVE - 4)
        for k in range(4):
            step(start + k)
        return carry

    lax.fori_loop(0, (LIVE + 3) // 4, fours, 0)


def fill_table(table, k, first, ref, tile, rows):
    for slot, row in enumerate(rows):
        table[k, first + slot] = jnp.broadcast_to(ref[tile, row : row + 1, :], BLOCK).T


def fold_rows(fold, width):
    def step(index, carry):
        for k in range(width):
            fold(index * width + k)
        return carry

    lax.fori_loop(0, TILES // width, step, 0)
    for tile in range(TILES, LIVE):
        fold(tile)


def diagonal(start):
    rows = lax.broadcasted_iota(jnp.int32, ROWS, 0) + start
    return jnp.where(rows == lax.broadcasted_iota(jnp.int32, ROWS, 1), 4.0 * CUT, 0.0)


def decode(item):
    return lax.shift_right_logical(item, 7), lax.bitwise_and(item, ATOMS - 1)


def span(start):
    return pl.ds(start if isinstance(start, int) else pl.multiple_of(start, CHUNK), CHUNK)


def part_starts(code):
    return [lax.bitwise_and(lax.shift_right_logical(code, 3 * j), 7) * CHUNK for j in range(CHUNKS // 2)]


def row_of(ref, tile, row):
    return jnp.broadcast_to(ref[tile, row : row + 1, :], ROWS)


def differences(table, tile, rows, far):
    return tuple(table[tile, axis, rows, :] - far[axis] for axis in range(3))


def distance_squared(gaps):
    dx, dy, dz = gaps
    return dx * dx + dy * dy + dz * dz


def half_descreen(r, own, far):
    upper = r + far
    lower = r - far
    inner = jnp.minimum(jnp.maximum(own, lower), upper)
    ratio = upper * pl.reciprocal(inner, approx=True)
    slope = lower * pl.reciprocal(upper, approx=True)
    square = ratio * ratio
    rise = ratio - 1.0
    twice = jnp.log(square)
    value = rise * (2.0 - slope * rise) - twice
    deriv = (twice + twice) - (square - 1.0) * (slope * slope + 1.0)
    return value, deriv


def ring_copies(ring, blocks, sems, size, rows):
    def copy(index, place, inward):
        slot = lax.rem(index, size)
        here = ring.at[slot]
        there = blocks.at[place, :, pl.ds(0, rows), :]
        source, target = (there, here) if inward else (here, there)
        return pltpu.make_async_copy(source, target, sems.at[slot])

    return copy


def edge_rows(values, first):
    rest = jnp.zeros((8 - 2 * EDGE, ATOMS), F32)
    return jnp.concatenate([values[first : first + EDGE], values[HALF + first : HALF + first + EDGE], rest])


def edge_rounds(values, one, two):
    to_next, to_last = edge_rows(values, TILES), edge_rows(values, 0)
    is_even = lax.rem(lax.axis_index("tile"), 2) == 0
    one[...] = jnp.where(is_even, to_next, to_last)
    two[...] = jnp.where(is_even, to_last, to_next)


def pack_kernel(positions, charges, radii, scales, neighbours, pad_mask, sent, edges, here):
    radius = radii[...]
    values = [positions[0], positions[1], positions[2], charges[...], radius, scales[...] * (radius - radius_offset)]
    edges[...] = jnp.zeros_like(edges)
    for index, value in enumerate(values):
        sent[index * TILES : (index + 1) * TILES, :] = value
        edges[EDGE * index : EDGE * (index + 1), :] = value[0:EDGE]
    cycle_count = lax.axis_size("tile")
    cycle_tiles = cycle_count * TILES
    listed = neighbours[...]
    slab_step = lax.div(listed, cycle_tiles) - lax.axis_index("slab")
    within = lax.rem(listed, cycle_tiles)
    cycle_step = lax.rem(lax.div(within, TILES) - lax.axis_index("tile") + cycle_count, cycle_count)
    place = cycle_step * TILES + lax.rem(within, TILES)
    slots = lax.broadcasted_iota(jnp.int32, listed.shape, 0)
    live = (pad_mask[...] == 1) & (slots > 0)
    here[...] = jnp.where(live & (slab_step >= 0), slab_step * HALF + place, -1)
    sent[6 * TILES :, :] = jnp.full(LANES, -1.0, F32)
    sent[6 * TILES :, 0:TILES] = jnp.where(live & (slab_step < 0), place, -1).astype(F32)


def born_kernel(
    total, items, reach, sent, edges, above, above_edges,
    own_part, above_part, round_one, round_two, data, plain, d_self, d_pair,
    table, fresh_a, fresh_b, own, far, rings, sems,
):
    full_ring, part_ring, self_ring = rings
    full_sems, part_sems, self_sems = sems
    far[...] = jnp.zeros_like(far)
    data[...] = jnp.zeros_like(data)
    plain[...] = jnp.ones_like(plain)
    fulls, parts = total[0], total[1]

    for index in range(6):
        origin = sent[index * TILES + TILES // 2 : index * TILES + TILES // 2 + 1, 0:1]
        for start, source, edge in ((0, sent, edges), (HALF, above, above_edges)):
            for place, values in (
                (start, source[index * TILES : (index + 1) * TILES, :]),
                (start + TILES, edge[EDGE * index : EDGE * (index + 1), :]),
            ):
                rows = slice(place, place + values.shape[0])
                if index < AT_Q:
                    data[rows, index, :] = (values - origin) * SCALE
                elif index == AT_Q:
                    data[rows, ROW_Q, :] = values
                    plain[2, rows, :] = values if place == 0 else jnp.zeros_like(values)
                elif index == AT_RADIUS:
                    data[rows, ROW_IN, :] = (values - radius_offset) * SCALE
                    plain[0, rows, :] = values
                    plain[1, rows, :] = values - radius_offset
                else:
                    data[rows, ROW_SCALED, :] = values * SCALE

    def build(tile, fresh, k):
        fill_table(fresh, k, 0, data, tile, (ROW_X, ROW_Y, ROW_Z, ROW_IN, ROW_SCALED))

    for tile in range(TILES, OWN_ROWS):
        own[tile] = jnp.zeros(BLOCK, F32)

    def shared(r2):
        inv = lax.rsqrt(r2)
        cut = jnp.maximum(1.0 - r2 * (1.0 / CUT), 0.0)
        cinv = cut * inv
        return r2 * inv, cut, cinv, cinv * cinv * inv

    def self_pair(tile, fresh, k):
        far_xyz = [row_of(data, tile, axis) for axis in range(3)]
        bs = row_of(data, tile, ROW_SCALED)
        for start in range(0, ATOMS, CHUNK):
            rows = span(start)
            r2 = distance_squared(differences(fresh, k, rows, far_xyz)) + diagonal(start)
            r, cut, cinv, g_deriv = shared(r2)
            value, deriv = half_descreen(r, fresh[k, 3, rows, :], bs)
            value = cinv * value
            own[tile, rows, :] = cut * value
            self_ring[tile, rows, :] = g_deriv * deriv - value

    def self_copy(tile):
        return pltpu.make_async_copy(self_ring.at[tile], d_self.at[tile], self_sems.at[tile])

    def self_step(tile, fresh, k):
        self_pair(tile, fresh, k)
        self_copy(tile).start()

    build_beside(build, self_step, table, fresh_a, fresh_b)

    def pair(item, ring, slot, starts):
        first, second = item
        far_xyz = [row_of(data, second, axis) for axis in range(3)]
        bp, bs = row_of(data, second, ROW_IN), row_of(data, second, ROW_SCALED)
        sums = jnp.zeros(ROWS, F32)
        for place, start in enumerate(starts):
            rows = span(start)
            kept = span(place * CHUNK)
            r2 = distance_squared(differences(table, first, rows, far_xyz))
            r, cut, cinv, g_deriv = shared(r2)
            value, deriv = half_descreen(r, table[first, 3, rows, :], bs)
            value = cinv * value
            own[first, rows, :] += cut * value
            ring[slot, 0, kept, :] = g_deriv * deriv - value
            value, deriv = half_descreen(r, bp, table[first, 4, rows, :])
            value = cinv * value
            ring[slot, 1, kept, :] = g_deriv * deriv - value
            sums = sums + cut * value
        far[second] += fold2(sums)

    def run(width, size, ring, ring_sems, base, number, rows, starts_of):
        copy = ring_copies(ring, d_pair, ring_sems, size, rows)

        def body(index, carry):
            begin = index * width
            for k in range(width):

                @pl.when(begin + k >= size)
                def _():
                    copy(begin + k, base + begin + k, False).wait()

            for k in range(width):
                item = decode(items[base + begin + k])
                pair(item, ring, lax.rem(begin + k, size), starts_of(item))
            for k in range(width):
                copy(begin + k, base + begin + k, False).start()
            return carry

        lax.fori_loop(0, lax.div(number, width), body, 0)

    def drain(size, ring, ring_sems, number, rows):
        copy = ring_copies(ring, d_pair, ring_sems, size, rows)

        def wait(slot, carry):
            copy(slot, slot, False).wait()
            return carry

        lax.fori_loop(0, jnp.minimum(number, size), wait, 0)

    def listed_starts(item):
        return part_starts(reach[item[0] * REGION + item[1]])

    run(FULL_WIDTH, FULL_RING, full_ring, full_sems, 0, fulls, ATOMS, lambda item: range(0, ATOMS, CHUNK))
    run(PART_WIDTH, PART_RING, part_ring, part_sems, fulls, parts, PART, listed_starts)

    def fold(tile):
        far[tile] += fold_own(own[tile])

    fold_rows(fold, 8)
    sums = jnp.sum(far[...], axis=1) * (0.125 * SCALE)
    own_part[...] = sums[0:HALF]
    above_part[...] = sums[HALF:]
    edge_rounds(sums, round_one, round_two)

    def wait_self(tile, carry):
        self_copy(tile).wait()
        return carry

    lax.fori_loop(0, TILES, wait_self, 0)
    drain(FULL_RING, full_ring, full_sems, fulls, ATOMS)
    drain(PART_RING, part_ring, part_sems, parts, PART)


def energy_kernel(
    total, items, reach, data, plain, own_part, above_part, from_below, from_above,
    radii_born, slope, own_grad, above_grad, round_one, round_two, force,
    table, fresh_a, fresh_b, own, far, born,
):
    far[...] = jnp.zeros_like(far)
    force[...] = jnp.zeros_like(force)
    fulls, parts = total[0], total[1]
    sums = jnp.concatenate([own_part[...] + from_below[...], above_part[...] + from_above[...]])
    all_radii, all_slopes = born_radius(sums, plain[0], plain[1])
    inverse = 1.0 / all_radii
    radii_born[...] = all_radii[0:TILES]
    slope[...] = all_slopes
    born[:, 0, :] = SCALE * all_radii
    born[:, 1, :] = EXP_SCALE * inverse

    def build(tile, fresh, k):
        fill_table(fresh, k, 0, data, tile, (ROW_X, ROW_Y, ROW_Z, ROW_Q))
        fill_table(fresh, k, 4, born, tile, (0, 1))

    for tile in range(TILES, OWN_ROWS):
        own[tile] = jnp.zeros((4,) + BLOCK, F32)

    def pair(first, second, starts, tables, k, is_self):
        far_xyz = [row_of(data, second, axis) for axis in range(3)]
        br, bi, bq = row_of(born, second, 0), -row_of(born, second, 1), row_of(data, second, ROW_Q)
        sums = [jnp.zeros(ROWS, F32)] * 4
        for start in starts:
            rows = span(start)
            gaps = differences(tables, k, rows, far_xyz)
            r2 = distance_squared(gaps)
            if is_self:
                r2 = r2 + diagonal(start)
            cut = jnp.maximum(1.0 - r2 * (1.0 / CUT), 0.0)
            power = r2 * (tables[k, 5, rows, :] * bi)
            decay = lax.exp2(power)
            screen = (tables[k, 4, rows, :] * br) * decay
            inv = lax.rsqrt(r2 + screen)
            cinv = cut * inv
            lead = (tables[k, 3, rows, :] * bq) * cinv
            square = cinv * inv
            grad = (lead * square) * (screen * (1.0 - math.log(2.0) * power))
            pull = lead * (square * (4.0 - decay) + 16.0 / CUT)
            terms = [grad] + [pull * gap for gap in gaps]
            for which, term in enumerate(terms):
                if is_self:
                    own[first, which, rows, :] = term
                else:
                    own[first, which, rows, :] += term
                    sums[which] = sums[which] + term
        if not is_self:
            far[second] += fold2(sums[0])
            for axis in range(3):
                force[second, axis] -= fold2(sums[1 + axis])

    def self_step(tile, fresh, k):
        pair(tile, tile, range(0, ATOMS, CHUNK), fresh, k, True)

    build_beside(build, self_step, table, fresh_a, fresh_b)

    def full_step(index, carry):
        for k in range(FULL_WIDTH):
            first, second = decode(items[index * FULL_WIDTH + k])
            pair(first, second, range(0, ATOMS, CHUNK), table, first, False)
        return carry

    def part_step(index, carry):
        for k in range(PART_WIDTH):
            first, second = decode(items[fulls + index * PART_WIDTH + k])
            starts = part_starts(reach[first * REGION + second])
            pair(first, second, starts, table, first, False)
        return carry

    lax.fori_loop(0, lax.div(fulls, FULL_WIDTH), full_step, 0)
    lax.fori_loop(0, lax.div(parts, PART_WIDTH), part_step, 0)

    def fold(tile):
        far[tile] += fold_own(own[tile, 0])
        for axis in range(3):
            force[tile, axis] += fold_own(own[tile, 1 + axis])

    fold_rows(fold, 4)
    charge = plain[2] * inverse
    sums = jnp.sum(far[...], axis=1) * (0.5 * SCALE) * inverse + 0.5 * charge * charge
    own_grad[...] = sums[0:HALF]
    above_grad[...] = sums[HALF:]
    edge_rounds(sums, round_one, round_two)


def force_kernel(
    total, items, reach, data, slope, own_grad, above_grad, from_below, from_above, force_in, d_self, d_pair,
    gradient, own_force, above_force, to_next, to_across,
    table, own, far, chain, rings, sems,
):
    full_ring, part_ring, self_ring = rings
    full_sems, part_sems, self_sems = sems
    fulls, parts = total[0], total[1]
    full_copy = ring_copies(full_ring, d_pair, full_sems, FULL_RING, ATOMS)
    part_copy = ring_copies(part_ring, d_pair, part_sems, PART_RING, PART)

    self_copy = pltpu.make_async_copy(d_self, self_ring, self_sems.at[0])

    def start(copy, base):
        def step(index, carry):
            copy(index, base + index, True).start()
            return carry

        return step

    self_copy.start()
    lax.fori_loop(0, jnp.minimum(fulls, FULL_RING), start(full_copy, 0), 0)
    lax.fori_loop(0, jnp.minimum(parts, PART_RING), start(part_copy, fulls), 0)

    far[...] = force_in[...] * 4.0
    grads = jnp.concatenate([own_grad[...] + from_below[...], above_grad[...] + from_above[...]])
    gradient[...] = grads[0:TILES]
    chain[:, 0, :] = grads * slope[...]

    def build(tile):
        fill_table(table, tile, 0, data, tile, (ROW_X, ROW_Y, ROW_Z))
        fill_table(table, tile, 3, chain, tile, (0,))

    by_fours(build)
    for tile in range(TILES, OWN_ROWS):
        own[tile] = jnp.zeros((3,) + BLOCK, F32)

    def pair(first, second, starts, tables, k, pull_of, is_self):
        far_xyz = [row_of(data, second, axis) for axis in range(3)]
        sums = [jnp.zeros(ROWS, F32)] * 3
        for place, start in enumerate(starts):
            rows = span(start)
            pull = pull_of(rows, span(place * CHUNK))
            terms = [pull * gap for gap in differences(tables, k, rows, far_xyz)]
            for which, term in enumerate(terms):
                if is_self:
                    own[first, which, rows, :] = term
                else:
                    own[first, which, rows, :] += term
                sums[which] = sums[which] + term
        for axis in range(3):
            far[second, axis] -= fold2(sums[axis])

    self_copy.wait()

    def self_step(quad, carry):
        begin = quad * 4
        for k in range(4):
            tile = begin + k
            pair(
                tile,
                tile,
                range(0, ATOMS, CHUNK),
                table,
                tile,
                lambda rows, kept: table[tile, 3, rows, :] * self_ring[tile, kept, :],
                True,
            )
        return carry

    lax.fori_loop(0, TILES // 4, self_step, 0)

    def run(width, size, ring, copy, base, number, starts_of):
        def body(index, carry):
            begin = index * width
            for k in range(width):
                copy(begin + k, base + begin + k, True).wait()
            for k in range(width):
                first, second = decode(items[base + begin + k])
                slot = lax.rem(begin + k, size)
                factor = row_of(chain, second, 0)
                pair(
                    first,
                    second,
                    starts_of(first, second),
                    table,
                    first,
                    lambda rows, kept: table[first, 3, rows, :] * ring[slot, 0, kept, :]
                    + factor * ring[slot, 1, kept, :],
                    False,
                )
            for k in range(width):

                @pl.when(begin + k + size < number)
                def _():
                    copy(begin + k + size, base + begin + k + size, True).start()

            return carry

        lax.fori_loop(0, lax.div(number, width), body, 0)

    run(FULL_WIDTH, FULL_RING, full_ring, full_copy, 0, fulls, lambda *_: range(0, ATOMS, CHUNK))
    run(
        PART_WIDTH,
        PART_RING,
        part_ring,
        part_copy,
        fulls,
        parts,
        lambda first, second: part_starts(reach[first * REGION + second]),
    )

    def fold(tile):
        for axis in range(3):
            far[tile, axis] += fold_own(own[tile, axis])

    fold_rows(fold, 4)
    for axis in range(3):
        sums = jnp.sum(far[:, axis], axis=1) * (-SCALE * SCALE / 16.0)
        own_force[axis] = sums[0:TILES]
        above_force[axis] = sums[HALF : HALF + TILES]
        to_next[axis] = sums[TILES : TILES + 8]
        to_across[axis] = sums[HALF + TILES : HALF + TILES + 8]


SMEM = pl.BlockSpec(memory_space=pltpu.SMEM)
VMEM = pl.BlockSpec(memory_space=pltpu.VMEM)
ANY = pl.BlockSpec(memory_space=pl.ANY)
PARAMS = pltpu.CompilerParams(vmem_limit_bytes=VMEM_LIMIT)
RING_BLOCKS = (
    pltpu.VMEM((FULL_RING, 2) + BLOCK, F32),
    pltpu.VMEM((PART_RING, 2, PART, ATOMS), F32),
    pltpu.VMEM((TILES,) + BLOCK, F32),
)
RING_SEMS = (
    pltpu.SemaphoreType.DMA((FULL_RING,)),
    pltpu.SemaphoreType.DMA((PART_RING,)),
    pltpu.SemaphoreType.DMA((TILES,)),
)


def f32(*shape):
    return jax.ShapeDtypeStruct(shape, F32)


def run_pack(positions, charges, radii, scales, neighbours, pad_mask):
    return pl.pallas_call(
        pack_kernel,
        name="pack_atoms",
        out_shape=(
            f32(SENT_ROWS, ATOMS),
            f32(16, ATOMS),
            jax.ShapeDtypeStruct(neighbours.shape, jnp.int32),
        ),
        in_specs=[VMEM] * 6,
        out_specs=(VMEM,) * 3,
        compiler_params=PARAMS,
    )(positions, charges, radii, scales, neighbours, pad_mask)


def run_born(total, items, reach, sent, edges, above, above_edges):
    return pl.pallas_call(
        born_kernel,
        name="born_sums",
        out_shape=(
            f32(HALF, ATOMS),
            f32(HALF, ATOMS),
            f32(*LANES),
            f32(*LANES),
            f32(REGION, *LANES),
            f32(3, REGION, ATOMS),
            f32(TILES, *BLOCK),
            f32(PAIRS, 2, *BLOCK),
        ),
        in_specs=[SMEM] * 3 + [VMEM] * 4,
        out_specs=(VMEM,) * 6 + (ANY,) * 2,
        scratch_shapes=[
            pltpu.VMEM((OWN_ROWS, 5) + BLOCK, F32),
            pltpu.VMEM((2, 5) + BLOCK, F32),
            pltpu.VMEM((2, 5) + BLOCK, F32),
            pltpu.VMEM((OWN_ROWS,) + BLOCK, F32),
            pltpu.VMEM((REGION,) + LANES, F32),
            RING_BLOCKS,
            RING_SEMS,
        ],
        compiler_params=PARAMS,
    )(total, items, reach, sent, edges, above, above_edges)


def run_energy(total, items, reach, data, plain, shares):
    return pl.pallas_call(
        energy_kernel,
        name="radius_gradient",
        out_shape=(
            f32(TILES, ATOMS),
            f32(REGION, ATOMS),
            f32(HALF, ATOMS),
            f32(HALF, ATOMS),
            f32(*LANES),
            f32(*LANES),
            f32(REGION, 3, *LANES),
        ),
        in_specs=[SMEM] * 3 + [VMEM] * 6,
        out_specs=(VMEM,) * 7,
        scratch_shapes=[
            pltpu.VMEM((OWN_ROWS, 6) + BLOCK, F32),
            pltpu.VMEM((2, 6) + BLOCK, F32),
            pltpu.VMEM((2, 6) + BLOCK, F32),
            pltpu.VMEM((OWN_ROWS, 4) + BLOCK, F32),
            pltpu.VMEM((REGION,) + LANES, F32),
            pltpu.VMEM((REGION,) + LANES, F32),
        ],
        compiler_params=PARAMS,
    )(total, items, reach, data, plain, *shares)


def run_force(total, items, reach, data, slope, shares, force_in, d_self, d_pair):
    return pl.pallas_call(
        force_kernel,
        name="forces",
        out_shape=(
            f32(TILES, ATOMS),
            f32(3, TILES, ATOMS),
            f32(3, TILES, ATOMS),
            f32(3, *LANES),
            f32(3, *LANES),
        ),
        in_specs=[SMEM] * 3 + [VMEM] * 7 + [ANY] * 2,
        out_specs=(VMEM,) * 5,
        scratch_shapes=[
            pltpu.VMEM((OWN_ROWS, 4) + BLOCK, F32),
            pltpu.VMEM((OWN_ROWS, 3) + BLOCK, F32),
            pltpu.VMEM((REGION, 3) + LANES, F32),
            pltpu.VMEM((REGION,) + LANES, F32),
            RING_BLOCKS,
            RING_SEMS,
        ],
        compiler_params=PARAMS,
    )(total, items, reach, data, slope, *shares, force_in, d_self, d_pair)


def born_radius(descreen_sum, radius, radius_in):
    scaled = radius_in * descreen_sum
    polynomial = scaled * (obc_alpha + scaled * (-obc_beta + obc_gamma * scaled))
    tangent = jnp.tanh(polynomial)
    radii_born = 1.0 / (1.0 / radius_in - tangent / radius)
    radius_slope = (
        radii_born
        * radii_born
        * (1.0 - tangent * tangent)
        / radius
        * (obc_alpha - 2.0 * obc_beta * scaled + 3.0 * obc_gamma * scaled * scaled)
        * radius_in
    )
    return (radii_born, radius_slope)


def above_to_here(block):
    ends = lax.axis_size("slab") - 1
    return lax.ppermute(block, "slab", [(i + 1, i) for i in range(ends)])


def here_to_above(block):
    ends = lax.axis_size("slab") - 1
    return lax.ppermute(block, "slab", [(i, i + 1) for i in range(ends)])


def next_to_here(block):
    count = lax.axis_size("tile")
    return lax.ppermute(block, "tile", [((i + 1) % count, i) for i in range(count)])


def here_to_next(block):
    count = lax.axis_size("tile")
    return lax.ppermute(block, "tile", [(i, (i + 1) % count) for i in range(count)])


def pairwise(block, last):
    count = lax.axis_size("tile")
    pairs = [(i, (i + (-1 if (i % 2 == 0) == last else 1)) % count) for i in range(count)]
    return lax.ppermute(block, "tile", pairs)


def across_to_here(block):
    slabs, count = lax.axis_size("slab"), lax.axis_size("tile")
    pairs = [
        ((slab + 1) * count + (tile + 1) % count, slab * count + tile)
        for slab in range(slabs - 1)
        for tile in range(count)
    ]
    return lax.ppermute(block, ("slab", "tile"), pairs)


def placed(block, first, last):
    return jnp.pad(block[first : first + EDGE], ((0, HALF - EDGE), (0, 0))) + jnp.pad(
        last[first : first + EDGE], ((TILES, HALF - LIVE), (0, 0))
    )


def swap_sums(own, above, round_one, round_two):
    one, two = pairwise(round_one, False), pairwise(round_two, True)
    is_even = lax.axis_index("tile") % 2 == 0
    from_next, from_last = jnp.where(is_even, one, two), jnp.where(is_even, two, one)
    own = own + placed(from_last, 0, from_next)
    above = above + placed(from_last, EDGE, from_next)
    own, above = lax.optimization_barrier((own, above))
    return own, above, here_to_above(above), above_to_here(own)


def here_to_across(block):
    slabs, count = lax.axis_size("slab"), lax.axis_size("tile")
    pairs = [
        (slab * count + tile, (slab + 1) * count + (tile + 1) % count)
        for slab in range(slabs - 1)
        for tile in range(count)
    ]
    return lax.ppermute(block, ("slab", "tile"), pairs)


def slab_boxes(block, edges, across, along):
    rows = [
        jnp.concatenate(
            [
                block[axis * TILES : (axis + 1) * TILES],
                edges[axis * EDGE : (axis + 1) * EDGE],
                jnp.zeros((HALF - LIVE, ATOMS), F32),
            ]
        )
        for axis in range(3)
    ]
    x, y, z = rows
    pieces = jnp.stack([x * across + y * along, y * across - x * along, z]).reshape(3, HALF, CHUNKS, CHUNK)
    low, high = jnp.min(pieces, axis=3), jnp.max(pieces, axis=3)
    return low, high, jnp.min(low, axis=2), jnp.max(high, axis=2)


def chunk_codes(low, high, tile_low, tile_high):
    near = []
    for chunk in range(CHUNKS):
        own_low, own_high = low[:, :OWN_ROWS, chunk, None], high[:, :OWN_ROWS, chunk, None]
        gap = jnp.maximum(jnp.maximum(tile_low[:, None, :] - own_high, own_low - tile_high[:, None, :]), 0.0)
        far = jnp.sum(gap * gap, axis=0) >= cutoff_sq * 1.001
        near.append(jnp.logical_not(far).astype(jnp.int32))
    number = sum(near)
    code = number << (3 * CHUNKS)
    before = jnp.zeros_like(number)
    for chunk in range(CHUNKS):
        rank = jnp.where(near[chunk] == 1, before, number + chunk - before)
        code = code + (chunk << (3 * rank))
        before = before + near[chunk]
    return code


def chunk_reach(sent, edges, above, above_edges):
    across, along = sent[TILES // 2, 0], sent[TILES + TILES // 2, 0]
    inverse = lax.rsqrt(across * across + along * along)
    across, along = across * inverse, along * inverse
    low, high, *tile = slab_boxes(sent, edges, across, along)
    *_, above_low, above_high = slab_boxes(above, above_edges, across, along)
    own_codes = chunk_codes(low, high, *tile)
    code = jnp.concatenate([own_codes, chunk_codes(low, high, above_low, above_high)], axis=1)
    return code.reshape(-1), (code >> (3 * CHUNKS)) <= CHUNKS // 2


def packed(first, second, valid, is_part):
    first, second, valid = first.reshape(-1), second.reshape(-1), valid.reshape(-1)
    mine = (first[:, None] == jnp.arange(OWN_ROWS)[None, :]).astype(jnp.bfloat16)
    rows = jnp.dot(mine, is_part.astype(jnp.bfloat16), preferred_element_type=F32)
    in_part = jnp.sum(jnp.where(second[:, None] == jnp.arange(REGION)[None, :], rows, 0.0), axis=1) > 0.5
    entry = jnp.arange(valid.shape[0])
    ahead = valid[None, :] & (entry[None, :] < entry[:, None]) & (in_part[None, :] == in_part[:, None])
    rank = jnp.sum(ahead, axis=1)
    fulls = jnp.sum(valid & jnp.logical_not(in_part), dtype=jnp.int32)
    parts = jnp.sum(valid & in_part, dtype=jnp.int32)
    fulls = (fulls + FULL_WIDTH - 1) // FULL_WIDTH * FULL_WIDTH
    parts = (parts + PART_WIDTH - 1) // PART_WIDTH * PART_WIDTH
    rank = jnp.where(in_part, fulls + rank, rank)
    chosen = valid[None, :] & (rank[None, :] == jnp.arange(ITEMS)[:, None])
    value = first * ATOMS + second - DUMMY
    items = DUMMY + jnp.sum(jnp.where(chosen, value[None, :], 0), axis=1)
    return jnp.stack([fulls, parts]), items.astype(jnp.int32)


def pair_items(here, above, is_part):
    listed = above[6 * TILES :, 0:TILES].astype(jnp.int32)
    has_above = lax.axis_index("slab") < lax.axis_size("slab") - 1
    tiles = lax.broadcasted_iota(jnp.int32, here.shape, 1)
    return packed(
        jnp.concatenate([tiles, listed]),
        jnp.concatenate([here, HALF + tiles]),
        jnp.concatenate([here >= 0, (listed >= 0) & has_above]),
        is_part,
    )


def body(positions, charges, radii, scales, neighbours, pad_mask):
    sent, edges, here = run_pack(
        jnp.swapaxes(positions[0, 0], 0, 1),
        charges[0, 0],
        radii[0, 0],
        scales[0, 0],
        neighbours[0, 0].T,
        pad_mask[0, 0].T,
    )
    above = above_to_here(sent)
    next_edges = next_to_here(edges)
    above_edges = across_to_here(edges)
    reach, is_part = chunk_reach(sent, next_edges, above, above_edges)
    total, items = pair_items(here, above, is_part)

    *parts, data, plain, d_self, d_pair = run_born(total, items, reach, sent, next_edges, above, above_edges)
    shares = swap_sums(*parts)
    radii_born, slope, *parts, force = run_energy(total, items, reach, data, plain, shares)
    shares = swap_sums(*parts)
    gradient, own, over, to_next, to_across = run_force(
        total, items, reach, data, slope, shares, force, d_self, d_pair
    )
    from_below = here_to_above(over)
    edge = here_to_next(to_next) + here_to_across(to_across)
    forces = own + from_below + jnp.pad(edge[:, 0:EDGE], ((0, 0), (0, TILES - EDGE), (0, 0)))
    return (radii_born[None, None], gradient[None, None], jnp.swapaxes(forces, 0, 1)[None, None])


def solution(mesh):
    return jax.shard_map(
        body,
        mesh=mesh,
        in_specs=(
            P("slab", "tile", None, None, None),
            P("slab", "tile", None, None),
            P("slab", "tile", None, None),
            P("slab", "tile", None, None),
            P("slab", "tile", None, None),
            P("slab", "tile", None, None),
        ),
        out_specs=(
            P("slab", "tile", None, None),
            P("slab", "tile", None, None),
            P("slab", "tile", None, None, None),
        ),
        check_vma=False,
    )
```

```python
import functools
import math

import jax
import jax.numpy as jnp
import numpy as np
from jax import lax
from jax.experimental import pallas as pl
from jax.experimental.pallas import tpu as pltpu
from jax.sharding import PartitionSpec as P

radius_offset = 0.09
obc_alpha = 1.0
obc_beta = 0.8
obc_gamma = 4.85
cutoff_len = 14.0
cutoff_sq = cutoff_len * cutoff_len

TILES = 32
EDGE = 2
LIVE = TILES + EDGE
HALF = 40
REGION = 2 * HALF
OWN_ROWS = LIVE + 1
SENT_ROWS = 6 * TILES + 8
LISTED = 7
ATOMS = 128
CHUNK = 16
CHUNKS = ATOMS // CHUNK
FULL_WIDTH = 4
PART_WIDTH = 4
FULL_RING = 32
PART_RING = 32
PAIRS = 2 * TILES * LISTED + 6
ITEMS = 512
DUMMY = LIVE * ATOMS + LIVE
ROW = (1, ATOMS)
LANES = (8, ATOMS)
ROWS = (CHUNK, ATOMS)
BLOCK = (ATOMS, ATOMS)
PART = ATOMS // 2
VMEM_LIMIT = 56 * 1024 * 1024
SCALE = math.sqrt(8.0) / cutoff_len
CUT = 8.0
EXP_SCALE = math.sqrt(0.25 / math.log(2.0)) / SCALE

ROW_X, ROW_Y, ROW_Z, ROW_Q, ROW_IN, ROW_SCALED = range(6)
AT_Q, AT_RADIUS, AT_SCALED = 3, 4, 5

F32 = jnp.float32


def fold2(block):
    return block[0:8] + block[8:16]


def fold_own(own):
    flipped = own.T
    total = flipped[0:8]
    for chunk in range(1, ATOMS // 8):
        total = total + flipped[8 * chunk : 8 * chunk + 8]
    return total


def build_beside(build, work, table, fresh_a, fresh_b):
    def keep(tile, fresh, k):
        table[tile] = fresh[k]

    def step(index, carry):
        first = index * 4
        for k in range(2):
            build(first + 2 + k, fresh_b, k)
            work(first + k, fresh_a, k)
        for k in range(2):
            keep(first + k, fresh_a, k)
        for k in range(2):
            build(first + 4 + k, fresh_a, k)
            work(first + 2 + k, fresh_b, k)
        for k in range(2):
            keep(first + 2 + k, fresh_b, k)
        return carry

    for k in range(2):
        build(k, fresh_a, k)
    lax.fori_loop(0, TILES // 4, step, 0)
    for k in range(EDGE):
        keep(TILES + k, fresh_a, k)


def by_fours(step):
    def fours(index, carry):
        start = jnp.minimum(index * 4, LIVE - 4)
        for k in range(4):
            step(start + k)
        return carry

    lax.fori_loop(0, (LIVE + 3) // 4, fours, 0)


def fill_table(table, k, first, ref, tile, rows):
    for slot, row in enumerate(rows):
        table[k, first + slot] = jnp.broadcast_to(ref[tile, row : row + 1, :], BLOCK).T


def fold_rows(fold, width):
    def step(index, carry):
        for k in range(width):
            fold(index * width + k)
        return carry

    lax.fori_loop(0, TILES // width, step, 0)
    for tile in range(TILES, LIVE):
        fold(tile)


def diagonal(start):
    rows = lax.broadcasted_iota(jnp.int32, ROWS, 0) + start
    return jnp.where(rows == lax.broadcasted_iota(jnp.int32, ROWS, 1), 4.0 * CUT, 0.0)


def decode(item):
    return lax.shift_right_logical(item, 7), lax.bitwise_and(item, ATOMS - 1)


def span(start):
    return pl.ds(start if isinstance(start, int) else pl.multiple_of(start, CHUNK), CHUNK)


def part_starts(code):
    return [lax.bitwise_and(lax.shift_right_logical(code, 3 * j), 7) * CHUNK for j in range(CHUNKS // 2)]


def row_of(ref, tile, row):
    return jnp.broadcast_to(ref[tile, row : row + 1, :], ROWS)


def differences(table, tile, rows, far):
    return tuple(table[tile, axis, rows, :] - far[axis] for axis in range(3))


def distance_squared(gaps):
    dx, dy, dz = gaps
    return dx * dx + dy * dy + dz * dz


def half_descreen(r, own, far):
    upper = r + far
    lower = r - far
    inner = jnp.minimum(jnp.maximum(own, lower), upper)
    ratio = upper * pl.reciprocal(inner, approx=True)
    slope = lower * pl.reciprocal(upper, approx=True)
    square = ratio * ratio
    rise = ratio - 1.0
    twice = jnp.log(square)
    value = rise * (2.0 - slope * rise) - twice
    deriv = (twice + twice) - (square - 1.0) * (slope * slope + 1.0)
    return value, deriv


def ring_copies(ring, blocks, sems, size, rows):
    def copy(index, place, inward):
        slot = lax.rem(index, size)
        here = ring.at[slot]
        there = blocks.at[place, :, pl.ds(0, rows), :]
        source, target = (there, here) if inward else (here, there)
        return pltpu.make_async_copy(source, target, sems.at[slot])

    return copy


def edge_rows(values, first):
    rest = jnp.zeros((8 - 2 * EDGE, ATOMS), F32)
    return jnp.concatenate([values[first : first + EDGE], values[HALF + first : HALF + first + EDGE], rest])


def edge_rounds(values, one, two):
    to_next, to_last = edge_rows(values, TILES), edge_rows(values, 0)
    is_even = lax.rem(lax.axis_index("tile"), 2) == 0
    one[...] = jnp.where(is_even, to_next, to_last)
    two[...] = jnp.where(is_even, to_last, to_next)


def pack_kernel(positions, charges, radii, scales, neighbours, pad_mask, sent, edges, here):
    radius = radii[...]
    values = [positions[0], positions[1], positions[2], charges[...], radius, scales[...] * (radius - radius_offset)]
    edges[...] = jnp.zeros_like(edges)
    for index, value in enumerate(values):
        sent[index * TILES : (index + 1) * TILES, :] = value
        edges[EDGE * index : EDGE * (index + 1), :] = value[0:EDGE]
    cycle_count = lax.axis_size("tile")
    cycle_tiles = cycle_count * TILES
    listed = neighbours[...]
    slab_step = lax.div(listed, cycle_tiles) - lax.axis_index("slab")
    within = lax.rem(listed, cycle_tiles)
    cycle_step = lax.rem(lax.div(within, TILES) - lax.axis_index("tile") + cycle_count, cycle_count)
    place = cycle_step * TILES + lax.rem(within, TILES)
    slots = lax.broadcasted_iota(jnp.int32, listed.shape, 0)
    live = (pad_mask[...] == 1) & (slots > 0)
    here[...] = jnp.where(live & (slab_step >= 0), slab_step * HALF + place, -1)
    sent[6 * TILES :, :] = jnp.full(LANES, -1.0, F32)
    sent[6 * TILES :, 0:TILES] = jnp.where(live & (slab_step < 0), place, -1).astype(F32)


def born_kernel(
    total, items, reach, sent, edges, above, above_edges,
    own_part, above_part, round_one, round_two, data, plain, d_self, d_pair,
    table, fresh_a, fresh_b, own, far, rings, sems,
):
    full_ring, part_ring, self_ring = rings
    full_sems, part_sems, self_sems = sems
    far[...] = jnp.zeros_like(far)
    data[...] = jnp.zeros_like(data)
    plain[...] = jnp.ones_like(plain)
    fulls, parts = total[0], total[1]

    for index in range(6):
        origin = sent[index * TILES + TILES // 2 : index * TILES + TILES // 2 + 1, 0:1]
        for start, source, edge in ((0, sent, edges), (HALF, above, above_edges)):
            for place, values in (
                (start, source[index * TILES : (index + 1) * TILES, :]),
                (start + TILES, edge[EDGE * index : EDGE * (index + 1), :]),
            ):
                rows = slice(place, place + values.shape[0])
                if index < AT_Q:
                    data[rows, index, :] = (values - origin) * SCALE
                elif index == AT_Q:
                    data[rows, ROW_Q, :] = values
                    plain[2, rows, :] = values if place == 0 else jnp.zeros_like(values)
                elif index == AT_RADIUS:
                    data[rows, ROW_IN, :] = (values - radius_offset) * SCALE
                    plain[0, rows, :] = values
                    plain[1, rows, :] = values - radius_offset
                else:
                    data[rows, ROW_SCALED, :] = values * SCALE

    def build(tile, fresh, k):
        fill_table(fresh, k, 0, data, tile, (ROW_X, ROW_Y, ROW_Z, ROW_IN, ROW_SCALED))

    for tile in range(TILES, OWN_ROWS):
        own[tile] = jnp.zeros(BLOCK, F32)

    def shared(r2):
        inv = lax.rsqrt(r2)
        cut = jnp.maximum(1.0 - r2 * (1.0 / CUT), 0.0)
        cinv = cut * inv
        return r2 * inv, cut, cinv, cinv * cinv * inv

    def self_pair(tile, fresh, k):
        far_xyz = [row_of(data, tile, axis) for axis in range(3)]
        bs = row_of(data, tile, ROW_SCALED)
        for start in range(0, ATOMS, CHUNK):
            rows = span(start)
            r2 = distance_squared(differences(fresh, k, rows, far_xyz)) + diagonal(start)
            r, cut, cinv, g_deriv = shared(r2)
            value, deriv = half_descreen(r, fresh[k, 3, rows, :], bs)
            value = cinv * value
            own[tile, rows, :] = cut * value
            self_ring[tile, rows, :] = g_deriv * deriv - value

    def self_copy(tile):
        return pltpu.make_async_copy(self_ring.at[tile], d_self.at[tile], self_sems.at[tile])

    def self_step(tile, fresh, k):
        self_pair(tile, fresh, k)
        self_copy(tile).start()

    build_beside(build, self_step, table, fresh_a, fresh_b)

    def pair(item, ring, slot, starts):
        first, second = item
        far_xyz = [row_of(data, second, axis) for axis in range(3)]
        bp, bs = row_of(data, second, ROW_IN), row_of(data, second, ROW_SCALED)
        sums = jnp.zeros(ROWS, F32)
        for place, start in enumerate(starts):
            rows = span(start)
            kept = span(place * CHUNK)
            r2 = distance_squared(differences(table, first, rows, far_xyz))
            r, cut, cinv, g_deriv = shared(r2)
            value, deriv = half_descreen(r, table[first, 3, rows, :], bs)
            value = cinv * value
            own[first, rows, :] += cut * value
            ring[slot, 0, kept, :] = g_deriv * deriv - value
            value, deriv = half_descreen(r, bp, table[first, 4, rows, :])
            value = cinv * value
            ring[slot, 1, kept, :] = g_deriv * deriv - value
            sums = sums + cut * value
        far[second] += fold2(sums)

    def run(width, size, ring, ring_sems, base, number, rows, starts_of):
        copy = ring_copies(ring, d_pair, ring_sems, size, rows)

        def body(index, carry):
            begin = index * width
            for k in range(width):

                @pl.when(begin + k >= size)
                def _():
                    copy(begin + k, base + begin + k, False).wait()

            for k in range(width):
                item = decode(items[base + begin + k])
                pair(item, ring, lax.rem(begin + k, size), starts_of(item))
            for k in range(width):
                copy(begin + k, base + begin + k, False).start()
            return carry

        lax.fori_loop(0, lax.div(number, width), body, 0)

    def drain(size, ring, ring_sems, number, rows):
        copy = ring_copies(ring, d_pair, ring_sems, size, rows)

        def wait(slot, carry):
            copy(slot, slot, False).wait()
            return carry

        lax.fori_loop(0, jnp.minimum(number, size), wait, 0)

    def listed_starts(item):
        return part_starts(reach[item[0] * REGION + item[1]])

    run(FULL_WIDTH, FULL_RING, full_ring, full_sems, 0, fulls, ATOMS, lambda item: range(0, ATOMS, CHUNK))
    run(PART_WIDTH, PART_RING, part_ring, part_sems, fulls, parts, PART, listed_starts)

    def fold(tile):
        far[tile] += fold_own(own[tile])

    fold_rows(fold, 8)
    sums = jnp.sum(far[...], axis=1) * (0.125 * SCALE)
    own_part[...] = sums[0:HALF]
    above_part[...] = sums[HALF:]
    edge_rounds(sums, round_one, round_two)

    def wait_self(tile, carry):
        self_copy(tile).wait()
        return carry

    lax.fori_loop(0, TILES, wait_self, 0)
    drain(FULL_RING, full_ring, full_sems, fulls, ATOMS)
    drain(PART_RING, part_ring, part_sems, parts, PART)


def energy_kernel(
    total, items, reach, data, plain, own_part, above_part, from_below, from_above,
    radii_born, slope, own_grad, above_grad, round_one, round_two, force,
    table, fresh_a, fresh_b, own, far, born,
):
    far[...] = jnp.zeros_like(far)
    force[...] = jnp.zeros_like(force)
    fulls, parts = total[0], total[1]
    sums = jnp.concatenate([own_part[...] + from_below[...], above_part[...] + from_above[...]])
    all_radii, all_slopes = born_radius(sums, plain[0], plain[1])
    inverse = 1.0 / all_radii
    radii_born[...] = all_radii[0:TILES]
    slope[...] = all_slopes
    born[:, 0, :] = SCALE * all_radii
    born[:, 1, :] = EXP_SCALE * inverse

    def build(tile, fresh, k):
        fill_table(fresh, k, 0, data, tile, (ROW_X, ROW_Y, ROW_Z, ROW_Q))
        fill_table(fresh, k, 4, born, tile, (0, 1))

    for tile in range(TILES, OWN_ROWS):
        own[tile] = jnp.zeros((4,) + BLOCK, F32)

    def pair(first, second, starts, tables, k, is_self):
        far_xyz = [row_of(data, second, axis) for axis in range(3)]
        br, bi, bq = row_of(born, second, 0), -row_of(born, second, 1), row_of(data, second, ROW_Q)
        sums = [jnp.zeros(ROWS, F32)] * 4
        for start in starts:
            rows = span(start)
            gaps = differences(tables, k, rows, far_xyz)
            r2 = distance_squared(gaps)
            if is_self:
                r2 = r2 + diagonal(start)
            cut = jnp.maximum(1.0 - r2 * (1.0 / CUT), 0.0)
            power = r2 * (tables[k, 5, rows, :] * bi)
            decay = lax.exp2(power)
            screen = (tables[k, 4, rows, :] * br) * decay
            inv = lax.rsqrt(r2 + screen)
            cinv = cut * inv
            lead = (tables[k, 3, rows, :] * bq) * cinv
            square = cinv * inv
            grad = (lead * square) * (screen * (1.0 - math.log(2.0) * power))
            pull = lead * (square * (4.0 - decay) + 16.0 / CUT)
            terms = [grad] + [pull * gap for gap in gaps]
            for which, term in enumerate(terms):
                if is_self:
                    own[first, which, rows, :] = term
                else:
                    own[first, which, rows, :] += term
                    sums[which] = sums[which] + term
        if not is_self:
            far[second] += fold2(sums[0])
            for axis in range(3):
                force[second, axis] -= fold2(sums[1 + axis])

    def self_step(tile, fresh, k):
        pair(tile, tile, range(0, ATOMS, CHUNK), fresh, k, True)

    build_beside(build, self_step, table, fresh_a, fresh_b)

    def full_step(index, carry):
        for k in range(FULL_WIDTH):
            first, second = decode(items[index * FULL_WIDTH + k])
            pair(first, second, range(0, ATOMS, CHUNK), table, first, False)
        return carry

    def part_step(index, carry):
        for k in range(PART_WIDTH):
            first, second = decode(items[fulls + index * PART_WIDTH + k])
            starts = part_starts(reach[first * REGION + second])
            pair(first, second, starts, table, first, False)
        return carry

    lax.fori_loop(0, lax.div(fulls, FULL_WIDTH), full_step, 0)
    lax.fori_loop(0, lax.div(parts, PART_WIDTH), part_step, 0)

    def fold(tile):
        far[tile] += fold_own(own[tile, 0])
        for axis in range(3):
            force[tile, axis] += fold_own(own[tile, 1 + axis])

    fold_rows(fold, 4)
    charge = plain[2] * inverse
    sums = jnp.sum(far[...], axis=1) * (0.5 * SCALE) * inverse + 0.5 * charge * charge
    own_grad[...] = sums[0:HALF]
    above_grad[...] = sums[HALF:]
    edge_rounds(sums, round_one, round_two)


def force_kernel(
    total, items, reach, data, slope, own_grad, above_grad, from_below, from_above, force_in, d_self, d_pair,
    gradient, own_force, above_force, to_next, to_across,
    table, own, far, chain, rings, sems,
):
    full_ring, part_ring, self_ring = rings
    full_sems, part_sems, self_sems = sems
    fulls, parts = total[0], total[1]
    full_copy = ring_copies(full_ring, d_pair, full_sems, FULL_RING, ATOMS)
    part_copy = ring_copies(part_ring, d_pair, part_sems, PART_RING, PART)

    self_copy = pltpu.make_async_copy(d_self, self_ring, self_sems.at[0])

    def start(copy, base):
        def step(index, carry):
            copy(index, base + index, True).start()
            return carry

        return step

    self_copy.start()
    lax.fori_loop(0, jnp.minimum(fulls, FULL_RING), start(full_copy, 0), 0)
    lax.fori_loop(0, jnp.minimum(parts, PART_RING), start(part_copy, fulls), 0)

    far[...] = force_in[...] * 4.0
    grads = jnp.concatenate([own_grad[...] + from_below[...], above_grad[...] + from_above[...]])
    gradient[...] = grads[0:TILES]
    chain[:, 0, :] = grads * slope[...]

    def build(tile):
        fill_table(table, tile, 0, data, tile, (ROW_X, ROW_Y, ROW_Z))
        fill_table(table, tile, 3, chain, tile, (0,))

    by_fours(build)
    for tile in range(TILES, OWN_ROWS):
        own[tile] = jnp.zeros((3,) + BLOCK, F32)

    def pair(first, second, starts, tables, k, pull_of, is_self):
        far_xyz = [row_of(data, second, axis) for axis in range(3)]
        sums = [jnp.zeros(ROWS, F32)] * 3
        for place, start in enumerate(starts):
            rows = span(start)
            pull = pull_of(rows, span(place * CHUNK))
            terms = [pull * gap for gap in differences(tables, k, rows, far_xyz)]
            for which, term in enumerate(terms):
                if is_self:
                    own[first, which, rows, :] = term
                else:
                    own[first, which, rows, :] += term
                sums[which] = sums[which] + term
        for axis in range(3):
            far[second, axis] -= fold2(sums[axis])

    self_copy.wait()

    def self_step(quad, carry):
        begin = quad * 4
        for k in range(4):
            tile = begin + k
            pair(
                tile,
                tile,
                range(0, ATOMS, CHUNK),
                table,
                tile,
                lambda rows, kept: table[tile, 3, rows, :] * self_ring[tile, kept, :],
                True,
            )
        return carry

    lax.fori_loop(0, TILES // 4, self_step, 0)

    def run(width, size, ring, copy, base, number, starts_of):
        def body(index, carry):
            begin = index * width
            for k in range(width):
                copy(begin + k, base + begin + k, True).wait()
            for k in range(width):
                first, second = decode(items[base + begin + k])
                slot = lax.rem(begin + k, size)
                factor = row_of(chain, second, 0)
                pair(
                    first,
                    second,
                    starts_of(first, second),
                    table,
                    first,
                    lambda rows, kept: table[first, 3, rows, :] * ring[slot, 0, kept, :]
                    + factor * ring[slot, 1, kept, :],
                    False,
                )
            for k in range(width):

                @pl.when(begin + k + size < number)
                def _():
                    copy(begin + k + size, base + begin + k + size, True).start()

            return carry

        lax.fori_loop(0, lax.div(number, width), body, 0)

    run(FULL_WIDTH, FULL_RING, full_ring, full_copy, 0, fulls, lambda *_: range(0, ATOMS, CHUNK))
    run(
        PART_WIDTH,
        PART_RING,
        part_ring,
        part_copy,
        fulls,
        parts,
        lambda first, second: part_starts(reach[first * REGION + second]),
    )

    def fold(tile):
        for axis in range(3):
            far[tile, axis] += fold_own(own[tile, axis])

    fold_rows(fold, 4)
    for axis in range(3):
        sums = jnp.sum(far[:, axis], axis=1) * (-SCALE * SCALE / 16.0)
        own_force[axis] = sums[0:TILES]
        above_force[axis] = sums[HALF : HALF + TILES]
        to_next[axis] = sums[TILES : TILES + 8]
        to_across[axis] = sums[HALF + TILES : HALF + TILES + 8]


SMEM = pl.BlockSpec(memory_space=pltpu.SMEM)
VMEM = pl.BlockSpec(memory_space=pltpu.VMEM)
ANY = pl.BlockSpec(memory_space=pl.ANY)
PARAMS = pltpu.CompilerParams(vmem_limit_bytes=VMEM_LIMIT)
RING_BLOCKS = (
    pltpu.VMEM((FULL_RING, 2) + BLOCK, F32),
    pltpu.VMEM((PART_RING, 2, PART, ATOMS), F32),
    pltpu.VMEM((TILES,) + BLOCK, F32),
)
RING_SEMS = (
    pltpu.SemaphoreType.DMA((FULL_RING,)),
    pltpu.SemaphoreType.DMA((PART_RING,)),
    pltpu.SemaphoreType.DMA((TILES,)),
)


def f32(*shape):
    return jax.ShapeDtypeStruct(shape, F32)


def run_pack(positions, charges, radii, scales, neighbours, pad_mask):
    return pl.pallas_call(
        pack_kernel,
        name="pack_atoms",
        out_shape=(
            f32(SENT_ROWS, ATOMS),
            f32(16, ATOMS),
            jax.ShapeDtypeStruct(neighbours.shape, jnp.int32),
        ),
        in_specs=[VMEM] * 6,
        out_specs=(VMEM,) * 3,
        compiler_params=PARAMS,
    )(positions, charges, radii, scales, neighbours, pad_mask)


def run_born(total, items, reach, sent, edges, above, above_edges):
    return pl.pallas_call(
        born_kernel,
        name="born_sums",
        out_shape=(
            f32(HALF, ATOMS),
            f32(HALF, ATOMS),
            f32(*LANES),
            f32(*LANES),
            f32(REGION, *LANES),
            f32(3, REGION, ATOMS),
            f32(TILES, *BLOCK),
            f32(PAIRS, 2, *BLOCK),
        ),
        in_specs=[SMEM] * 3 + [VMEM] * 4,
        out_specs=(VMEM,) * 6 + (ANY,) * 2,
        scratch_shapes=[
            pltpu.VMEM((OWN_ROWS, 5) + BLOCK, F32),
            pltpu.VMEM((2, 5) + BLOCK, F32),
            pltpu.VMEM((2, 5) + BLOCK, F32),
            pltpu.VMEM((OWN_ROWS,) + BLOCK, F32),
            pltpu.VMEM((REGION,) + LANES, F32),
            RING_BLOCKS,
            RING_SEMS,
        ],
        compiler_params=PARAMS,
    )(total, items, reach, sent, edges, above, above_edges)


def run_energy(total, items, reach, data, plain, shares):
    return pl.pallas_call(
        energy_kernel,
        name="radius_gradient",
        out_shape=(
            f32(TILES, ATOMS),
            f32(REGION, ATOMS),
            f32(HALF, ATOMS),
            f32(HALF, ATOMS),
            f32(*LANES),
            f32(*LANES),
            f32(REGION, 3, *LANES),
        ),
        in_specs=[SMEM] * 3 + [VMEM] * 6,
        out_specs=(VMEM,) * 7,
        scratch_shapes=[
            pltpu.VMEM((OWN_ROWS, 6) + BLOCK, F32),
            pltpu.VMEM((2, 6) + BLOCK, F32),
            pltpu.VMEM((2, 6) + BLOCK, F32),
            pltpu.VMEM((OWN_ROWS, 4) + BLOCK, F32),
            pltpu.VMEM((REGION,) + LANES, F32),
            pltpu.VMEM((REGION,) + LANES, F32),
        ],
        compiler_params=PARAMS,
    )(total, items, reach, data, plain, *shares)


def run_force(total, items, reach, data, slope, shares, force_in, d_self, d_pair):
    return pl.pallas_call(
        force_kernel,
        name="forces",
        out_shape=(
            f32(TILES, ATOMS),
            f32(3, TILES, ATOMS),
            f32(3, TILES, ATOMS),
            f32(3, *LANES),
            f32(3, *LANES),
        ),
        in_specs=[SMEM] * 3 + [VMEM] * 7 + [ANY] * 2,
        out_specs=(VMEM,) * 5,
        scratch_shapes=[
            pltpu.VMEM((OWN_ROWS, 4) + BLOCK, F32),
            pltpu.VMEM((OWN_ROWS, 3) + BLOCK, F32),
            pltpu.VMEM((REGION, 3) + LANES, F32),
            pltpu.VMEM((REGION,) + LANES, F32),
            RING_BLOCKS,
            RING_SEMS,
        ],
        compiler_params=PARAMS,
    )(total, items, reach, data, slope, *shares, force_in, d_self, d_pair)


def born_radius(descreen_sum, radius, radius_in):
    scaled = radius_in * descreen_sum
    polynomial = scaled * (obc_alpha + scaled * (-obc_beta + obc_gamma * scaled))
    tangent = jnp.tanh(polynomial)
    radii_born = 1.0 / (1.0 / radius_in - tangent / radius)
    radius_slope = (
        radii_born
        * radii_born
        * (1.0 - tangent * tangent)
        / radius
        * (obc_alpha - 2.0 * obc_beta * scaled + 3.0 * obc_gamma * scaled * scaled)
        * radius_in
    )
    return (radii_born, radius_slope)


def above_to_here(block):
    ends = lax.axis_size("slab") - 1
    return lax.ppermute(block, "slab", [(i + 1, i) for i in range(ends)])


def here_to_above(block):
    ends = lax.axis_size("slab") - 1
    return lax.ppermute(block, "slab", [(i, i + 1) for i in range(ends)])


def next_to_here(block):
    count = lax.axis_size("tile")
    return lax.ppermute(block, "tile", [((i + 1) % count, i) for i in range(count)])


def here_to_next(block):
    count = lax.axis_size("tile")
    return lax.ppermute(block, "tile", [(i, (i + 1) % count) for i in range(count)])


def pairwise(block, last):
    count = lax.axis_size("tile")
    pairs = [(i, (i + (-1 if (i % 2 == 0) == last else 1)) % count) for i in range(count)]
    return lax.ppermute(block, "tile", pairs)


def across_to_here(block):
    slabs, count = lax.axis_size("slab"), lax.axis_size("tile")
    pairs = [
        ((slab + 1) * count + (tile + 1) % count, slab * count + tile)
        for slab in range(slabs - 1)
        for tile in range(count)
    ]
    return lax.ppermute(block, ("slab", "tile"), pairs)


def placed(block, first, last):
    return jnp.pad(block[first : first + EDGE], ((0, HALF - EDGE), (0, 0))) + jnp.pad(
        last[first : first + EDGE], ((TILES, HALF - LIVE), (0, 0))
    )


def swap_sums(own, above, round_one, round_two):
    one, two = pairwise(round_one, False), pairwise(round_two, True)
    is_even = lax.axis_index("tile") % 2 == 0
    from_next, from_last = jnp.where(is_even, one, two), jnp.where(is_even, two, one)
    own = own + placed(from_last, 0, from_next)
    above = above + placed(from_last, EDGE, from_next)
    own, above = lax.optimization_barrier((own, above))
    return own, above, here_to_above(above), above_to_here(own)


def here_to_across(block):
    slabs, count = lax.axis_size("slab"), lax.axis_size("tile")
    pairs = [
        (slab * count + tile, (slab + 1) * count + (tile + 1) % count)
        for slab in range(slabs - 1)
        for tile in range(count)
    ]
    return lax.ppermute(block, ("slab", "tile"), pairs)


def slab_boxes(block, edges, across, along):
    rows = [
        jnp.concatenate(
            [
                block[axis * TILES : (axis + 1) * TILES],
                edges[axis * EDGE : (axis + 1) * EDGE],
                jnp.zeros((HALF - LIVE, ATOMS), F32),
            ]
        )
        for axis in range(3)
    ]
    x, y, z = rows
    pieces = jnp.stack([x * across + y * along, y * across - x * along, z]).reshape(3, HALF, CHUNKS, CHUNK)
    low, high = jnp.min(pieces, axis=3), jnp.max(pieces, axis=3)
    return low, high, jnp.min(low, axis=2), jnp.max(high, axis=2)


def chunk_codes(low, high, tile_low, tile_high):
    near = []
    for chunk in range(CHUNKS):
        own_low, own_high = low[:, :OWN_ROWS, chunk, None], high[:, :OWN_ROWS, chunk, None]
        gap = jnp.maximum(jnp.maximum(tile_low[:, None, :] - own_high, own_low - tile_high[:, None, :]), 0.0)
        far = jnp.sum(gap * gap, axis=0) >= cutoff_sq * 1.001
        near.append(jnp.logical_not(far).astype(jnp.int32))
    number = sum(near)
    code = number << (3 * CHUNKS)
    before = jnp.zeros_like(number)
    for chunk in range(CHUNKS):
        rank = jnp.where(near[chunk] == 1, before, number + chunk - before)
        code = code + (chunk << (3 * rank))
        before = before + near[chunk]
    return code


def chunk_reach(sent, edges, above, above_edges):
    across, along = sent[TILES // 2, 0], sent[TILES + TILES // 2, 0]
    inverse = lax.rsqrt(across * across + along * along)
    across, along = across * inverse, along * inverse
    low, high, *tile = slab_boxes(sent, edges, across, along)
    *_, above_low, above_high = slab_boxes(above, above_edges, across, along)
    own_codes = chunk_codes(low, high, *tile)
    code = jnp.concatenate([own_codes, chunk_codes(low, high, above_low, above_high)], axis=1)
    return code.reshape(-1), (code >> (3 * CHUNKS)) <= CHUNKS // 2


def packed(first, second, valid, is_part):
    first, second, valid = first.reshape(-1), second.reshape(-1), valid.reshape(-1)
    mine = (first[:, None] == jnp.arange(OWN_ROWS)[None, :]).astype(jnp.bfloat16)
    rows = jnp.dot(mine, is_part.astype(jnp.bfloat16), preferred_element_type=F32)
    in_part = jnp.sum(jnp.where(second[:, None] == jnp.arange(REGION)[None, :], rows, 0.0), axis=1) > 0.5
    entry = jnp.arange(valid.shape[0])
    ahead = valid[None, :] & (entry[None, :] < entry[:, None]) & (in_part[None, :] == in_part[:, None])
    rank = jnp.sum(ahead, axis=1)
    fulls = jnp.sum(valid & jnp.logical_not(in_part), dtype=jnp.int32)
    parts = jnp.sum(valid & in_part, dtype=jnp.int32)
    fulls = (fulls + FULL_WIDTH - 1) // FULL_WIDTH * FULL_WIDTH
    parts = (parts + PART_WIDTH - 1) // PART_WIDTH * PART_WIDTH
    rank = jnp.where(in_part, fulls + rank, rank)
    chosen = valid[None, :] & (rank[None, :] == jnp.arange(ITEMS)[:, None])
    value = first * ATOMS + second - DUMMY
    items = DUMMY + jnp.sum(jnp.where(chosen, value[None, :], 0), axis=1)
    return jnp.stack([fulls, parts]), items.astype(jnp.int32)


def pair_items(here, above, is_part):
    listed = above[6 * TILES :, 0:TILES].astype(jnp.int32)
    has_above = lax.axis_index("slab") < lax.axis_size("slab") - 1
    tiles = lax.broadcasted_iota(jnp.int32, here.shape, 1)
    return packed(
        jnp.concatenate([tiles, listed]),
        jnp.concatenate([here, HALF + tiles]),
        jnp.concatenate([here >= 0, (listed >= 0) & has_above]),
        is_part,
    )


def body(positions, charges, radii, scales, neighbours, pad_mask):
    sent, edges, here = run_pack(
        jnp.swapaxes(positions[0, 0], 0, 1),
        charges[0, 0],
        radii[0, 0],
        scales[0, 0],
        neighbours[0, 0].T,
        pad_mask[0, 0].T,
    )
    above = above_to_here(sent)
    next_edges = next_to_here(edges)
    above_edges = across_to_here(edges)
    reach, is_part = chunk_reach(sent, next_edges, above, above_edges)
    total, items = pair_items(here, above, is_part)

    *parts, data, plain, d_self, d_pair = run_born(total, items, reach, sent, next_edges, above, above_edges)
    shares = swap_sums(*parts)
    radii_born, slope, *parts, force = run_energy(total, items, reach, data, plain, shares)
    shares = swap_sums(*parts)
    gradient, own, over, to_next, to_across = run_force(
        total, items, reach, data, slope, shares, force, d_self, d_pair
    )
    forces, to_next, to_across = lax.optimization_barrier(
        (own + here_to_above(over), here_to_next(to_next), here_to_across(to_across))
    )
    forces = forces + jnp.pad((to_next + to_across)[:, 0:EDGE], ((0, 0), (0, TILES - EDGE), (0, 0)))
    return (radii_born[None, None], gradient[None, None], jnp.swapaxes(forces, 0, 1)[None, None])


def solution(mesh):
    return jax.shard_map(
        body,
        mesh=mesh,
        in_specs=(
            P("slab", "tile", None, None, None),
            P("slab", "tile", None, None),
            P("slab", "tile", None, None),
            P("slab", "tile", None, None),
            P("slab", "tile", None, None),
            P("slab", "tile", None, None),
        ),
        out_specs=(
            P("slab", "tile", None, None),
            P("slab", "tile", None, None),
            P("slab", "tile", None, None, None),
        ),
        check_vma=False,
    )
```

```python
import functools
import math

import jax
import jax.numpy as jnp
import numpy as np
from jax import lax
from jax.experimental import pallas as pl
from jax.experimental.pallas import tpu as pltpu
from jax.sharding import PartitionSpec as P

radius_offset = 0.09
obc_alpha = 1.0
obc_beta = 0.8
obc_gamma = 4.85
cutoff_len = 14.0
cutoff_sq = cutoff_len * cutoff_len

TILES = 32
EDGE = 2
LIVE = TILES + EDGE
HALF = 40
REGION = 2 * HALF
OWN_ROWS = LIVE + 1
SENT_ROWS = 6 * TILES + 8
LISTED = 7
ATOMS = 128
CHUNK = 16
CHUNKS = ATOMS // CHUNK
FULL_WIDTH = 4
PART_WIDTH = 4
FULL_RING = 32
PART_RING = 32
PAIRS = 2 * TILES * LISTED + 6
ITEMS = 512
DUMMY = LIVE * ATOMS + LIVE
ROW = (1, ATOMS)
LANES = (8, ATOMS)
ROWS = (CHUNK, ATOMS)
BLOCK = (ATOMS, ATOMS)
PART = ATOMS // 2
VMEM_LIMIT = 56 * 1024 * 1024
SCALE = math.sqrt(8.0) / cutoff_len
CUT = 8.0
EXP_SCALE = math.sqrt(0.25 / math.log(2.0)) / SCALE

ROW_X, ROW_Y, ROW_Z, ROW_Q, ROW_IN, ROW_SCALED = range(6)
AT_Q, AT_RADIUS, AT_SCALED = 3, 4, 5

F32 = jnp.float32


def fold2(block):
    return block[0:8] + block[8:16]


def fold_own(own):
    flipped = own.T
    total = flipped[0:8]
    for chunk in range(1, ATOMS // 8):
        total = total + flipped[8 * chunk : 8 * chunk + 8]
    return total


def build_beside(build, work, table, fresh_a, fresh_b):
    def keep(tile, fresh, k):
        table[tile] = fresh[k]

    def step(index, carry):
        first = index * 4
        for k in range(2):
            build(first + 2 + k, fresh_b, k)
            work(first + k, fresh_a, k)
        for k in range(2):
            keep(first + k, fresh_a, k)
        for k in range(2):
            build(first + 4 + k, fresh_a, k)
            work(first + 2 + k, fresh_b, k)
        for k in range(2):
            keep(first + 2 + k, fresh_b, k)
        return carry

    for k in range(2):
        build(k, fresh_a, k)
    lax.fori_loop(0, TILES // 4, step, 0)
    for k in range(EDGE):
        keep(TILES + k, fresh_a, k)


def by_fours(step):
    def fours(index, carry):
        start = jnp.minimum(index * 4, LIVE - 4)
        for k in range(4):
            step(start + k)
        return carry

    lax.fori_loop(0, (LIVE + 3) // 4, fours, 0)


def fill_table(table, k, first, ref, tile, rows):
    for slot, row in enumerate(rows):
        table[k, first + slot] = jnp.broadcast_to(ref[tile, row : row + 1, :], BLOCK).T


def fold_rows(fold, width):
    def step(index, carry):
        for k in range(width):
            fold(index * width + k)
        return carry

    lax.fori_loop(0, TILES // width, step, 0)
    for tile in range(TILES, LIVE):
        fold(tile)


def diagonal(start):
    rows = lax.broadcasted_iota(jnp.int32, ROWS, 0) + start
    return jnp.where(rows == lax.broadcasted_iota(jnp.int32, ROWS, 1), 4.0 * CUT, 0.0)


def decode(item):
    return lax.shift_right_logical(item, 7), lax.bitwise_and(item, ATOMS - 1)


def span(start):
    return pl.ds(start if isinstance(start, int) else pl.multiple_of(start, CHUNK), CHUNK)


def part_starts(code):
    return [lax.bitwise_and(lax.shift_right_logical(code, 3 * j), 7) * CHUNK for j in range(CHUNKS // 2)]


def row_of(ref, tile, row):
    return jnp.broadcast_to(ref[tile, row : row + 1, :], ROWS)


def differences(table, tile, rows, far):
    return tuple(table[tile, axis, rows, :] - far[axis] for axis in range(3))


def distance_squared(gaps):
    dx, dy, dz = gaps
    return dx * dx + dy * dy + dz * dz


def half_descreen(r, own, far):
    upper = r + far
    lower = r - far
    inner = jnp.minimum(jnp.maximum(own, lower), upper)
    ratio = upper * pl.reciprocal(inner, approx=True)
    slope = lower * pl.reciprocal(upper, approx=True)
    square = ratio * ratio
    rise = ratio - 1.0
    twice = jnp.log(square)
    value = rise * (2.0 - slope * rise) - twice
    deriv = (twice + twice) - (square - 1.0) * (slope * slope + 1.0)
    return value, deriv


def ring_copies(ring, blocks, sems, size, rows):
    def copy(index, place, inward):
        slot = lax.rem(index, size)
        here = ring.at[slot]
        there = blocks.at[place, :, pl.ds(0, rows), :]
        source, target = (there, here) if inward else (here, there)
        return pltpu.make_async_copy(source, target, sems.at[slot])

    return copy


def edge_rows(values, first):
    rest = jnp.zeros((8 - 2 * EDGE, ATOMS), F32)
    return jnp.concatenate([values[first : first + EDGE], values[HALF + first : HALF + first + EDGE], rest])


def edge_rounds(values, one, two):
    to_next, to_last = edge_rows(values, TILES), edge_rows(values, 0)
    is_even = lax.rem(lax.axis_index("tile"), 2) == 0
    one[...] = jnp.where(is_even, to_next, to_last)
    two[...] = jnp.where(is_even, to_last, to_next)


def pack_kernel(positions, charges, radii, scales, neighbours, pad_mask, sent, edges, here):
    radius = radii[...]
    values = [positions[0], positions[1], positions[2], charges[...], radius, scales[...] * (radius - radius_offset)]
    edges[...] = jnp.zeros_like(edges)
    for index, value in enumerate(values):
        sent[index * TILES : (index + 1) * TILES, :] = value
        edges[EDGE * index : EDGE * (index + 1), :] = value[0:EDGE]
    cycle_count = lax.axis_size("tile")
    cycle_tiles = cycle_count * TILES
    listed = neighbours[...]
    slab_step = lax.div(listed, cycle_tiles) - lax.axis_index("slab")
    within = lax.rem(listed, cycle_tiles)
    cycle_step = lax.rem(lax.div(within, TILES) - lax.axis_index("tile") + cycle_count, cycle_count)
    place = cycle_step * TILES + lax.rem(within, TILES)
    slots = lax.broadcasted_iota(jnp.int32, listed.shape, 0)
    live = (pad_mask[...] == 1) & (slots > 0)
    here[...] = jnp.where(live & (slab_step >= 0), slab_step * HALF + place, -1)
    sent[6 * TILES :, :] = jnp.full(LANES, -1.0, F32)
    sent[6 * TILES :, 0:TILES] = jnp.where(live & (slab_step < 0), place, -1).astype(F32)


def born_kernel(
    items, reach, sent, edges, above, above_edges,
    own_part, above_part, round_one, round_two, data, plain, d_self, d_pair,
    table, fresh_a, fresh_b, own, far, rings, sems,
):
    full_ring, part_ring, self_ring = rings
    full_sems, part_sems, self_sems = sems
    far[...] = jnp.zeros_like(far)
    data[...] = jnp.zeros_like(data)
    plain[...] = jnp.ones_like(plain)
    fulls, parts = items[ITEMS - 2], items[ITEMS - 1]

    for index in range(6):
        origin = sent[index * TILES + TILES // 2 : index * TILES + TILES // 2 + 1, 0:1]
        for start, source, edge in ((0, sent, edges), (HALF, above, above_edges)):
            for place, values in (
                (start, source[index * TILES : (index + 1) * TILES, :]),
                (start + TILES, edge[EDGE * index : EDGE * (index + 1), :]),
            ):
                rows = slice(place, place + values.shape[0])
                if index < AT_Q:
                    data[rows, index, :] = (values - origin) * SCALE
                elif index == AT_Q:
                    data[rows, ROW_Q, :] = values
                    plain[2, rows, :] = values if place == 0 else jnp.zeros_like(values)
                elif index == AT_RADIUS:
                    data[rows, ROW_IN, :] = (values - radius_offset) * SCALE
                    plain[0, rows, :] = values
                    plain[1, rows, :] = values - radius_offset
                else:
                    data[rows, ROW_SCALED, :] = values * SCALE

    def build(tile, fresh, k):
        fill_table(fresh, k, 0, data, tile, (ROW_X, ROW_Y, ROW_Z, ROW_IN, ROW_SCALED))

    for tile in range(TILES, OWN_ROWS):
        own[tile] = jnp.zeros(BLOCK, F32)

    def shared(r2):
        inv = lax.rsqrt(r2)
        cut = jnp.maximum(1.0 - r2 * (1.0 / CUT), 0.0)
        cinv = cut * inv
        return r2 * inv, cut, cinv, cinv * cinv * inv

    def self_pair(tile, fresh, k):
        far_xyz = [row_of(data, tile, axis) for axis in range(3)]
        bs = row_of(data, tile, ROW_SCALED)
        for start in range(0, ATOMS, CHUNK):
            rows = span(start)
            r2 = distance_squared(differences(fresh, k, rows, far_xyz)) + diagonal(start)
            r, cut, cinv, g_deriv = shared(r2)
            value, deriv = half_descreen(r, fresh[k, 3, rows, :], bs)
            value = cinv * value
            own[tile, rows, :] = cut * value
            self_ring[tile, rows, :] = g_deriv * deriv - value

    def self_copy(tile):
        return pltpu.make_async_copy(self_ring.at[tile], d_self.at[tile], self_sems.at[tile])

    def self_step(tile, fresh, k):
        self_pair(tile, fresh, k)
        self_copy(tile).start()

    build_beside(build, self_step, table, fresh_a, fresh_b)

    def pair(item, ring, slot, starts):
        first, second = item
        far_xyz = [row_of(data, second, axis) for axis in range(3)]
        bp, bs = row_of(data, second, ROW_IN), row_of(data, second, ROW_SCALED)
        sums = jnp.zeros(ROWS, F32)
        for place, start in enumerate(starts):
            rows = span(start)
            kept = span(place * CHUNK)
            r2 = distance_squared(differences(table, first, rows, far_xyz))
            r, cut, cinv, g_deriv = shared(r2)
            value, deriv = half_descreen(r, table[first, 3, rows, :], bs)
            value = cinv * value
            own[first, rows, :] += cut * value
            ring[slot, 0, kept, :] = g_deriv * deriv - value
            value, deriv = half_descreen(r, bp, table[first, 4, rows, :])
            value = cinv * value
            ring[slot, 1, kept, :] = g_deriv * deriv - value
            sums = sums + cut * value
        far[second] += fold2(sums)

    def run(width, size, ring, ring_sems, base, number, rows, starts_of):
        copy = ring_copies(ring, d_pair, ring_sems, size, rows)

        def body(index, carry):
            begin = index * width
            for k in range(width):

                @pl.when(begin + k >= size)
                def _():
                    copy(begin + k, base + begin + k, False).wait()

            for k in range(width):
                item = decode(items[base + begin + k])
                pair(item, ring, lax.rem(begin + k, size), starts_of(item))
            for k in range(width):
                copy(begin + k, base + begin + k, False).start()
            return carry

        lax.fori_loop(0, lax.div(number, width), body, 0)

    def drain(size, ring, ring_sems, number, rows):
        copy = ring_copies(ring, d_pair, ring_sems, size, rows)

        def wait(slot, carry):
            copy(slot, slot, False).wait()
            return carry

        lax.fori_loop(0, jnp.minimum(number, size), wait, 0)

    def listed_starts(item):
        return part_starts(reach[item[0], item[1]])

    run(FULL_WIDTH, FULL_RING, full_ring, full_sems, 0, fulls, ATOMS, lambda item: range(0, ATOMS, CHUNK))
    run(PART_WIDTH, PART_RING, part_ring, part_sems, fulls, parts, PART, listed_starts)

    def fold(tile):
        far[tile] += fold_own(own[tile])

    fold_rows(fold, 8)
    sums = jnp.sum(far[...], axis=1) * (0.125 * SCALE)
    own_part[...] = sums[0:HALF]
    above_part[...] = sums[HALF:]
    edge_rounds(sums, round_one, round_two)

    def wait_self(tile, carry):
        self_copy(tile).wait()
        return carry

    lax.fori_loop(0, TILES, wait_self, 0)
    drain(FULL_RING, full_ring, full_sems, fulls, ATOMS)
    drain(PART_RING, part_ring, part_sems, parts, PART)


def energy_kernel(
    items, reach, data, plain, own_part, above_part, from_below, from_above,
    radii_born, slope, own_grad, above_grad, round_one, round_two, force_out,
    table, fresh_a, fresh_b, own, far, born, force,
):
    far[...] = jnp.zeros_like(far)
    force[...] = jnp.zeros_like(force)
    fulls, parts = items[ITEMS - 2], items[ITEMS - 1]
    sums = jnp.concatenate([own_part[...] + from_below[...], above_part[...] + from_above[...]])
    all_radii, all_slopes = born_radius(sums, plain[0], plain[1])
    inverse = 1.0 / all_radii
    radii_born[...] = all_radii[0:TILES]
    slope[...] = all_slopes
    born[:, 0, :] = SCALE * all_radii
    born[:, 1, :] = EXP_SCALE * inverse

    def build(tile, fresh, k):
        fill_table(fresh, k, 0, data, tile, (ROW_X, ROW_Y, ROW_Z, ROW_Q))
        fill_table(fresh, k, 4, born, tile, (0, 1))

    for tile in range(TILES, OWN_ROWS):
        own[tile] = jnp.zeros((4,) + BLOCK, F32)

    def pair(first, second, starts, tables, k, is_self):
        far_xyz = [row_of(data, second, axis) for axis in range(3)]
        br, bi, bq = row_of(born, second, 0), -row_of(born, second, 1), row_of(data, second, ROW_Q)
        sums = [jnp.zeros(ROWS, F32)] * 4
        for start in starts:
            rows = span(start)
            gaps = differences(tables, k, rows, far_xyz)
            r2 = distance_squared(gaps)
            if is_self:
                r2 = r2 + diagonal(start)
            cut = jnp.maximum(1.0 - r2 * (1.0 / CUT), 0.0)
            power = r2 * (tables[k, 5, rows, :] * bi)
            decay = lax.exp2(power)
            screen = (tables[k, 4, rows, :] * br) * decay
            inv = lax.rsqrt(r2 + screen)
            cinv = cut * inv
            lead = (tables[k, 3, rows, :] * bq) * cinv
            square = cinv * inv
            grad = (lead * square) * (screen * (1.0 - math.log(2.0) * power))
            pull = lead * (square * (4.0 - decay) + 16.0 / CUT)
            terms = [grad] + [pull * gap for gap in gaps]
            for which, term in enumerate(terms):
                if is_self:
                    own[first, which, rows, :] = term
                else:
                    own[first, which, rows, :] += term
                    sums[which] = sums[which] + term
        if not is_self:
            far[second] += fold2(sums[0])
            for axis in range(3):
                force[second, axis] -= fold2(sums[1 + axis])

    def self_step(tile, fresh, k):
        pair(tile, tile, range(0, ATOMS, CHUNK), fresh, k, True)

    build_beside(build, self_step, table, fresh_a, fresh_b)

    def full_step(index, carry):
        for k in range(FULL_WIDTH):
            first, second = decode(items[index * FULL_WIDTH + k])
            pair(first, second, range(0, ATOMS, CHUNK), table, first, False)
        return carry

    def part_step(index, carry):
        for k in range(PART_WIDTH):
            first, second = decode(items[fulls + index * PART_WIDTH + k])
            starts = part_starts(reach[first, second])
            pair(first, second, starts, table, first, False)
        return carry

    lax.fori_loop(0, lax.div(fulls, FULL_WIDTH), full_step, 0)
    lax.fori_loop(0, lax.div(parts, PART_WIDTH), part_step, 0)

    def fold(tile):
        far[tile] += fold_own(own[tile, 0])
        for axis in range(3):
            force[tile, axis] += fold_own(own[tile, 1 + axis])

    fold_rows(fold, 4)
    for axis in range(3):
        force_out[axis] = jnp.sum(force[:, axis], axis=1)
    charge = plain[2] * inverse
    sums = jnp.sum(far[...], axis=1) * (0.5 * SCALE) * inverse + 0.5 * charge * charge
    own_grad[...] = sums[0:HALF]
    above_grad[...] = sums[HALF:]
    edge_rounds(sums, round_one, round_two)


def force_kernel(
    items, reach, data, slope, own_grad, above_grad, from_below, from_above, force_in, d_self, d_pair,
    gradient, own_force, above_force, to_next, to_across,
    table, own, far, chain, rings, sems,
):
    full_ring, part_ring, self_ring = rings
    full_sems, part_sems, self_sems = sems
    fulls, parts = items[ITEMS - 2], items[ITEMS - 1]
    full_copy = ring_copies(full_ring, d_pair, full_sems, FULL_RING, ATOMS)
    part_copy = ring_copies(part_ring, d_pair, part_sems, PART_RING, PART)

    self_copy = pltpu.make_async_copy(d_self, self_ring, self_sems.at[0])

    def start(copy, base):
        def step(index, carry):
            copy(index, base + index, True).start()
            return carry

        return step

    self_copy.start()
    lax.fori_loop(0, jnp.minimum(fulls, FULL_RING), start(full_copy, 0), 0)
    lax.fori_loop(0, jnp.minimum(parts, PART_RING), start(part_copy, fulls), 0)

    far[...] = jnp.zeros_like(far)
    grads = jnp.concatenate([own_grad[...] + from_below[...], above_grad[...] + from_above[...]])
    gradient[...] = grads[0:TILES]
    chain[:, 0, :] = grads * slope[...]

    def build(tile):
        fill_table(table, tile, 0, data, tile, (ROW_X, ROW_Y, ROW_Z))
        fill_table(table, tile, 3, chain, tile, (0,))

    by_fours(build)
    for tile in range(TILES, OWN_ROWS):
        own[tile] = jnp.zeros((3,) + BLOCK, F32)

    def pair(first, second, starts, tables, k, pull_of, is_self):
        far_xyz = [row_of(data, second, axis) for axis in range(3)]
        sums = [jnp.zeros(ROWS, F32)] * 3
        for place, start in enumerate(starts):
            rows = span(start)
            pull = pull_of(rows, span(place * CHUNK))
            terms = [pull * gap for gap in differences(tables, k, rows, far_xyz)]
            for which, term in enumerate(terms):
                if is_self:
                    own[first, which, rows, :] = term
                else:
                    own[first, which, rows, :] += term
                sums[which] = sums[which] + term
        for axis in range(3):
            far[second, axis] -= fold2(sums[axis])

    self_copy.wait()

    def self_step(quad, carry):
        begin = quad * 4
        for k in range(4):
            tile = begin + k
            pair(
                tile,
                tile,
                range(0, ATOMS, CHUNK),
                table,
                tile,
                lambda rows, kept: table[tile, 3, rows, :] * self_ring[tile, kept, :],
                True,
            )
        return carry

    lax.fori_loop(0, TILES // 4, self_step, 0)

    def run(width, size, ring, copy, base, number, starts_of):
        def body(index, carry):
            begin = index * width
            for k in range(width):
                copy(begin + k, base + begin + k, True).wait()
            for k in range(width):
                first, second = decode(items[base + begin + k])
                slot = lax.rem(begin + k, size)
                factor = row_of(chain, second, 0)
                pair(
                    first,
                    second,
                    starts_of(first, second),
                    table,
                    first,
                    lambda rows, kept: table[first, 3, rows, :] * ring[slot, 0, kept, :]
                    + factor * ring[slot, 1, kept, :],
                    False,
                )
            for k in range(width):

                @pl.when(begin + k + size < number)
                def _():
                    copy(begin + k + size, base + begin + k + size, True).start()

            return carry

        lax.fori_loop(0, lax.div(number, width), body, 0)

    run(FULL_WIDTH, FULL_RING, full_ring, full_copy, 0, fulls, lambda *_: range(0, ATOMS, CHUNK))
    run(
        PART_WIDTH,
        PART_RING,
        part_ring,
        part_copy,
        fulls,
        parts,
        lambda first, second: part_starts(reach[first, second]),
    )

    def fold(tile):
        for axis in range(3):
            far[tile, axis] += fold_own(own[tile, axis])

    fold_rows(fold, 4)
    for axis in range(3):
        sums = (jnp.sum(far[:, axis], axis=1) + 4.0 * force_in[axis]) * (-SCALE * SCALE / 16.0)
        own_force[axis] = sums[0:TILES]
        above_force[axis] = sums[HALF : HALF + TILES]
        to_next[axis] = sums[TILES : TILES + 8]
        to_across[axis] = sums[HALF + TILES : HALF + TILES + 8]


SMEM = pl.BlockSpec(memory_space=pltpu.SMEM)
VMEM = pl.BlockSpec(memory_space=pltpu.VMEM)
ANY = pl.BlockSpec(memory_space=pl.ANY)
PARAMS = pltpu.CompilerParams(vmem_limit_bytes=VMEM_LIMIT)
RING_BLOCKS = (
    pltpu.VMEM((FULL_RING, 2) + BLOCK, F32),
    pltpu.VMEM((PART_RING, 2, PART, ATOMS), F32),
    pltpu.VMEM((TILES,) + BLOCK, F32),
)
RING_SEMS = (
    pltpu.SemaphoreType.DMA((FULL_RING,)),
    pltpu.SemaphoreType.DMA((PART_RING,)),
    pltpu.SemaphoreType.DMA((TILES,)),
)


def f32(*shape):
    return jax.ShapeDtypeStruct(shape, F32)


def run_pack(positions, charges, radii, scales, neighbours, pad_mask):
    return pl.pallas_call(
        pack_kernel,
        name="pack_atoms",
        out_shape=(
            f32(SENT_ROWS, ATOMS),
            f32(16, ATOMS),
            jax.ShapeDtypeStruct(neighbours.shape, jnp.int32),
        ),
        in_specs=[VMEM] * 6,
        out_specs=(VMEM,) * 3,
        compiler_params=PARAMS,
    )(positions, charges, radii, scales, neighbours, pad_mask)


def run_born(items, reach, sent, edges, above, above_edges):
    return pl.pallas_call(
        born_kernel,
        name="born_sums",
        out_shape=(
            f32(HALF, ATOMS),
            f32(HALF, ATOMS),
            f32(*LANES),
            f32(*LANES),
            f32(REGION, *LANES),
            f32(3, REGION, ATOMS),
            f32(TILES, *BLOCK),
            f32(PAIRS, 2, *BLOCK),
        ),
        in_specs=[SMEM] * 2 + [VMEM] * 4,
        out_specs=(VMEM,) * 6 + (ANY,) * 2,
        scratch_shapes=[
            pltpu.VMEM((OWN_ROWS, 5) + BLOCK, F32),
            pltpu.VMEM((2, 5) + BLOCK, F32),
            pltpu.VMEM((2, 5) + BLOCK, F32),
            pltpu.VMEM((OWN_ROWS,) + BLOCK, F32),
            pltpu.VMEM((REGION,) + LANES, F32),
            RING_BLOCKS,
            RING_SEMS,
        ],
        compiler_params=PARAMS,
    )(items, reach, sent, edges, above, above_edges)


def run_energy(items, reach, data, plain, shares):
    return pl.pallas_call(
        energy_kernel,
        name="radius_gradient",
        out_shape=(
            f32(TILES, ATOMS),
            f32(REGION, ATOMS),
            f32(HALF, ATOMS),
            f32(HALF, ATOMS),
            f32(*LANES),
            f32(*LANES),
            f32(3, REGION, ATOMS),
        ),
        in_specs=[SMEM] * 2 + [VMEM] * 6,
        out_specs=(VMEM,) * 7,
        scratch_shapes=[
            pltpu.VMEM((OWN_ROWS, 6) + BLOCK, F32),
            pltpu.VMEM((2, 6) + BLOCK, F32),
            pltpu.VMEM((2, 6) + BLOCK, F32),
            pltpu.VMEM((OWN_ROWS, 4) + BLOCK, F32),
            pltpu.VMEM((REGION,) + LANES, F32),
            pltpu.VMEM((REGION,) + LANES, F32),
            pltpu.VMEM((REGION, 3) + LANES, F32),
        ],
        compiler_params=PARAMS,
    )(items, reach, data, plain, *shares)


def run_force(items, reach, data, slope, shares, force_in, d_self, d_pair):
    return pl.pallas_call(
        force_kernel,
        name="forces",
        out_shape=(
            f32(TILES, ATOMS),
            f32(3, TILES, ATOMS),
            f32(3, TILES, ATOMS),
            f32(3, *LANES),
            f32(3, *LANES),
        ),
        in_specs=[SMEM] * 2 + [VMEM] * 7 + [ANY] * 2,
        out_specs=(VMEM,) * 5,
        scratch_shapes=[
            pltpu.VMEM((OWN_ROWS, 4) + BLOCK, F32),
            pltpu.VMEM((OWN_ROWS, 3) + BLOCK, F32),
            pltpu.VMEM((REGION, 3) + LANES, F32),
            pltpu.VMEM((REGION,) + LANES, F32),
            RING_BLOCKS,
            RING_SEMS,
        ],
        compiler_params=PARAMS,
    )(items, reach, data, slope, *shares, force_in, d_self, d_pair)


def born_radius(descreen_sum, radius, radius_in):
    scaled = radius_in * descreen_sum
    polynomial = scaled * (obc_alpha + scaled * (-obc_beta + obc_gamma * scaled))
    tangent = jnp.tanh(polynomial)
    radii_born = 1.0 / (1.0 / radius_in - tangent / radius)
    radius_slope = (
        radii_born
        * radii_born
        * (1.0 - tangent * tangent)
        / radius
        * (obc_alpha - 2.0 * obc_beta * scaled + 3.0 * obc_gamma * scaled * scaled)
        * radius_in
    )
    return (radii_born, radius_slope)


def above_to_here(block):
    ends = lax.axis_size("slab") - 1
    return lax.ppermute(block, "slab", [(i + 1, i) for i in range(ends)])


def here_to_above(block):
    ends = lax.axis_size("slab") - 1
    return lax.ppermute(block, "slab", [(i, i + 1) for i in range(ends)])


def next_to_here(block):
    count = lax.axis_size("tile")
    return lax.ppermute(block, "tile", [((i + 1) % count, i) for i in range(count)])


def here_to_next(block):
    count = lax.axis_size("tile")
    return lax.ppermute(block, "tile", [(i, (i + 1) % count) for i in range(count)])


def pairwise(block, last):
    count = lax.axis_size("tile")
    pairs = [(i, (i + (-1 if (i % 2 == 0) == last else 1)) % count) for i in range(count)]
    return lax.ppermute(block, "tile", pairs)


def across_to_here(block):
    slabs, count = lax.axis_size("slab"), lax.axis_size("tile")
    pairs = [
        ((slab + 1) * count + (tile + 1) % count, slab * count + tile)
        for slab in range(slabs - 1)
        for tile in range(count)
    ]
    return lax.ppermute(block, ("slab", "tile"), pairs)


def placed(block, first, last):
    return jnp.pad(block[first : first + EDGE], ((0, HALF - EDGE), (0, 0))) + jnp.pad(
        last[first : first + EDGE], ((TILES, HALF - LIVE), (0, 0))
    )


def swap_sums(own, above, round_one, round_two):
    one, two = pairwise(round_one, False), pairwise(round_two, True)
    is_even = lax.axis_index("tile") % 2 == 0
    from_next, from_last = jnp.where(is_even, one, two), jnp.where(is_even, two, one)
    own = own + placed(from_last, 0, from_next)
    above = above + placed(from_last, EDGE, from_next)
    own, above = lax.optimization_barrier((own, above))
    return own, above, here_to_above(above), above_to_here(own)


def here_to_across(block):
    slabs, count = lax.axis_size("slab"), lax.axis_size("tile")
    pairs = [
        (slab * count + tile, (slab + 1) * count + (tile + 1) % count)
        for slab in range(slabs - 1)
        for tile in range(count)
    ]
    return lax.ppermute(block, ("slab", "tile"), pairs)


def slab_boxes(block, edges, across, along):
    rows = [
        jnp.concatenate(
            [
                block[axis * TILES : (axis + 1) * TILES],
                edges[axis * EDGE : (axis + 1) * EDGE],
                jnp.zeros((HALF - LIVE, ATOMS), F32),
            ]
        )
        for axis in range(3)
    ]
    x, y, z = rows
    pieces = jnp.stack([x * across + y * along, y * across - x * along, z]).reshape(3, HALF, CHUNKS, CHUNK)
    low, high = jnp.min(pieces, axis=3), jnp.max(pieces, axis=3)
    return low, high, jnp.min(low, axis=2), jnp.max(high, axis=2)


def chunk_codes(low, high, tile_low, tile_high):
    near = []
    for chunk in range(CHUNKS):
        own_low, own_high = low[:, :OWN_ROWS, chunk, None], high[:, :OWN_ROWS, chunk, None]
        gap = jnp.maximum(jnp.maximum(tile_low[:, None, :] - own_high, own_low - tile_high[:, None, :]), 0.0)
        far = jnp.sum(gap * gap, axis=0) >= cutoff_sq * 1.001
        near.append(jnp.logical_not(far).astype(jnp.int32))
    number = sum(near)
    code = number << (3 * CHUNKS)
    before = jnp.zeros_like(number)
    for chunk in range(CHUNKS):
        rank = jnp.where(near[chunk] == 1, before, number + chunk - before)
        code = code + (chunk << (3 * rank))
        before = before + near[chunk]
    return code


def chunk_reach(sent, edges, above, above_edges):
    across, along = sent[TILES // 2, 0], sent[TILES + TILES // 2, 0]
    inverse = lax.rsqrt(across * across + along * along)
    across, along = across * inverse, along * inverse
    low, high, *tile = slab_boxes(sent, edges, across, along)
    *_, above_low, above_high = slab_boxes(above, above_edges, across, along)
    own_codes = chunk_codes(low, high, *tile)
    code = jnp.concatenate([own_codes, chunk_codes(low, high, above_low, above_high)], axis=1)
    return code, (code >> (3 * CHUNKS)) <= CHUNKS // 2


def packed(first, second, valid, is_part):
    first, second, valid = first.reshape(-1), second.reshape(-1), valid.reshape(-1)
    mine = (first[:, None] == jnp.arange(OWN_ROWS)[None, :]).astype(jnp.bfloat16)
    rows = jnp.dot(mine, is_part.astype(jnp.bfloat16), preferred_element_type=F32)
    in_part = jnp.sum(jnp.where(second[:, None] == jnp.arange(REGION)[None, :], rows, 0.0), axis=1) > 0.5
    entry = jnp.arange(valid.shape[0])
    ahead = valid[None, :] & (entry[None, :] < entry[:, None]) & (in_part[None, :] == in_part[:, None])
    rank = jnp.sum(ahead, axis=1)
    fulls = jnp.sum(valid & jnp.logical_not(in_part), dtype=jnp.int32)
    parts = jnp.sum(valid & in_part, dtype=jnp.int32)
    fulls = (fulls + FULL_WIDTH - 1) // FULL_WIDTH * FULL_WIDTH
    parts = (parts + PART_WIDTH - 1) // PART_WIDTH * PART_WIDTH
    rank = jnp.where(in_part, fulls + rank, rank)
    chosen = valid[None, :] & (rank[None, :] == jnp.arange(ITEMS)[:, None])
    value = first * ATOMS + second - DUMMY
    items = DUMMY + jnp.sum(jnp.where(chosen, value[None, :], 0), axis=1)
    slot = jnp.arange(ITEMS)
    items = jnp.where(slot == ITEMS - 2, fulls, jnp.where(slot == ITEMS - 1, parts, items))
    return items.astype(jnp.int32)


def pair_items(here, above, is_part):
    listed = above[6 * TILES :, 0:TILES].astype(jnp.int32)
    has_above = lax.axis_index("slab") < lax.axis_size("slab") - 1
    tiles = lax.broadcasted_iota(jnp.int32, here.shape, 1)
    return packed(
        jnp.concatenate([tiles, listed]),
        jnp.concatenate([here, HALF + tiles]),
        jnp.concatenate([here >= 0, (listed >= 0) & has_above]),
        is_part,
    )


def body(positions, charges, radii, scales, neighbours, pad_mask):
    sent, edges, here = run_pack(
        jnp.swapaxes(positions[0, 0], 0, 1),
        charges[0, 0],
        radii[0, 0],
        scales[0, 0],
        neighbours[0, 0].T,
        pad_mask[0, 0].T,
    )
    above = above_to_here(sent)
    next_edges = next_to_here(edges)
    above_edges = across_to_here(edges)
    reach, is_part = chunk_reach(sent, next_edges, above, above_edges)
    items = pair_items(here, above, is_part)

    *parts, data, plain, d_self, d_pair = run_born(items, reach, sent, next_edges, above, above_edges)
    shares = swap_sums(*parts)
    radii_born, slope, *parts, force = run_energy(items, reach, data, plain, shares)
    shares = swap_sums(*parts)
    gradient, own, over, to_next, to_across = run_force(
        items, reach, data, slope, shares, force, d_self, d_pair
    )
    forces, to_next, to_across = lax.optimization_barrier(
        (own + here_to_above(over), here_to_next(to_next), here_to_across(to_across))
    )
    forces = forces + jnp.pad((to_next + to_across)[:, 0:EDGE], ((0, 0), (0, TILES - EDGE), (0, 0)))
    return (radii_born[None, None], gradient[None, None], jnp.swapaxes(forces, 0, 1)[None, None])


def solution(mesh):
    return jax.shard_map(
        body,
        mesh=mesh,
        in_specs=(
            P("slab", "tile", None, None, None),
            P("slab", "tile", None, None),
            P("slab", "tile", None, None),
            P("slab", "tile", None, None),
            P("slab", "tile", None, None),
            P("slab", "tile", None, None),
        ),
        out_specs=(
            P("slab", "tile", None, None),
            P("slab", "tile", None, None),
            P("slab", "tile", None, None, None),
        ),
        check_vma=False,
    )
```

```python
import functools
import math

import jax
import jax.numpy as jnp
import numpy as np
from jax import lax
from jax.experimental import pallas as pl
from jax.experimental.pallas import tpu as pltpu
from jax.sharding import PartitionSpec as P

radius_offset = 0.09
obc_alpha = 1.0
obc_beta = 0.8
obc_gamma = 4.85
cutoff_len = 14.0
cutoff_sq = cutoff_len * cutoff_len

TILES = 32
EDGE = 2
LIVE = TILES + EDGE
HALF = 40
REGION = 2 * HALF
OWN_ROWS = LIVE + 1
SENT_ROWS = 6 * TILES + 8
LISTED = 7
ATOMS = 128
CHUNK = 16
CHUNKS = ATOMS // CHUNK
FULL_WIDTH = 4
PART_WIDTH = 4
FULL_RING = 32
PART_RING = 32
PAIRS = 2 * TILES * LISTED + 6
ITEMS = 512
DUMMY = LIVE * ATOMS + LIVE
ROW = (1, ATOMS)
LANES = (8, ATOMS)
ROWS = (CHUNK, ATOMS)
BLOCK = (ATOMS, ATOMS)
PART = ATOMS // 2
VMEM_LIMIT = 56 * 1024 * 1024
SCALE = math.sqrt(8.0) / cutoff_len
CUT = 8.0
EXP_SCALE = math.sqrt(0.25 / math.log(2.0)) / SCALE

ROW_X, ROW_Y, ROW_Z, ROW_Q, ROW_IN, ROW_SCALED = range(6)
AT_Q, AT_RADIUS, AT_SCALED = 3, 4, 5

F32 = jnp.float32


def fold2(block):
    return block[0:8] + block[8:16]


def fold_own(own):
    flipped = own.T
    total = flipped[0:8]
    for chunk in range(1, ATOMS // 8):
        total = total + flipped[8 * chunk : 8 * chunk + 8]
    return total


def build_beside(build, work, table, fresh_a, fresh_b):
    def keep(tile, fresh, k):
        table[tile] = fresh[k]

    def step(index, carry):
        first = index * 4
        for k in range(2):
            build(first + 2 + k, fresh_b, k)
            work(first + k, fresh_a, k)
        for k in range(2):
            keep(first + k, fresh_a, k)
        for k in range(2):
            build(first + 4 + k, fresh_a, k)
            work(first + 2 + k, fresh_b, k)
        for k in range(2):
            keep(first + 2 + k, fresh_b, k)
        return carry

    for k in range(2):
        build(k, fresh_a, k)
    lax.fori_loop(0, TILES // 4, step, 0)
    for k in range(EDGE):
        keep(TILES + k, fresh_a, k)


def by_fours(step):
    def fours(index, carry):
        start = jnp.minimum(index * 4, LIVE - 4)
        for k in range(4):
            step(start + k)
        return carry

    lax.fori_loop(0, (LIVE + 3) // 4, fours, 0)


def fill_table(table, k, first, ref, tile, rows):
    for slot, row in enumerate(rows):
        table[k, first + slot] = jnp.broadcast_to(ref[tile, row : row + 1, :], BLOCK).T


def fold_rows(fold, width):
    def step(index, carry):
        for k in range(width):
            fold(index * width + k)
        return carry

    lax.fori_loop(0, TILES // width, step, 0)
    for tile in range(TILES, LIVE):
        fold(tile)


def diagonal(start):
    rows = lax.broadcasted_iota(jnp.int32, ROWS, 0) + start
    return jnp.where(rows == lax.broadcasted_iota(jnp.int32, ROWS, 1), 4.0 * CUT, 0.0)


def decode(item):
    return lax.shift_right_logical(item, 7), lax.bitwise_and(item, ATOMS - 1)


def span(start):
    return pl.ds(start if isinstance(start, int) else pl.multiple_of(start, CHUNK), CHUNK)


def part_starts(code):
    return [lax.bitwise_and(lax.shift_right_logical(code, 3 * j), 7) * CHUNK for j in range(CHUNKS // 2)]


def row_of(ref, tile, row):
    return jnp.broadcast_to(ref[tile, row : row + 1, :], ROWS)


def differences(table, tile, rows, far):
    return tuple(table[tile, axis, rows, :] - far[axis] for axis in range(3))


def distance_squared(gaps):
    dx, dy, dz = gaps
    return dx * dx + dy * dy + dz * dz


def half_descreen(r, own, far):
    upper = r + far
    lower = r - far
    inner = jnp.minimum(jnp.maximum(own, lower), upper)
    ratio = upper * pl.reciprocal(inner, approx=True)
    slope = lower * pl.reciprocal(upper, approx=True)
    square = ratio * ratio
    rise = ratio - 1.0
    twice = jnp.log(square)
    value = rise * (2.0 - slope * rise) - twice
    deriv = (twice + twice) - (square - 1.0) * (slope * slope + 1.0)
    return value, deriv


def ring_copies(ring, blocks, sems, size, rows):
    def copy(index, place, inward):
        slot = lax.rem(index, size)
        here = ring.at[slot]
        there = blocks.at[place, :, pl.ds(0, rows), :]
        source, target = (there, here) if inward else (here, there)
        return pltpu.make_async_copy(source, target, sems.at[slot])

    return copy


def edge_rows(values, first):
    rest = jnp.zeros((8 - 2 * EDGE, ATOMS), F32)
    return jnp.concatenate([values[first : first + EDGE], values[HALF + first : HALF + first + EDGE], rest])


def edge_rounds(values, one, two):
    to_next, to_last = edge_rows(values, TILES), edge_rows(values, 0)
    is_even = lax.rem(lax.axis_index("tile"), 2) == 0
    one[...] = jnp.where(is_even, to_next, to_last)
    two[...] = jnp.where(is_even, to_last, to_next)


def pack_kernel(positions, charges, radii, scales, neighbours, pad_mask, sent, edges, here):
    radius = radii[...]
    values = [positions[0], positions[1], positions[2], charges[...], radius, scales[...] * (radius - radius_offset)]
    edges[...] = jnp.zeros_like(edges)
    for index, value in enumerate(values):
        sent[index * TILES : (index + 1) * TILES, :] = value
        edges[EDGE * index : EDGE * (index + 1), :] = value[0:EDGE]
    cycle_count = lax.axis_size("tile")
    cycle_tiles = cycle_count * TILES
    listed = neighbours[...]
    slab_step = lax.div(listed, cycle_tiles) - lax.axis_index("slab")
    within = lax.rem(listed, cycle_tiles)
    cycle_step = lax.rem(lax.div(within, TILES) - lax.axis_index("tile") + cycle_count, cycle_count)
    place = cycle_step * TILES + lax.rem(within, TILES)
    slots = lax.broadcasted_iota(jnp.int32, listed.shape, 0)
    live = (pad_mask[...] == 1) & (slots > 0)
    here[...] = jnp.where(live & (slab_step >= 0), slab_step * HALF + place, -1)
    sent[6 * TILES :, :] = jnp.full(LANES, -1.0, F32)
    sent[6 * TILES :, 0:TILES] = jnp.where(live & (slab_step < 0), place, -1).astype(F32)


def born_kernel(
    items, reach, sent, edges, above, above_edges,
    own_part, above_part, round_one, round_two, data, plain, d_self, d_pair,
    table, fresh_a, fresh_b, own, far, rings, sems,
):
    full_ring, part_ring, self_ring = rings
    full_sems, part_sems, self_sems = sems
    far[...] = jnp.zeros_like(far)
    data[...] = jnp.zeros_like(data)
    plain[...] = jnp.ones_like(plain)
    fulls, parts = items[ITEMS - 2], items[ITEMS - 1]

    for index in range(6):
        origin = sent[index * TILES + TILES // 2 : index * TILES + TILES // 2 + 1, 0:1]
        for start, source, edge in ((0, sent, edges), (HALF, above, above_edges)):
            for place, values in (
                (start, source[index * TILES : (index + 1) * TILES, :]),
                (start + TILES, edge[EDGE * index : EDGE * (index + 1), :]),
            ):
                rows = slice(place, place + values.shape[0])
                if index < AT_Q:
                    data[rows, index, :] = (values - origin) * SCALE
                elif index == AT_Q:
                    data[rows, ROW_Q, :] = values
                    plain[2, rows, :] = values if place == 0 else jnp.zeros_like(values)
                elif index == AT_RADIUS:
                    data[rows, ROW_IN, :] = (values - radius_offset) * SCALE
                    plain[0, rows, :] = values
                    plain[1, rows, :] = values - radius_offset
                else:
                    data[rows, ROW_SCALED, :] = values * SCALE

    def build(tile, fresh, k):
        fill_table(fresh, k, 0, data, tile, (ROW_X, ROW_Y, ROW_Z, ROW_IN, ROW_SCALED))

    for tile in range(TILES, OWN_ROWS):
        own[tile] = jnp.zeros(BLOCK, F32)

    def shared(r2):
        inv = lax.rsqrt(r2)
        cut = jnp.maximum(1.0 - r2 * (1.0 / CUT), 0.0)
        cinv = cut * inv
        return r2 * inv, cut, cinv, cinv * cinv * inv

    def self_pair(tile, fresh, k):
        far_xyz = [row_of(data, tile, axis) for axis in range(3)]
        bs = row_of(data, tile, ROW_SCALED)
        for start in range(0, ATOMS, CHUNK):
            rows = span(start)
            r2 = distance_squared(differences(fresh, k, rows, far_xyz)) + diagonal(start)
            r, cut, cinv, g_deriv = shared(r2)
            value, deriv = half_descreen(r, fresh[k, 3, rows, :], bs)
            value = cinv * value
            own[tile, rows, :] = cut * value
            self_ring[tile, rows, :] = g_deriv * deriv - value

    def self_copy(tile):
        return pltpu.make_async_copy(self_ring.at[tile], d_self.at[tile], self_sems.at[tile])

    def self_step(tile, fresh, k):
        self_pair(tile, fresh, k)
        self_copy(tile).start()

    build_beside(build, self_step, table, fresh_a, fresh_b)

    def pair(item, ring, slot, starts):
        first, second = item
        far_xyz = [row_of(data, second, axis) for axis in range(3)]
        bp, bs = row_of(data, second, ROW_IN), row_of(data, second, ROW_SCALED)
        sums = jnp.zeros(ROWS, F32)
        for place, start in enumerate(starts):
            rows = span(start)
            kept = span(place * CHUNK)
            r2 = distance_squared(differences(table, first, rows, far_xyz))
            r, cut, cinv, g_deriv = shared(r2)
            value, deriv = half_descreen(r, table[first, 3, rows, :], bs)
            value = cinv * value
            own[first, rows, :] += cut * value
            ring[slot, 0, kept, :] = g_deriv * deriv - value
            value, deriv = half_descreen(r, bp, table[first, 4, rows, :])
            value = cinv * value
            ring[slot, 1, kept, :] = g_deriv * deriv - value
            sums = sums + cut * value
        far[second] += fold2(sums)

    def run(width, size, ring, ring_sems, base, number, rows, starts_of):
        copy = ring_copies(ring, d_pair, ring_sems, size, rows)

        def body(index, carry):
            begin = index * width
            for k in range(width):

                @pl.when(begin + k >= size)
                def _():
                    copy(begin + k, base + begin + k, False).wait()

            for k in range(width):
                item = decode(items[base + begin + k])
                pair(item, ring, lax.rem(begin + k, size), starts_of(item))
            for k in range(width):
                copy(begin + k, base + begin + k, False).start()
            return carry

        lax.fori_loop(0, lax.div(number, width), body, 0)

    def drain(size, ring, ring_sems, number, rows):
        copy = ring_copies(ring, d_pair, ring_sems, size, rows)

        def wait(slot, carry):
            copy(slot, slot, False).wait()
            return carry

        lax.fori_loop(0, jnp.minimum(number, size), wait, 0)

    def listed_starts(item):
        return part_starts(reach[item[0], item[1]])

    run(FULL_WIDTH, FULL_RING, full_ring, full_sems, 0, fulls, ATOMS, lambda item: range(0, ATOMS, CHUNK))
    run(PART_WIDTH, PART_RING, part_ring, part_sems, fulls, parts, PART, listed_starts)

    def fold(tile):
        far[tile] += fold_own(own[tile])

    fold_rows(fold, 8)
    sums = jnp.sum(far[...], axis=1) * (0.125 * SCALE)
    own_part[...] = sums[0:HALF]
    above_part[...] = sums[HALF:]
    edge_rounds(sums, round_one, round_two)

    def wait_self(tile, carry):
        self_copy(tile).wait()
        return carry

    lax.fori_loop(0, TILES, wait_self, 0)
    drain(FULL_RING, full_ring, full_sems, fulls, ATOMS)
    drain(PART_RING, part_ring, part_sems, parts, PART)


def energy_kernel(
    items, reach, data, plain, own_part, above_part, from_below, from_above,
    radii_born, slope, own_grad, above_grad, round_one, round_two, force_out,
    table, fresh_a, fresh_b, own, far, born, force,
):
    far[...] = jnp.zeros_like(far)
    force[...] = jnp.zeros_like(force)
    fulls, parts = items[ITEMS - 2], items[ITEMS - 1]
    sums = jnp.concatenate([own_part[...] + from_below[...], above_part[...] + from_above[...]])
    all_radii, all_slopes = born_radius(sums, plain[0], plain[1])
    inverse = 1.0 / all_radii
    radii_born[...] = all_radii[0:TILES]
    slope[...] = all_slopes
    born[:, 0, :] = SCALE * all_radii
    born[:, 1, :] = EXP_SCALE * inverse

    def build(tile, fresh, k):
        fill_table(fresh, k, 0, data, tile, (ROW_X, ROW_Y, ROW_Z, ROW_Q))
        fill_table(fresh, k, 4, born, tile, (0, 1))

    for tile in range(TILES, OWN_ROWS):
        own[tile] = jnp.zeros((4,) + BLOCK, F32)

    def pair(first, second, starts, tables, k, is_self):
        far_xyz = [row_of(data, second, axis) for axis in range(3)]
        br, bi, bq = row_of(born, second, 0), -row_of(born, second, 1), row_of(data, second, ROW_Q)
        sums = [jnp.zeros(ROWS, F32)] * 4
        for start in starts:
            rows = span(start)
            gaps = differences(tables, k, rows, far_xyz)
            r2 = distance_squared(gaps)
            if is_self:
                r2 = r2 + diagonal(start)
            cut = jnp.maximum(1.0 - r2 * (1.0 / CUT), 0.0)
            power = r2 * (tables[k, 5, rows, :] * bi)
            decay = lax.exp2(power)
            screen = (tables[k, 4, rows, :] * br) * decay
            inv = lax.rsqrt(r2 + screen)
            cinv = cut * inv
            lead = (tables[k, 3, rows, :] * bq) * cinv
            square = cinv * inv
            grad = (lead * square) * (screen * (1.0 - math.log(2.0) * power))
            pull = lead * (square * (4.0 - decay) + 16.0 / CUT)
            terms = [grad] + [pull * gap for gap in gaps]
            for which, term in enumerate(terms):
                if is_self:
                    own[first, which, rows, :] = term
                else:
                    own[first, which, rows, :] += term
                    sums[which] = sums[which] + term
        if not is_self:
            far[second] += fold2(sums[0])
            for axis in range(3):
                force[second, axis] -= fold2(sums[1 + axis])

    def self_step(tile, fresh, k):
        pair(tile, tile, range(0, ATOMS, CHUNK), fresh, k, True)

    build_beside(build, self_step, table, fresh_a, fresh_b)

    def full_step(index, carry):
        for k in range(FULL_WIDTH):
            first, second = decode(items[index * FULL_WIDTH + k])
            pair(first, second, range(0, ATOMS, CHUNK), table, first, False)
        return carry

    def part_step(index, carry):
        for k in range(PART_WIDTH):
            first, second = decode(items[fulls + index * PART_WIDTH + k])
            starts = part_starts(reach[first, second])
            pair(first, second, starts, table, first, False)
        return carry

    lax.fori_loop(0, lax.div(fulls, FULL_WIDTH), full_step, 0)
    lax.fori_loop(0, lax.div(parts, PART_WIDTH), part_step, 0)

    def fold(tile):
        far[tile] += fold_own(own[tile, 0])
        for axis in range(3):
            force[tile, axis] += fold_own(own[tile, 1 + axis])

    fold_rows(fold, 4)
    for axis in range(3):
        force_out[axis] = jnp.sum(force[:, axis], axis=1)
    charge = plain[2] * inverse
    sums = jnp.sum(far[...], axis=1) * (0.5 * SCALE) * inverse + 0.5 * charge * charge
    own_grad[...] = sums[0:HALF]
    above_grad[...] = sums[HALF:]
    edge_rounds(sums, round_one, round_two)


def force_kernel(
    items, reach, data, slope, own_grad, above_grad, from_below, from_above, force_in, d_self, d_pair,
    gradient, own_force, above_force, to_next, to_across,
    table, own, far, chain, rings, sems,
):
    full_ring, part_ring, self_ring = rings
    full_sems, part_sems, self_sems = sems
    fulls, parts = items[ITEMS - 2], items[ITEMS - 1]
    full_copy = ring_copies(full_ring, d_pair, full_sems, FULL_RING, ATOMS)
    part_copy = ring_copies(part_ring, d_pair, part_sems, PART_RING, PART)

    self_copy = pltpu.make_async_copy(d_self, self_ring, self_sems.at[0])

    def start(copy, base):
        def step(index, carry):
            copy(index, base + index, True).start()
            return carry

        return step

    self_copy.start()
    lax.fori_loop(0, jnp.minimum(fulls, FULL_RING), start(full_copy, 0), 0)
    lax.fori_loop(0, jnp.minimum(parts, PART_RING), start(part_copy, fulls), 0)

    far[...] = jnp.zeros_like(far)
    grads = jnp.concatenate([own_grad[...] + from_below[...], above_grad[...] + from_above[...]])
    gradient[...] = grads[0:TILES]
    chain[:, 0, :] = grads * slope[...]

    def build(tile):
        fill_table(table, tile, 0, data, tile, (ROW_X, ROW_Y, ROW_Z))
        fill_table(table, tile, 3, chain, tile, (0,))

    by_fours(build)
    for tile in range(TILES, OWN_ROWS):
        own[tile] = jnp.zeros((3,) + BLOCK, F32)

    def pair(first, second, starts, tables, k, pull_of, is_self):
        far_xyz = [row_of(data, second, axis) for axis in range(3)]
        sums = [jnp.zeros(ROWS, F32)] * 3
        for place, start in enumerate(starts):
            rows = span(start)
            pull = pull_of(rows, span(place * CHUNK))
            terms = [pull * gap for gap in differences(tables, k, rows, far_xyz)]
            for which, term in enumerate(terms):
                if is_self:
                    own[first, which, rows, :] = term
                else:
                    own[first, which, rows, :] += term
                sums[which] = sums[which] + term
        for axis in range(3):
            far[second, axis] -= fold2(sums[axis])

    self_copy.wait()

    def self_step(quad, carry):
        begin = quad * 4
        for k in range(4):
            tile = begin + k
            pair(
                tile,
                tile,
                range(0, ATOMS, CHUNK),
                table,
                tile,
                lambda rows, kept: table[tile, 3, rows, :] * self_ring[tile, kept, :],
                True,
            )
        return carry

    lax.fori_loop(0, TILES // 4, self_step, 0)

    def run(width, size, ring, copy, base, number, starts_of):
        def body(index, carry):
            begin = index * width
            for k in range(width):
                copy(begin + k, base + begin + k, True).wait()
            for k in range(width):
                first, second = decode(items[base + begin + k])
                slot = lax.rem(begin + k, size)
                factor = row_of(chain, second, 0)
                pair(
                    first,
                    second,
                    starts_of(first, second),
                    table,
                    first,
                    lambda rows, kept: table[first, 3, rows, :] * ring[slot, 0, kept, :]
                    + factor * ring[slot, 1, kept, :],
                    False,
                )
            for k in range(width):

                @pl.when(begin + k + size < number)
                def _():
                    copy(begin + k + size, base + begin + k + size, True).start()

            return carry

        lax.fori_loop(0, lax.div(number, width), body, 0)

    run(FULL_WIDTH, FULL_RING, full_ring, full_copy, 0, fulls, lambda *_: range(0, ATOMS, CHUNK))
    run(
        PART_WIDTH,
        PART_RING,
        part_ring,
        part_copy,
        fulls,
        parts,
        lambda first, second: part_starts(reach[first, second]),
    )

    def fold(tile):
        for axis in range(3):
            far[tile, axis] += fold_own(own[tile, axis])

    fold_rows(fold, 4)
    for axis in range(3):
        sums = (jnp.sum(far[:, axis], axis=1) + 4.0 * force_in[axis]) * (-SCALE * SCALE / 16.0)
        own_force[axis] = sums[0:TILES]
        above_force[axis] = sums[HALF : HALF + TILES]
        to_next[axis] = sums[TILES : TILES + 8]
        to_across[axis] = sums[HALF + TILES : HALF + TILES + 8]


SMEM = pl.BlockSpec(memory_space=pltpu.SMEM)
VMEM = pl.BlockSpec(memory_space=pltpu.VMEM)
ANY = pl.BlockSpec(memory_space=pl.ANY)
PARAMS = pltpu.CompilerParams(vmem_limit_bytes=VMEM_LIMIT)
RING_BLOCKS = (
    pltpu.VMEM((FULL_RING, 2) + BLOCK, F32),
    pltpu.VMEM((PART_RING, 2, PART, ATOMS), F32),
    pltpu.VMEM((TILES,) + BLOCK, F32),
)
RING_SEMS = (
    pltpu.SemaphoreType.DMA((FULL_RING,)),
    pltpu.SemaphoreType.DMA((PART_RING,)),
    pltpu.SemaphoreType.DMA((TILES,)),
)


def f32(*shape):
    return jax.ShapeDtypeStruct(shape, F32)


def run_pack(positions, charges, radii, scales, neighbours, pad_mask):
    return pl.pallas_call(
        pack_kernel,
        name="pack_atoms",
        out_shape=(
            f32(SENT_ROWS, ATOMS),
            f32(16, ATOMS),
            jax.ShapeDtypeStruct(neighbours.shape, jnp.int32),
        ),
        in_specs=[VMEM] * 6,
        out_specs=(VMEM,) * 3,
        compiler_params=PARAMS,
    )(positions, charges, radii, scales, neighbours, pad_mask)


def merge_kernel(own, above, one, two, own_out, above_out):
    is_even = lax.rem(lax.axis_index("tile"), 2) == 0
    from_next = jnp.where(is_even, one[...], two[...])
    from_last = jnp.where(is_even, two[...], one[...])
    for place, (source, target) in enumerate(((own, own_out), (above, above_out))):
        rows = slice(place * EDGE, (place + 1) * EDGE)
        target[...] = source[...]
        target[0:EDGE, :] = source[0:EDGE, :] + from_last[rows]
        target[TILES:LIVE, :] = source[TILES:LIVE, :] + from_next[rows]


def run_merge(own, above, one, two):
    return pl.pallas_call(
        merge_kernel,
        name="merge_edges",
        out_shape=(f32(HALF, ATOMS),) * 2,
        in_specs=[VMEM] * 4,
        out_specs=(VMEM,) * 2,
        compiler_params=PARAMS,
    )(own, above, one, two)


def run_born(items, reach, sent, edges, above, above_edges):
    return pl.pallas_call(
        born_kernel,
        name="born_sums",
        out_shape=(
            f32(HALF, ATOMS),
            f32(HALF, ATOMS),
            f32(*LANES),
            f32(*LANES),
            f32(REGION, *LANES),
            f32(3, REGION, ATOMS),
            f32(TILES, *BLOCK),
            f32(PAIRS, 2, *BLOCK),
        ),
        in_specs=[SMEM] * 2 + [VMEM] * 4,
        out_specs=(VMEM,) * 6 + (ANY,) * 2,
        scratch_shapes=[
            pltpu.VMEM((OWN_ROWS, 5) + BLOCK, F32),
            pltpu.VMEM((2, 5) + BLOCK, F32),
            pltpu.VMEM((2, 5) + BLOCK, F32),
            pltpu.VMEM((OWN_ROWS,) + BLOCK, F32),
            pltpu.VMEM((REGION,) + LANES, F32),
            RING_BLOCKS,
            RING_SEMS,
        ],
        compiler_params=PARAMS,
    )(items, reach, sent, edges, above, above_edges)


def run_energy(items, reach, data, plain, shares):
    return pl.pallas_call(
        energy_kernel,
        name="radius_gradient",
        out_shape=(
            f32(TILES, ATOMS),
            f32(REGION, ATOMS),
            f32(HALF, ATOMS),
            f32(HALF, ATOMS),
            f32(*LANES),
            f32(*LANES),
            f32(3, REGION, ATOMS),
        ),
        in_specs=[SMEM] * 2 + [VMEM] * 6,
        out_specs=(VMEM,) * 7,
        scratch_shapes=[
            pltpu.VMEM((OWN_ROWS, 6) + BLOCK, F32),
            pltpu.VMEM((2, 6) + BLOCK, F32),
            pltpu.VMEM((2, 6) + BLOCK, F32),
            pltpu.VMEM((OWN_ROWS, 4) + BLOCK, F32),
            pltpu.VMEM((REGION,) + LANES, F32),
            pltpu.VMEM((REGION,) + LANES, F32),
            pltpu.VMEM((REGION, 3) + LANES, F32),
        ],
        compiler_params=PARAMS,
    )(items, reach, data, plain, *shares)


def run_force(items, reach, data, slope, shares, force_in, d_self, d_pair):
    return pl.pallas_call(
        force_kernel,
        name="forces",
        out_shape=(
            f32(TILES, ATOMS),
            f32(3, TILES, ATOMS),
            f32(3, TILES, ATOMS),
            f32(3, *LANES),
            f32(3, *LANES),
        ),
        in_specs=[SMEM] * 2 + [VMEM] * 7 + [ANY] * 2,
        out_specs=(VMEM,) * 5,
        scratch_shapes=[
            pltpu.VMEM((OWN_ROWS, 4) + BLOCK, F32),
            pltpu.VMEM((OWN_ROWS, 3) + BLOCK, F32),
            pltpu.VMEM((REGION, 3) + LANES, F32),
            pltpu.VMEM((REGION,) + LANES, F32),
            RING_BLOCKS,
            RING_SEMS,
        ],
        compiler_params=PARAMS,
    )(items, reach, data, slope, *shares, force_in, d_self, d_pair)


def born_radius(descreen_sum, radius, radius_in):
    scaled = radius_in * descreen_sum
    polynomial = scaled * (obc_alpha + scaled * (-obc_beta + obc_gamma * scaled))
    tangent = jnp.tanh(polynomial)
    radii_born = 1.0 / (1.0 / radius_in - tangent / radius)
    radius_slope = (
        radii_born
        * radii_born
        * (1.0 - tangent * tangent)
        / radius
        * (obc_alpha - 2.0 * obc_beta * scaled + 3.0 * obc_gamma * scaled * scaled)
        * radius_in
    )
    return (radii_born, radius_slope)


def above_to_here(block):
    ends = lax.axis_size("slab") - 1
    return lax.ppermute(block, "slab", [(i + 1, i) for i in range(ends)])


def here_to_above(block):
    ends = lax.axis_size("slab") - 1
    return lax.ppermute(block, "slab", [(i, i + 1) for i in range(ends)])


def next_to_here(block):
    count = lax.axis_size("tile")
    return lax.ppermute(block, "tile", [((i + 1) % count, i) for i in range(count)])


def here_to_next(block):
    count = lax.axis_size("tile")
    return lax.ppermute(block, "tile", [(i, (i + 1) % count) for i in range(count)])


def pairwise(block, last):
    count = lax.axis_size("tile")
    pairs = [(i, (i + (-1 if (i % 2 == 0) == last else 1)) % count) for i in range(count)]
    return lax.ppermute(block, "tile", pairs)


def across_to_here(block):
    slabs, count = lax.axis_size("slab"), lax.axis_size("tile")
    pairs = [
        ((slab + 1) * count + (tile + 1) % count, slab * count + tile)
        for slab in range(slabs - 1)
        for tile in range(count)
    ]
    return lax.ppermute(block, ("slab", "tile"), pairs)


def swap_sums(own, above, round_one, round_two):
    own, above = run_merge(own, above, pairwise(round_one, False), pairwise(round_two, True))
    return own, above, here_to_above(above), above_to_here(own)


def here_to_across(block):
    slabs, count = lax.axis_size("slab"), lax.axis_size("tile")
    pairs = [
        (slab * count + tile, (slab + 1) * count + (tile + 1) % count)
        for slab in range(slabs - 1)
        for tile in range(count)
    ]
    return lax.ppermute(block, ("slab", "tile"), pairs)


def slab_boxes(block, edges, across, along):
    rows = [
        jnp.concatenate(
            [
                block[axis * TILES : (axis + 1) * TILES],
                edges[axis * EDGE : (axis + 1) * EDGE],
                jnp.zeros((HALF - LIVE, ATOMS), F32),
            ]
        )
        for axis in range(3)
    ]
    x, y, z = rows
    pieces = jnp.stack([x * across + y * along, y * across - x * along, z]).reshape(3, HALF, CHUNKS, CHUNK)
    low, high = jnp.min(pieces, axis=3), jnp.max(pieces, axis=3)
    return low, high, jnp.min(low, axis=2), jnp.max(high, axis=2)


def chunk_codes(low, high, tile_low, tile_high):
    near = []
    for chunk in range(CHUNKS):
        own_low, own_high = low[:, :OWN_ROWS, chunk, None], high[:, :OWN_ROWS, chunk, None]
        gap = jnp.maximum(jnp.maximum(tile_low[:, None, :] - own_high, own_low - tile_high[:, None, :]), 0.0)
        far = jnp.sum(gap * gap, axis=0) >= cutoff_sq * 1.001
        near.append(jnp.logical_not(far).astype(jnp.int32))
    number = sum(near)
    code = number << (3 * CHUNKS)
    before = jnp.zeros_like(number)
    for chunk in range(CHUNKS):
        rank = jnp.where(near[chunk] == 1, before, number + chunk - before)
        code = code + (chunk << (3 * rank))
        before = before + near[chunk]
    return code


def chunk_reach(sent, edges, above, above_edges):
    across, along = sent[TILES // 2, 0], sent[TILES + TILES // 2, 0]
    inverse = lax.rsqrt(across * across + along * along)
    across, along = across * inverse, along * inverse
    low, high, *tile = slab_boxes(sent, edges, across, along)
    *_, above_low, above_high = slab_boxes(above, above_edges, across, along)
    own_codes = chunk_codes(low, high, *tile)
    code = jnp.concatenate([own_codes, chunk_codes(low, high, above_low, above_high)], axis=1)
    return code, (code >> (3 * CHUNKS)) <= CHUNKS // 2


def packed(first, second, valid, is_part):
    first, second, valid = first.reshape(-1), second.reshape(-1), valid.reshape(-1)
    mine = (first[:, None] == jnp.arange(OWN_ROWS)[None, :]).astype(jnp.bfloat16)
    rows = jnp.dot(mine, is_part.astype(jnp.bfloat16), preferred_element_type=F32)
    in_part = jnp.sum(jnp.where(second[:, None] == jnp.arange(REGION)[None, :], rows, 0.0), axis=1) > 0.5
    entry = jnp.arange(valid.shape[0])
    ahead = valid[None, :] & (entry[None, :] < entry[:, None]) & (in_part[None, :] == in_part[:, None])
    rank = jnp.sum(ahead, axis=1)
    fulls = jnp.sum(valid & jnp.logical_not(in_part), dtype=jnp.int32)
    parts = jnp.sum(valid & in_part, dtype=jnp.int32)
    fulls = (fulls + FULL_WIDTH - 1) // FULL_WIDTH * FULL_WIDTH
    parts = (parts + PART_WIDTH - 1) // PART_WIDTH * PART_WIDTH
    rank = jnp.where(in_part, fulls + rank, rank)
    chosen = valid[None, :] & (rank[None, :] == jnp.arange(ITEMS)[:, None])
    value = first * ATOMS + second - DUMMY
    items = DUMMY + jnp.sum(jnp.where(chosen, value[None, :], 0), axis=1)
    slot = jnp.arange(ITEMS)
    items = jnp.where(slot == ITEMS - 2, fulls, jnp.where(slot == ITEMS - 1, parts, items))
    return items.astype(jnp.int32)


def pair_items(here, above, is_part):
    listed = above[6 * TILES :, 0:TILES].astype(jnp.int32)
    has_above = lax.axis_index("slab") < lax.axis_size("slab") - 1
    tiles = lax.broadcasted_iota(jnp.int32, here.shape, 1)
    return packed(
        jnp.concatenate([tiles, listed]),
        jnp.concatenate([here, HALF + tiles]),
        jnp.concatenate([here >= 0, (listed >= 0) & has_above]),
        is_part,
    )


def body(positions, charges, radii, scales, neighbours, pad_mask):
    sent, edges, here = run_pack(
        jnp.swapaxes(positions[0, 0], 0, 1),
        charges[0, 0],
        radii[0, 0],
        scales[0, 0],
        neighbours[0, 0].T,
        pad_mask[0, 0].T,
    )
    above = above_to_here(sent)
    next_edges = next_to_here(edges)
    above_edges = across_to_here(edges)
    reach, is_part = chunk_reach(sent, next_edges, above, above_edges)
    items = pair_items(here, above, is_part)

    *parts, data, plain, d_self, d_pair = run_born(items, reach, sent, next_edges, above, above_edges)
    shares = swap_sums(*parts)
    radii_born, slope, *parts, force = run_energy(items, reach, data, plain, shares)
    shares = swap_sums(*parts)
    gradient, own, over, to_next, to_across = run_force(
        items, reach, data, slope, shares, force, d_self, d_pair
    )
    forces, to_next, to_across = lax.optimization_barrier(
        (own + here_to_above(over), here_to_next(to_next), here_to_across(to_across))
    )
    forces = forces + jnp.pad((to_next + to_across)[:, 0:EDGE], ((0, 0), (0, TILES - EDGE), (0, 0)))
    return (radii_born[None, None], gradient[None, None], jnp.swapaxes(forces, 0, 1)[None, None])


def solution(mesh):
    return jax.shard_map(
        body,
        mesh=mesh,
        in_specs=(
            P("slab", "tile", None, None, None),
            P("slab", "tile", None, None),
            P("slab", "tile", None, None),
            P("slab", "tile", None, None),
            P("slab", "tile", None, None),
            P("slab", "tile", None, None),
        ),
        out_specs=(
            P("slab", "tile", None, None),
            P("slab", "tile", None, None),
            P("slab", "tile", None, None, None),
        ),
        check_vma=False,
    )
```

```python
import functools
import math

import jax
import jax.numpy as jnp
import numpy as np
from jax import lax
from jax.experimental import pallas as pl
from jax.experimental.pallas import tpu as pltpu
from jax.sharding import PartitionSpec as P

radius_offset = 0.09
obc_alpha = 1.0
obc_beta = 0.8
obc_gamma = 4.85
cutoff_len = 14.0
cutoff_sq = cutoff_len * cutoff_len

TILES = 32
EDGE = 2
LIVE = TILES + EDGE
HALF = 40
REGION = 2 * HALF
OWN_ROWS = LIVE + 1
SENT_ROWS = 6 * TILES + 8
LISTED = 7
ATOMS = 128
CHUNK = 16
CHUNKS = ATOMS // CHUNK
FULL_WIDTH = 4
PART_WIDTH = 4
FULL_RING = 32
PART_RING = 32
PAIRS = 2 * TILES * LISTED + 6
ITEMS = 512
DUMMY = LIVE * ATOMS + LIVE
ROW = (1, ATOMS)
LANES = (8, ATOMS)
ROWS = (CHUNK, ATOMS)
BLOCK = (ATOMS, ATOMS)
PART = ATOMS // 2
VMEM_LIMIT = 56 * 1024 * 1024
SCALE = math.sqrt(8.0) / cutoff_len
CUT = 8.0
EXP_SCALE = math.sqrt(0.25 / math.log(2.0)) / SCALE

ROW_X, ROW_Y, ROW_Z, ROW_Q, ROW_IN, ROW_SCALED = range(6)
AT_Q, AT_RADIUS, AT_SCALED = 3, 4, 5

F32 = jnp.float32


def fold2(block):
    return block[0:8] + block[8:16]


def fold_own(own):
    flipped = own.T
    total = flipped[0:8]
    for chunk in range(1, ATOMS // 8):
        total = total + flipped[8 * chunk : 8 * chunk + 8]
    return total


def build_beside(build, work, table, fresh_a, fresh_b):
    def keep(tile, fresh, k):
        table[tile] = fresh[k]

    def step(index, carry):
        first = index * 4
        for k in range(2):
            build(first + 2 + k, fresh_b, k)
            work(first + k, fresh_a, k)
        for k in range(2):
            keep(first + k, fresh_a, k)
        for k in range(2):
            build(first + 4 + k, fresh_a, k)
            work(first + 2 + k, fresh_b, k)
        for k in range(2):
            keep(first + 2 + k, fresh_b, k)
        return carry

    for k in range(2):
        build(k, fresh_a, k)
    lax.fori_loop(0, TILES // 4, step, 0)
    for k in range(EDGE):
        keep(TILES + k, fresh_a, k)


def by_fours(step):
    def fours(index, carry):
        start = jnp.minimum(index * 4, LIVE - 4)
        for k in range(4):
            step(start + k)
        return carry

    lax.fori_loop(0, (LIVE + 3) // 4, fours, 0)


def fill_table(table, k, first, ref, tile, rows):
    for slot, row in enumerate(rows):
        table[k, first + slot] = jnp.broadcast_to(ref[tile, row : row + 1, :], BLOCK).T


def fold_rows(fold, width):
    def step(index, carry):
        for k in range(width):
            fold(index * width + k)
        return carry

    lax.fori_loop(0, TILES // width, step, 0)
    for tile in range(TILES, LIVE):
        fold(tile)


def diagonal(start):
    rows = lax.broadcasted_iota(jnp.int32, ROWS, 0) + start
    return jnp.where(rows == lax.broadcasted_iota(jnp.int32, ROWS, 1), 4.0 * CUT, 0.0)


def decode(item):
    return lax.shift_right_logical(item, 7), lax.bitwise_and(item, ATOMS - 1)


def span(start):
    return pl.ds(start if isinstance(start, int) else pl.multiple_of(start, CHUNK), CHUNK)


def part_starts(code):
    return [lax.bitwise_and(lax.shift_right_logical(code, 3 * j), 7) * CHUNK for j in range(CHUNKS // 2)]


def row_of(ref, tile, row):
    return jnp.broadcast_to(ref[tile, row : row + 1, :], ROWS)


def differences(table, tile, rows, far):
    return tuple(table[tile, axis, rows, :] - far[axis] for axis in range(3))


def distance_squared(gaps):
    dx, dy, dz = gaps
    return dx * dx + dy * dy + dz * dz


def half_descreen(r, own, far):
    upper = r + far
    lower = r - far
    inner = jnp.minimum(jnp.maximum(own, lower), upper)
    ratio = upper * pl.reciprocal(inner, approx=True)
    slope = lower * pl.reciprocal(upper, approx=True)
    square = ratio * ratio
    rise = ratio - 1.0
    twice = jnp.log(square)
    value = rise * (2.0 - slope * rise) - twice
    deriv = (twice + twice) - (square - 1.0) * (slope * slope + 1.0)
    return value, deriv


def ring_copies(ring, blocks, sems, size, rows):
    def copy(index, place, inward):
        slot = lax.rem(index, size)
        here = ring.at[slot]
        there = blocks.at[place, :, pl.ds(0, rows), :]
        source, target = (there, here) if inward else (here, there)
        return pltpu.make_async_copy(source, target, sems.at[slot])

    return copy


def edge_rows(values, first):
    rest = jnp.zeros((8 - 2 * EDGE, ATOMS), F32)
    return jnp.concatenate([values[first : first + EDGE], values[HALF + first : HALF + first + EDGE], rest])


def edge_rounds(values, one, two):
    to_next, to_last = edge_rows(values, TILES), edge_rows(values, 0)
    is_even = lax.rem(lax.axis_index("tile"), 2) == 0
    one[...] = jnp.where(is_even, to_next, to_last)
    two[...] = jnp.where(is_even, to_last, to_next)


def pack_kernel(positions, charges, radii, scales, neighbours, pad_mask, sent, edges, here):
    radius = radii[...]
    values = [positions[0], positions[1], positions[2], charges[...], radius, scales[...] * (radius - radius_offset)]
    edges[...] = jnp.zeros_like(edges)
    for index, value in enumerate(values):
        sent[index * TILES : (index + 1) * TILES, :] = value
        edges[EDGE * index : EDGE * (index + 1), :] = value[0:EDGE]
    cycle_count = lax.axis_size("tile")
    cycle_tiles = cycle_count * TILES
    listed = neighbours[...]
    slab_step = lax.div(listed, cycle_tiles) - lax.axis_index("slab")
    within = lax.rem(listed, cycle_tiles)
    cycle_step = lax.rem(lax.div(within, TILES) - lax.axis_index("tile") + cycle_count, cycle_count)
    place = cycle_step * TILES + lax.rem(within, TILES)
    slots = lax.broadcasted_iota(jnp.int32, listed.shape, 0)
    live = (pad_mask[...] == 1) & (slots > 0)
    here[...] = jnp.where(live & (slab_step >= 0), slab_step * HALF + place, -1)
    sent[6 * TILES :, :] = jnp.full(LANES, -1.0, F32)
    sent[6 * TILES :, 0:TILES] = jnp.where(live & (slab_step < 0), place, -1).astype(F32)


def born_kernel(
    items, reach, sent, edges, above, above_edges,
    own_part, above_part, round_one, round_two, data, plain, d_self, d_pair,
    table, fresh_a, fresh_b, own, far, rings, sems,
):
    full_ring, part_ring, self_ring = rings
    full_sems, part_sems, self_sems = sems
    far[...] = jnp.zeros_like(far)
    data[...] = jnp.zeros_like(data)
    plain[...] = jnp.ones_like(plain)
    fulls, parts = items[ITEMS - 2], items[ITEMS - 1]

    for index in range(6):
        origin = sent[index * TILES + TILES // 2 : index * TILES + TILES // 2 + 1, 0:1]
        for start, source, edge in ((0, sent, edges), (HALF, above, above_edges)):
            for place, values in (
                (start, source[index * TILES : (index + 1) * TILES, :]),
                (start + TILES, edge[EDGE * index : EDGE * (index + 1), :]),
            ):
                rows = slice(place, place + values.shape[0])
                if index < AT_Q:
                    data[rows, index, :] = (values - origin) * SCALE
                elif index == AT_Q:
                    data[rows, ROW_Q, :] = values
                    plain[2, rows, :] = values if place == 0 else jnp.zeros_like(values)
                elif index == AT_RADIUS:
                    data[rows, ROW_IN, :] = (values - radius_offset) * SCALE
                    plain[0, rows, :] = values
                    plain[1, rows, :] = values - radius_offset
                else:
                    data[rows, ROW_SCALED, :] = values * SCALE

    def build(tile, fresh, k):
        fill_table(fresh, k, 0, data, tile, (ROW_X, ROW_Y, ROW_Z, ROW_IN, ROW_SCALED))

    for tile in range(TILES, OWN_ROWS):
        own[tile] = jnp.zeros(BLOCK, F32)

    def shared(r2):
        inv = lax.rsqrt(r2)
        cut = jnp.maximum(1.0 - r2 * (1.0 / CUT), 0.0)
        cinv = cut * inv
        return r2 * inv, cut, cinv, cinv * cinv * inv

    def self_pair(tile, fresh, k):
        far_xyz = [row_of(data, tile, axis) for axis in range(3)]
        bs = row_of(data, tile, ROW_SCALED)
        for start in range(0, ATOMS, CHUNK):
            rows = span(start)
            r2 = distance_squared(differences(fresh, k, rows, far_xyz)) + diagonal(start)
            r, cut, cinv, g_deriv = shared(r2)
            value, deriv = half_descreen(r, fresh[k, 3, rows, :], bs)
            value = cinv * value
            own[tile, rows, :] = cut * value
            self_ring[tile, rows, :] = g_deriv * deriv - value

    def self_copy(tile):
        return pltpu.make_async_copy(self_ring.at[tile], d_self.at[tile], self_sems.at[tile])

    def self_step(tile, fresh, k):
        self_pair(tile, fresh, k)
        self_copy(tile).start()

    build_beside(build, self_step, table, fresh_a, fresh_b)

    def pair(item, ring, slot, starts):
        first, second = item
        far_xyz = [row_of(data, second, axis) for axis in range(3)]
        bp, bs = row_of(data, second, ROW_IN), row_of(data, second, ROW_SCALED)
        sums = jnp.zeros(ROWS, F32)
        for place, start in enumerate(starts):
            rows = span(start)
            kept = span(place * CHUNK)
            r2 = distance_squared(differences(table, first, rows, far_xyz))
            r, cut, cinv, g_deriv = shared(r2)
            value, deriv = half_descreen(r, table[first, 3, rows, :], bs)
            value = cinv * value
            own[first, rows, :] += cut * value
            ring[slot, 0, kept, :] = g_deriv * deriv - value
            value, deriv = half_descreen(r, bp, table[first, 4, rows, :])
            value = cinv * value
            ring[slot, 1, kept, :] = g_deriv * deriv - value
            sums = sums + cut * value
        far[second] += fold2(sums)

    def run(width, size, ring, ring_sems, base, number, rows, starts_of):
        copy = ring_copies(ring, d_pair, ring_sems, size, rows)

        def body(index, carry):
            begin = index * width
            for k in range(width):

                @pl.when(begin + k >= size)
                def _():
                    copy(begin + k, base + begin + k, False).wait()

            for k in range(width):
                item = decode(items[base + begin + k])
                pair(item, ring, lax.rem(begin + k, size), starts_of(item))
            for k in range(width):
                copy(begin + k, base + begin + k, False).start()
            return carry

        lax.fori_loop(0, lax.div(number, width), body, 0)

    def drain(size, ring, ring_sems, number, rows):
        copy = ring_copies(ring, d_pair, ring_sems, size, rows)

        def wait(slot, carry):
            copy(slot, slot, False).wait()
            return carry

        lax.fori_loop(0, jnp.minimum(number, size), wait, 0)

    def listed_starts(item):
        return part_starts(reach[item[0], item[1]])

    run(FULL_WIDTH, FULL_RING, full_ring, full_sems, 0, fulls, ATOMS, lambda item: range(0, ATOMS, CHUNK))
    run(PART_WIDTH, PART_RING, part_ring, part_sems, fulls, parts, PART, listed_starts)

    def fold(tile):
        far[tile] += fold_own(own[tile])

    fold_rows(fold, 8)
    sums = jnp.sum(far[...], axis=1) * (0.125 * SCALE)
    own_part[...] = sums[0:HALF]
    above_part[...] = sums[HALF:]
    edge_rounds(sums, round_one, round_two)

    def wait_self(tile, carry):
        self_copy(tile).wait()
        return carry

    lax.fori_loop(0, TILES, wait_self, 0)
    drain(FULL_RING, full_ring, full_sems, fulls, ATOMS)
    drain(PART_RING, part_ring, part_sems, parts, PART)


def energy_kernel(
    items, reach, data, plain, own_part, above_part, from_below, from_above,
    radii_born, slope, own_grad, above_grad, round_one, round_two, force_out,
    table, fresh_a, fresh_b, own, far, born, force,
):
    far[...] = jnp.zeros_like(far)
    force[...] = jnp.zeros_like(force)
    fulls, parts = items[ITEMS - 2], items[ITEMS - 1]
    sums = jnp.concatenate([own_part[...] + from_below[...], above_part[...] + from_above[...]])
    all_radii, all_slopes = born_radius(sums, plain[0], plain[1])
    inverse = 1.0 / all_radii
    radii_born[...] = all_radii[0:TILES]
    slope[...] = all_slopes
    born[:, 0, :] = SCALE * all_radii
    born[:, 1, :] = EXP_SCALE * inverse

    def build(tile, fresh, k):
        fill_table(fresh, k, 0, data, tile, (ROW_X, ROW_Y, ROW_Z, ROW_Q))
        fill_table(fresh, k, 4, born, tile, (0, 1))

    for tile in range(TILES, OWN_ROWS):
        own[tile] = jnp.zeros((4,) + BLOCK, F32)

    def pair(first, second, starts, tables, k, is_self):
        far_xyz = [row_of(data, second, axis) for axis in range(3)]
        br, bi, bq = row_of(born, second, 0), -row_of(born, second, 1), row_of(data, second, ROW_Q)
        sums = [jnp.zeros(ROWS, F32)] * 4
        for start in starts:
            rows = span(start)
            gaps = differences(tables, k, rows, far_xyz)
            r2 = distance_squared(gaps)
            if is_self:
                r2 = r2 + diagonal(start)
            cut = jnp.maximum(1.0 - r2 * (1.0 / CUT), 0.0)
            power = r2 * (tables[k, 5, rows, :] * bi)
            decay = lax.exp2(power)
            screen = (tables[k, 4, rows, :] * br) * decay
            inv = lax.rsqrt(r2 + screen)
            cinv = cut * inv
            lead = (tables[k, 3, rows, :] * bq) * cinv
            square = cinv * inv
            grad = (lead * square) * (screen * (1.0 - math.log(2.0) * power))
            pull = lead * (square * (4.0 - decay) + 16.0 / CUT)
            terms = [grad] + [pull * gap for gap in gaps]
            for which, term in enumerate(terms):
                if is_self:
                    own[first, which, rows, :] = term
                else:
                    own[first, which, rows, :] += term
                    sums[which] = sums[which] + term
        if not is_self:
            far[second] += fold2(sums[0])
            for axis in range(3):
                force[second, axis] -= fold2(sums[1 + axis])

    def self_step(tile, fresh, k):
        pair(tile, tile, range(0, ATOMS, CHUNK), fresh, k, True)

    build_beside(build, self_step, table, fresh_a, fresh_b)

    def full_step(index, carry):
        for k in range(FULL_WIDTH):
            first, second = decode(items[index * FULL_WIDTH + k])
            pair(first, second, range(0, ATOMS, CHUNK), table, first, False)
        return carry

    def part_step(index, carry):
        for k in range(PART_WIDTH):
            first, second = decode(items[fulls + index * PART_WIDTH + k])
            starts = part_starts(reach[first, second])
            pair(first, second, starts, table, first, False)
        return carry

    lax.fori_loop(0, lax.div(fulls, FULL_WIDTH), full_step, 0)
    lax.fori_loop(0, lax.div(parts, PART_WIDTH), part_step, 0)

    def fold(tile):
        far[tile] += fold_own(own[tile, 0])
        for axis in range(3):
            force[tile, axis] += fold_own(own[tile, 1 + axis])

    fold_rows(fold, 4)
    for axis in range(3):
        force_out[axis] = jnp.sum(force[:, axis], axis=1)
    charge = plain[2] * inverse
    sums = jnp.sum(far[...], axis=1) * (0.5 * SCALE) * inverse + 0.5 * charge * charge
    own_grad[...] = sums[0:HALF]
    above_grad[...] = sums[HALF:]
    edge_rounds(sums, round_one, round_two)


def force_kernel(
    items, reach, data, slope, own_grad, above_grad, from_below, from_above, force_in, d_self, d_pair,
    gradient, own_force, above_force, to_next, to_across,
    table, own, far, chain, rings, sems,
):
    full_ring, part_ring, self_ring = rings
    full_sems, part_sems, self_sems = sems
    fulls, parts = items[ITEMS - 2], items[ITEMS - 1]
    full_copy = ring_copies(full_ring, d_pair, full_sems, FULL_RING, ATOMS)
    part_copy = ring_copies(part_ring, d_pair, part_sems, PART_RING, PART)

    self_copy = pltpu.make_async_copy(d_self, self_ring, self_sems.at[0])

    def start(copy, base):
        def step(index, carry):
            copy(index, base + index, True).start()
            return carry

        return step

    self_copy.start()
    lax.fori_loop(0, jnp.minimum(fulls, FULL_RING), start(full_copy, 0), 0)
    lax.fori_loop(0, jnp.minimum(parts, PART_RING), start(part_copy, fulls), 0)

    far[...] = jnp.zeros_like(far)
    grads = jnp.concatenate([own_grad[...] + from_below[...], above_grad[...] + from_above[...]])
    gradient[...] = grads[0:TILES]
    chain[:, 0, :] = grads * slope[...]

    def build(tile):
        fill_table(table, tile, 0, data, tile, (ROW_X, ROW_Y, ROW_Z))
        fill_table(table, tile, 3, chain, tile, (0,))

    by_fours(build)
    for tile in range(TILES, OWN_ROWS):
        own[tile] = jnp.zeros((3,) + BLOCK, F32)

    def pair(first, second, starts, tables, k, pull_of, is_self):
        far_xyz = [row_of(data, second, axis) for axis in range(3)]
        sums = [jnp.zeros(ROWS, F32)] * 3
        for place, start in enumerate(starts):
            rows = span(start)
            pull = pull_of(rows, span(place * CHUNK))
            terms = [pull * gap for gap in differences(tables, k, rows, far_xyz)]
            for which, term in enumerate(terms):
                if is_self:
                    own[first, which, rows, :] = term
                else:
                    own[first, which, rows, :] += term
                sums[which] = sums[which] + term
        for axis in range(3):
            far[second, axis] -= fold2(sums[axis])

    self_copy.wait()

    def self_step(quad, carry):
        begin = quad * 4
        for k in range(4):
            tile = begin + k
            pair(
                tile,
                tile,
                range(0, ATOMS, CHUNK),
                table,
                tile,
                lambda rows, kept: table[tile, 3, rows, :] * self_ring[tile, kept, :],
                True,
            )
        return carry

    lax.fori_loop(0, TILES // 4, self_step, 0)

    def run(width, size, ring, copy, base, number, starts_of):
        def body(index, carry):
            begin = index * width
            for k in range(width):
                copy(begin + k, base + begin + k, True).wait()
            for k in range(width):
                first, second = decode(items[base + begin + k])
                slot = lax.rem(begin + k, size)
                factor = row_of(chain, second, 0)
                pair(
                    first,
                    second,
                    starts_of(first, second),
                    table,
                    first,
                    lambda rows, kept: table[first, 3, rows, :] * ring[slot, 0, kept, :]
                    + factor * ring[slot, 1, kept, :],
                    False,
                )
            for k in range(width):

                @pl.when(begin + k + size < number)
                def _():
                    copy(begin + k + size, base + begin + k + size, True).start()

            return carry

        lax.fori_loop(0, lax.div(number, width), body, 0)

    run(FULL_WIDTH, FULL_RING, full_ring, full_copy, 0, fulls, lambda *_: range(0, ATOMS, CHUNK))
    run(
        PART_WIDTH,
        PART_RING,
        part_ring,
        part_copy,
        fulls,
        parts,
        lambda first, second: part_starts(reach[first, second]),
    )

    def fold(tile):
        for axis in range(3):
            far[tile, axis] += fold_own(own[tile, axis])

    fold_rows(fold, 4)
    for axis in range(3):
        sums = (jnp.sum(far[:, axis], axis=1) + 4.0 * force_in[axis]) * (-SCALE * SCALE / 16.0)
        own_force[axis] = sums[0:TILES]
        above_force[axis] = sums[HALF : HALF + TILES]
        to_next[axis] = sums[TILES : TILES + 8]
        to_across[axis] = sums[HALF + TILES : HALF + TILES + 8]


SMEM = pl.BlockSpec(memory_space=pltpu.SMEM)
VMEM = pl.BlockSpec(memory_space=pltpu.VMEM)
ANY = pl.BlockSpec(memory_space=pl.ANY)
PARAMS = pltpu.CompilerParams(vmem_limit_bytes=VMEM_LIMIT)
RING_BLOCKS = (
    pltpu.VMEM((FULL_RING, 2) + BLOCK, F32),
    pltpu.VMEM((PART_RING, 2, PART, ATOMS), F32),
    pltpu.VMEM((TILES,) + BLOCK, F32),
)
RING_SEMS = (
    pltpu.SemaphoreType.DMA((FULL_RING,)),
    pltpu.SemaphoreType.DMA((PART_RING,)),
    pltpu.SemaphoreType.DMA((TILES,)),
)


def f32(*shape):
    return jax.ShapeDtypeStruct(shape, F32)


def run_pack(positions, charges, radii, scales, neighbours, pad_mask):
    return pl.pallas_call(
        pack_kernel,
        name="pack_atoms",
        out_shape=(
            f32(SENT_ROWS, ATOMS),
            f32(16, ATOMS),
            jax.ShapeDtypeStruct(neighbours.shape, jnp.int32),
        ),
        in_specs=[VMEM] * 6,
        out_specs=(VMEM,) * 3,
        compiler_params=PARAMS,
    )(positions, charges, radii, scales, neighbours, pad_mask)


def run_born(items, reach, sent, edges, above, above_edges):
    return pl.pallas_call(
        born_kernel,
        name="born_sums",
        out_shape=(
            f32(HALF, ATOMS),
            f32(HALF, ATOMS),
            f32(*LANES),
            f32(*LANES),
            f32(REGION, *LANES),
            f32(3, REGION, ATOMS),
            f32(TILES, *BLOCK),
            f32(PAIRS, 2, *BLOCK),
        ),
        in_specs=[SMEM] * 2 + [VMEM] * 4,
        out_specs=(VMEM,) * 6 + (ANY,) * 2,
        scratch_shapes=[
            pltpu.VMEM((OWN_ROWS, 5) + BLOCK, F32),
            pltpu.VMEM((2, 5) + BLOCK, F32),
            pltpu.VMEM((2, 5) + BLOCK, F32),
            pltpu.VMEM((OWN_ROWS,) + BLOCK, F32),
            pltpu.VMEM((REGION,) + LANES, F32),
            RING_BLOCKS,
            RING_SEMS,
        ],
        compiler_params=PARAMS,
    )(items, reach, sent, edges, above, above_edges)


def run_energy(items, reach, data, plain, shares):
    return pl.pallas_call(
        energy_kernel,
        name="radius_gradient",
        out_shape=(
            f32(TILES, ATOMS),
            f32(REGION, ATOMS),
            f32(HALF, ATOMS),
            f32(HALF, ATOMS),
            f32(*LANES),
            f32(*LANES),
            f32(3, REGION, ATOMS),
        ),
        in_specs=[SMEM] * 2 + [VMEM] * 6,
        out_specs=(VMEM,) * 7,
        scratch_shapes=[
            pltpu.VMEM((OWN_ROWS, 6) + BLOCK, F32),
            pltpu.VMEM((2, 6) + BLOCK, F32),
            pltpu.VMEM((2, 6) + BLOCK, F32),
            pltpu.VMEM((OWN_ROWS, 4) + BLOCK, F32),
            pltpu.VMEM((REGION,) + LANES, F32),
            pltpu.VMEM((REGION,) + LANES, F32),
            pltpu.VMEM((REGION, 3) + LANES, F32),
        ],
        compiler_params=PARAMS,
    )(items, reach, data, plain, *shares)


def run_force(items, reach, data, slope, shares, force_in, d_self, d_pair):
    return pl.pallas_call(
        force_kernel,
        name="forces",
        out_shape=(
            f32(TILES, ATOMS),
            f32(3, TILES, ATOMS),
            f32(3, TILES, ATOMS),
            f32(3, *LANES),
            f32(3, *LANES),
        ),
        in_specs=[SMEM] * 2 + [VMEM] * 7 + [ANY] * 2,
        out_specs=(VMEM,) * 5,
        scratch_shapes=[
            pltpu.VMEM((OWN_ROWS, 4) + BLOCK, F32),
            pltpu.VMEM((OWN_ROWS, 3) + BLOCK, F32),
            pltpu.VMEM((REGION, 3) + LANES, F32),
            pltpu.VMEM((REGION,) + LANES, F32),
            RING_BLOCKS,
            RING_SEMS,
        ],
        compiler_params=PARAMS,
    )(items, reach, data, slope, *shares, force_in, d_self, d_pair)


def born_radius(descreen_sum, radius, radius_in):
    scaled = radius_in * descreen_sum
    polynomial = scaled * (obc_alpha + scaled * (-obc_beta + obc_gamma * scaled))
    tangent = jnp.tanh(polynomial)
    radii_born = 1.0 / (1.0 / radius_in - tangent / radius)
    radius_slope = (
        radii_born
        * radii_born
        * (1.0 - tangent * tangent)
        / radius
        * (obc_alpha - 2.0 * obc_beta * scaled + 3.0 * obc_gamma * scaled * scaled)
        * radius_in
    )
    return (radii_born, radius_slope)


def above_to_here(block):
    ends = lax.axis_size("slab") - 1
    return lax.ppermute(block, "slab", [(i + 1, i) for i in range(ends)])


def here_to_above(block):
    ends = lax.axis_size("slab") - 1
    return lax.ppermute(block, "slab", [(i, i + 1) for i in range(ends)])


def next_to_here(block):
    count = lax.axis_size("tile")
    return lax.ppermute(block, "tile", [((i + 1) % count, i) for i in range(count)])


def here_to_next(block):
    count = lax.axis_size("tile")
    return lax.ppermute(block, "tile", [(i, (i + 1) % count) for i in range(count)])


def pairwise(block, last):
    count = lax.axis_size("tile")
    pairs = [(i, (i + (-1 if (i % 2 == 0) == last else 1)) % count) for i in range(count)]
    return lax.ppermute(block, "tile", pairs)


def across_to_here(block):
    slabs, count = lax.axis_size("slab"), lax.axis_size("tile")
    pairs = [
        ((slab + 1) * count + (tile + 1) % count, slab * count + tile)
        for slab in range(slabs - 1)
        for tile in range(count)
    ]
    return lax.ppermute(block, ("slab", "tile"), pairs)


def placed(block, first, last):
    return jnp.pad(block[first : first + EDGE], ((0, HALF - EDGE), (0, 0))) + jnp.pad(
        last[first : first + EDGE], ((TILES, HALF - LIVE), (0, 0))
    )


def swap_sums(own, above, round_one, round_two):
    one, two = pairwise(round_one, False), pairwise(round_two, True)
    is_even = lax.axis_index("tile") % 2 == 0
    from_next, from_last = jnp.where(is_even, one, two), jnp.where(is_even, two, one)
    own = own + placed(from_last, 0, from_next)
    above = above + placed(from_last, EDGE, from_next)
    own, above = lax.optimization_barrier((own, above))
    return own, above, here_to_above(above), above_to_here(own)


def here_to_across(block):
    slabs, count = lax.axis_size("slab"), lax.axis_size("tile")
    pairs = [
        (slab * count + tile, (slab + 1) * count + (tile + 1) % count)
        for slab in range(slabs - 1)
        for tile in range(count)
    ]
    return lax.ppermute(block, ("slab", "tile"), pairs)


def slab_boxes(block, edges, across, along):
    rows = [
        jnp.concatenate(
            [
                block[axis * TILES : (axis + 1) * TILES],
                edges[axis * EDGE : (axis + 1) * EDGE],
                jnp.zeros((HALF - LIVE, ATOMS), F32),
            ]
        )
        for axis in range(3)
    ]
    x, y, z = rows
    pieces = jnp.stack([x * across + y * along, y * across - x * along, z]).reshape(3, HALF, CHUNKS, CHUNK)
    low, high = jnp.min(pieces, axis=3), jnp.max(pieces, axis=3)
    return low, high, jnp.min(low, axis=2), jnp.max(high, axis=2)


def chunk_codes(low, high, tile_low, tile_high):
    near = []
    for chunk in range(CHUNKS):
        own_low, own_high = low[:, :OWN_ROWS, chunk, None], high[:, :OWN_ROWS, chunk, None]
        gap = jnp.maximum(jnp.maximum(tile_low[:, None, :] - own_high, own_low - tile_high[:, None, :]), 0.0)
        far = jnp.sum(gap * gap, axis=0) >= cutoff_sq * 1.001
        near.append(jnp.logical_not(far).astype(jnp.int32))
    number = sum(near)
    code = number << (3 * CHUNKS)
    before = jnp.zeros_like(number)
    for chunk in range(CHUNKS):
        rank = jnp.where(near[chunk] == 1, before, number + chunk - before)
        code = code + (chunk << (3 * rank))
        before = before + near[chunk]
    return code


def chunk_reach(sent, edges, above, above_edges):
    across, along = sent[TILES // 2, 0], sent[TILES + TILES // 2, 0]
    inverse = lax.rsqrt(across * across + along * along)
    across, along = across * inverse, along * inverse
    low, high, *tile = slab_boxes(sent, edges, across, along)
    *_, above_low, above_high = slab_boxes(above, above_edges, across, along)
    own_codes = chunk_codes(low, high, *tile)
    code = jnp.concatenate([own_codes, chunk_codes(low, high, above_low, above_high)], axis=1)
    return code, (code >> (3 * CHUNKS)) <= CHUNKS // 2


def packed(first, second, valid, is_part):
    first, second, valid = first.reshape(-1), second.reshape(-1), valid.reshape(-1)
    mine = (first[:, None] == jnp.arange(OWN_ROWS)[None, :]).astype(jnp.bfloat16)
    rows = jnp.dot(mine, is_part.astype(jnp.bfloat16), preferred_element_type=F32)
    in_part = jnp.sum(jnp.where(second[:, None] == jnp.arange(REGION)[None, :], rows, 0.0), axis=1) > 0.5
    entry = jnp.arange(valid.shape[0])
    ahead = valid[None, :] & (entry[None, :] < entry[:, None]) & (in_part[None, :] == in_part[:, None])
    rank = jnp.sum(ahead, axis=1)
    fulls = jnp.sum(valid & jnp.logical_not(in_part), dtype=jnp.int32)
    parts = jnp.sum(valid & in_part, dtype=jnp.int32)
    fulls = (fulls + FULL_WIDTH - 1) // FULL_WIDTH * FULL_WIDTH
    parts = (parts + PART_WIDTH - 1) // PART_WIDTH * PART_WIDTH
    rank = jnp.where(in_part, fulls + rank, rank)
    chosen = valid[None, :] & (rank[None, :] == jnp.arange(ITEMS)[:, None])
    value = first * ATOMS + second - DUMMY
    items = DUMMY + jnp.sum(jnp.where(chosen, value[None, :], 0), axis=1)
    slot = jnp.arange(ITEMS)
    items = jnp.where(slot == ITEMS - 2, fulls, jnp.where(slot == ITEMS - 1, parts, items))
    return items.astype(jnp.int32)


def pair_items(here, above, is_part):
    listed = above[6 * TILES + 1 :, 0:TILES].astype(jnp.int32)
    here = here[1:]
    has_above = lax.axis_index("slab") < lax.axis_size("slab") - 1
    tiles = lax.broadcasted_iota(jnp.int32, here.shape, 1)
    return packed(
        jnp.concatenate([tiles, listed]),
        jnp.concatenate([here, HALF + tiles]),
        jnp.concatenate([here >= 0, (listed >= 0) & has_above]),
        is_part,
    )


def body(positions, charges, radii, scales, neighbours, pad_mask):
    sent, edges, here = run_pack(
        jnp.swapaxes(positions[0, 0], 0, 1),
        charges[0, 0],
        radii[0, 0],
        scales[0, 0],
        neighbours[0, 0].T,
        pad_mask[0, 0].T,
    )
    above = above_to_here(sent)
    next_edges = next_to_here(edges)
    above_edges = across_to_here(edges)
    reach, is_part = chunk_reach(sent, next_edges, above, above_edges)
    items = pair_items(here, above, is_part)

    *parts, data, plain, d_self, d_pair = run_born(items, reach, sent, next_edges, above, above_edges)
    shares = swap_sums(*parts)
    radii_born, slope, *parts, force = run_energy(items, reach, data, plain, shares)
    shares = swap_sums(*parts)
    gradient, own, over, to_next, to_across = run_force(
        items, reach, data, slope, shares, force, d_self, d_pair
    )
    forces, to_next, to_across = lax.optimization_barrier(
        (own + here_to_above(over), here_to_next(to_next), here_to_across(to_across))
    )
    forces = forces + jnp.pad((to_next + to_across)[:, 0:EDGE], ((0, 0), (0, TILES - EDGE), (0, 0)))
    return (radii_born[None, None], gradient[None, None], jnp.swapaxes(forces, 0, 1)[None, None])


def solution(mesh):
    return jax.shard_map(
        body,
        mesh=mesh,
        in_specs=(
            P("slab", "tile", None, None, None),
            P("slab", "tile", None, None),
            P("slab", "tile", None, None),
            P("slab", "tile", None, None),
            P("slab", "tile", None, None),
            P("slab", "tile", None, None),
        ),
        out_specs=(
            P("slab", "tile", None, None),
            P("slab", "tile", None, None),
            P("slab", "tile", None, None, None),
        ),
        check_vma=False,
    )
```
